32 devices in a mesh: comp: 2 (over x), tx: 4 (over z), ty: 4 (over y, core).
Axes of the slice: x: 2, y: 2, z: 4, core: 2. Of those that a mesh axis runs over, the one named last changes fastest.
Arguments:
- spectrum: float32 [1800, 32, 1024], P('comp', 'tx', 'ty'), may hold values from 0.05 to 2
- sea_mask: int32 [32, 1024], P('tx', 'ty'), may hold values from 0 to 1, as said below
- owner_list: int32 [4, 4, 8, 256], P('tx', 'ty'), may hold values from 0 to 2047, as said below
- owner_count: int32 [4, 4, 8], P('tx', 'ty'), may hold values from 0 to 256, as said below
- slopes: float32 [2, 32, 1024], P(None, 'tx', 'ty'), may hold values from -0.00015 to 0.00015
- friction: float32 [32, 1024], P('tx', 'ty'), may hold values from 0.15 to 0.6
- wind_angle: float32 [32, 1024], P('tx', 'ty'), may hold values from -3.140625 to 3.140625
Outputs:
- new_spectrum: float32 [1800, 32, 1024], P('comp', 'tx', 'ty')
The draws below stay inside these ranges and needn't reach their ends.
Inputs may be any that keep to these rules, and one draw needn't show every extreme that they name: `sea_mask`: 1 marks sea, 0 land. Each row of tiles along tx holds a tile without land, and each latitude row of a tile has a sea cell. `owner_list`: owner o is the device of index o along comp+tx (comp slowest) in the same row of tiles. For each tile, the first owner_count slots of each owner name cells of the tile as ix * 256 + iy; together they name every sea cell of the tile exactly once and no land cell. The other slots hold 0. `owner_count`: points of one tile given to one owner, at most 256; 256 is reached in every draw.
All inputs are finite; a program needn't handle non-finite values.
Results may differ from the reference program's by a relative error of at most 0.0003.
Values sent between devices are 32-bit elements; how exact they have to be, the bound alone decides.
No kernel may reach another device: no remote copies, remote signals or barrier semaphores. Data moves between devices by JAX's collectives and lax.ppermute only.
A program may use at most 128 MiB of HBM per device.

```python
import math
import jax
import jax.numpy as jnp
from jax import lax

NDIR = 36
NFREQ = 50
CX = 8
CY = 256
KTOT = 1800
NX = 32
NY = 1024
CELLS = 2048
OWNERS = 8
CAP = 256
TX_TILES = 4
TY_TILES = 4


def coast_layout(key):
    base_key = jax.random.fold_in(key, 4177)
    key_list = jax.random.split(base_key, 5)
    widest = jax.random.randint(key_list[0], (TX_TILES, TY_TILES), 0, CX)
    open_tile = jax.random.randint(key_list[1], (TY_TILES,), 0, TX_TILES)
    widest = jnp.where(jnp.arange(TX_TILES, dtype=jnp.int32)[:, None] == open_tile[None, :], 0, widest)
    shore_width = jax.random.randint(key_list[2], (TX_TILES, TY_TILES, CY), 0, widest[:, :, None] + 1)
    column_ids = jnp.arange(CX, dtype=jnp.int32)[None, None, :, None]
    sea_tile = (column_ids >= shore_width[:, :, None, :]).astype(jnp.int32)
    sea_flat = sea_tile.reshape(TX_TILES * TY_TILES, CELLS)
    tile_keys = jax.random.split(key_list[3], TX_TILES * TY_TILES)

    def tile_ranks(tile_key):
        return jax.random.permutation(tile_key, CELLS).astype(jnp.int32)
    shuffled = jax.vmap(tile_ranks)(tile_keys)
    offsets = jax.random.randint(key_list[4], (TX_TILES * TY_TILES,), 0, OWNERS)
    positions = jnp.arange(CELLS, dtype=jnp.int32)
    owner_ids = jnp.arange(OWNERS, dtype=jnp.int32)

    def one_tile(sea_row, ranks, shift_by):
        order_key = (1 - sea_row) * CELLS + ranks
        ordering = jnp.argsort(order_key, stable=True).astype(jnp.int32)
        sea_total = jnp.sum(sea_row)
        owner_of = (positions + shift_by) % OWNERS
        slot_index = owner_of * CAP + positions // OWNERS
        target = jnp.where(positions < sea_total, slot_index, OWNERS * CAP)
        cell_names = jnp.zeros((OWNERS * CAP,), jnp.int32).at[target].set(ordering, mode='drop')
        taken = ((positions < sea_total)[:, None] & (owner_of[:, None] == owner_ids[None, :])).astype(jnp.int32)
        return (cell_names.reshape(OWNERS, CAP), jnp.sum(taken, axis=0))
    name_lists, count_lists = jax.vmap(one_tile)(sea_flat, shuffled, offsets)
    sea_grid = sea_tile.transpose(0, 2, 1, 3).reshape(TX_TILES * CX, TY_TILES * CY)
    return (sea_grid, name_lists.reshape(TX_TILES, TY_TILES, OWNERS, CAP), count_lists.reshape(TX_TILES, TY_TILES, OWNERS))


def draw_sea_mask(key, part):
    return coast_layout(key)[0]


def draw_owner_list(key, part):
    return coast_layout(key)[1]


def draw_owner_count(key, part):
    return coast_layout(key)[2]


def level_of(own_key, extent, pieces, smallest, top_value):
    level = 1.0
    for position, shards_of in pieces:
        steps = jax.random.uniform(jax.random.fold_in(jax.random.fold_in(own_key, 6), position), (shards_of,), jnp.float32, smallest / len(pieces), top_value / len(pieces))
        level = level * jnp.repeat(jnp.exp(steps), extent[position] // shards_of).reshape((-1,) + (1,) * (len(extent) - 1 - position))
    return level


def setup_inputs(seed: int = 0) -> dict:
    key_of = jax.random.split(jax.random.key(seed), 8)
    spectrum = jnp.clip(jnp.exp(math.log(2.0) - 3.6888794 * jax.random.uniform(key_of[0], (KTOT, NX, NY), jnp.float32) ** level_of(key_of[0], (KTOT, NX, NY), ((0, 2), (1, 4), (2, 4)), -0.2, 0.2)), 0.05, 2.0)
    sea_mask = draw_sea_mask(jax.random.fold_in(key_of[7], 71), 0)
    owner_list = draw_owner_list(jax.random.fold_in(key_of[7], 71), 0)
    owner_count = draw_owner_count(jax.random.fold_in(key_of[7], 71), 0)
    slopes = jnp.clip(jax.random.uniform(key_of[4], (2, NX, NY), jnp.float32, -0.00015, 0.00015) * level_of(key_of[4], (2, NX, NY), ((1, 4), (2, 4)), -0.4, 0.0), -0.00015, 0.00015)
    friction = jnp.clip(0.15 + 0.45000002 * jax.random.uniform(key_of[5], (NX, NY), jnp.float32) ** level_of(key_of[5], (NX, NY), ((0, 4), (1, 4)), -0.2, 0.2), 0.15, 0.6)
    wind_angle = jnp.clip(jax.random.uniform(key_of[6], (NX, NY), jnp.float32, -3.140625, 3.140625), -3.140625, 3.140625)
    return {"spectrum": spectrum, "sea_mask": sea_mask, "owner_list": owner_list, "owner_count": owner_count, "slopes": slopes, "friction": friction, "wind_angle": wind_angle}


TIME_STEP = 240.0
CELL_SIZE = 11100.0
GRAVITY = 9.81
LOW_FREQ = 0.0373
HIGH_FREQ = 1.0
WIND_GROWTH = 1e-4
WIND_FACTOR = 28.0
SATURATION_LOSS = 5e-4
CUMULATIVE_LOSS = 1e-3
STEEPNESS_LOSS = 5e-3
SATURATION_LEVEL = 0.6


def freq_values(freq_ids):
    return (2.0 * math.pi * LOW_FREQ) * jnp.exp(freq_ids.astype(jnp.float32) * (math.log(HIGH_FREQ / LOW_FREQ) / (NFREQ - 1)))


def wave_tables(first_comp, comp_count):
    comp_ids = first_comp + jnp.arange(comp_count, dtype=jnp.int32)
    headings = (comp_ids // NFREQ).astype(jnp.float32) * (2.0 * math.pi / NDIR)
    return headings, freq_values(comp_ids % NFREQ)


def advect(energy, west_side, east_side, south_side, north_side, prev_dir, next_dir, headings, ang_freq, slopes):
    group_speed = GRAVITY / (2.0 * ang_freq)
    along_x = ((TIME_STEP / CELL_SIZE) * group_speed * jnp.cos(headings))[:, None, None]
    along_y = ((TIME_STEP / CELL_SIZE) * group_speed * jnp.sin(headings))[:, None, None]
    bending = (TIME_STEP * NDIR / (2.0 * math.pi)) * (2.0 * math.pi * LOW_FREQ) / ang_freq
    turning = bending[:, None, None] * (jnp.sin(headings)[:, None, None] * slopes[0][None] - jnp.cos(headings)[:, None, None] * slopes[1][None])
    change = jnp.maximum(along_x, 0.0) * (energy - west_side) + jnp.minimum(along_x, 0.0) * (east_side - energy)
    change = change + jnp.maximum(along_y, 0.0) * (energy - south_side) + jnp.minimum(along_y, 0.0) * (north_side - energy)
    change = change + jnp.maximum(turning, 0.0) * (energy - prev_dir) + jnp.minimum(turning, 0.0) * (next_dir - energy)
    return energy - change


def source_terms(spectra, friction, wind_angle):
    dir_ids = jnp.arange(NDIR, dtype=jnp.int32)
    offset = (dir_ids[:, None] - dir_ids[None, :]) % NDIR
    nearest = jnp.minimum(offset, NDIR - offset)
    spread = jnp.where(4 * nearest < NDIR, jnp.cos(offset.astype(jnp.float32) * (2.0 * math.pi / NDIR)) ** 2, 0.0)
    spread = spread / jnp.sum(spread, axis=1, keepdims=True)
    sat_level = jnp.einsum("de,efp->dfp", spread, spectra, precision=lax.Precision.HIGHEST)
    excess = jnp.maximum(sat_level / SATURATION_LEVEL - 1.0, 0.0)
    excess_sq = excess * excess
    freq_ids = jnp.arange(NFREQ, dtype=jnp.int32)
    below_mask = (freq_ids[None, :] < freq_ids[:, None]).astype(jnp.float32)
    running = jnp.einsum("fg,dgp->dfp", below_mask, excess_sq, precision=lax.Precision.HIGHEST) / NFREQ
    ang_freq = freq_values(freq_ids)
    weights = (ang_freq / ang_freq[NFREQ - 1]) ** 2
    steepness = jnp.einsum("dfp,f->p", spectra, weights, precision=lax.Precision.HIGHEST) / (NDIR * NFREQ)
    headings = dir_ids.astype(jnp.float32) * (2.0 * math.pi / NDIR)
    alignment = jnp.cos(headings)[:, None, None] * jnp.cos(wind_angle)[None, None, :] + jnp.sin(headings)[:, None, None] * jnp.sin(wind_angle)[None, None, :]
    forcing = (WIND_FACTOR / GRAVITY) * friction[None, None, :] * ang_freq[None, :, None] * alignment
    growth = WIND_GROWTH * ang_freq[None, :, None] * jnp.maximum(forcing - 1.0, 0.0)
    losses = ang_freq[None, :, None] * (SATURATION_LOSS * excess_sq + CUMULATIVE_LOSS * running + STEEPNESS_LOSS * (steepness * steepness)[None, None, :])
    return spectra * (1.0 + TIME_STEP * growth) / (1.0 + TIME_STEP * losses)


def listed_cells(owner_list, owner_count):
    slot_ids = jnp.arange(CAP, dtype=jnp.int32)

    def one_tile(cell_names, counts_here):
        in_use = slot_ids[None, :] < counts_here[:, None]
        target = jnp.where(in_use, cell_names, CELLS).reshape(-1)
        listed = jnp.zeros((CELLS,), jnp.int32).at[target].set(1, mode="drop")
        return listed.reshape(CX, CY)

    per_tile = jax.vmap(jax.vmap(one_tile))(owner_list, owner_count)
    return per_tile.transpose(0, 2, 1, 3).reshape(NX, NY)


def reference(spectrum, sea_mask, owner_list, owner_count, slopes, friction, wind_angle):
    sea_cells = sea_mask.astype(jnp.float32)
    masked = spectrum * sea_cells[None]

    def one_heading(heading):
        first_comp = heading * NFREQ
        centre = lax.dynamic_slice_in_dim(masked, first_comp, NFREQ, 0)
        prev_dir = lax.dynamic_slice_in_dim(masked, ((heading + NDIR - 1) % NDIR) * NFREQ, NFREQ, 0)
        next_dir = lax.dynamic_slice_in_dim(masked, ((heading + 1) % NDIR) * NFREQ, NFREQ, 0)
        west_side = jnp.roll(centre, 1, axis=1)
        east_side = jnp.roll(centre, -1, axis=1)
        south_side = jnp.pad(centre, ((0, 0), (0, 0), (1, 0)))[:, :, :-1]
        north_side = jnp.pad(centre, ((0, 0), (0, 0), (0, 1)))[:, :, 1:]
        headings, ang_freq = wave_tables(first_comp, NFREQ)
        advected = advect(centre, west_side, east_side, south_side, north_side, prev_dir, next_dir, headings, ang_freq, slopes)
        return advected * sea_cells[None]

    advected = lax.map(one_heading, jnp.arange(NDIR, dtype=jnp.int32)).reshape(NDIR * NFREQ, NX, NY)

    def one_row(row_index):
        column = lax.dynamic_index_in_dim(advected, row_index, 1, keepdims=False)
        result = source_terms(column.reshape(NDIR, NFREQ, NY), friction[row_index], wind_angle[row_index])
        return result.reshape(NDIR * NFREQ, NY)

    updated = jnp.moveaxis(lax.map(one_row, jnp.arange(NX, dtype=jnp.int32)), 0, 1)
    listed = listed_cells(owner_list, owner_count)
    return jnp.where(listed[None] > 0, updated, advected)
```

```python
import functools
import math

import jax
import jax.numpy as jnp
import numpy as np
from jax import lax
from jax.experimental import pallas as pl
from jax.experimental.pallas import tpu as pltpu
from jax.sharding import PartitionSpec as P

NDIR = 36
NFREQ = 50


TIME_STEP = 240.0
CELL_SIZE = 11100.0
GRAVITY = 9.81
LOW_FREQ = 0.0373
HIGH_FREQ = 1.0
WIND_GROWTH = 0.0001
WIND_FACTOR = 28.0
SATURATION_LOSS = 0.0005
CUMULATIVE_LOSS = 0.001
STEEPNESS_LOSS = 0.005
SATURATION_LEVEL = 0.6


def padded(value, sides, width, wrap):
    for axis, dim in sides:
        size, length = (lax.axis_size(axis), value.shape[dim])
        up = [(i, (i + 1) % size) for i in range(size if wrap else size - 1)]
        down = [(j, i) for i, j in up]
        last = lax.slice_in_dim(value, length - width, length, axis=dim)
        first = lax.slice_in_dim(value, 0, width, axis=dim)
        before = lax.ppermute(last, axis, up)
        after = lax.ppermute(first, axis, down)
        value = jnp.concatenate([before, value, after], axis=dim)
    return value


def freq_values(freq_ids):
    return (
        2.0
        * math.pi
        * LOW_FREQ
        * jnp.exp(freq_ids.astype(jnp.float32) * (math.log(HIGH_FREQ / LOW_FREQ) / (NFREQ - 1)))
    )


def wave_tables(first_comp, comp_count):
    comp_ids = first_comp + jnp.arange(comp_count, dtype=jnp.int32)
    headings = (comp_ids // NFREQ).astype(jnp.float32) * (2.0 * math.pi / NDIR)
    return (headings, freq_values(comp_ids % NFREQ))


def advect(
    energy,
    west_side,
    east_side,
    south_side,
    north_side,
    prev_dir,
    next_dir,
    headings,
    ang_freq,
    slopes,
):
    group_speed = GRAVITY / (2.0 * ang_freq)
    along_x = (TIME_STEP / CELL_SIZE * group_speed * jnp.cos(headings))[:, None, None]
    along_y = (TIME_STEP / CELL_SIZE * group_speed * jnp.sin(headings))[:, None, None]
    bending = TIME_STEP * NDIR / (2.0 * math.pi) * (2.0 * math.pi * LOW_FREQ) / ang_freq
    turning = bending[:, None, None] * (
        jnp.sin(headings)[:, None, None] * slopes[0][None]
        - jnp.cos(headings)[:, None, None] * slopes[1][None]
    )
    change = jnp.maximum(along_x, 0.0) * (energy - west_side) + jnp.minimum(along_x, 0.0) * (
        east_side - energy
    )
    change = (
        change
        + jnp.maximum(along_y, 0.0) * (energy - south_side)
        + jnp.minimum(along_y, 0.0) * (north_side - energy)
    )
    change = (
        change
        + jnp.maximum(turning, 0.0) * (energy - prev_dir)
        + jnp.minimum(turning, 0.0) * (next_dir - energy)
    )
    return energy - change


def source_terms(spectra, friction, wind_angle):
    dir_ids = jnp.arange(NDIR, dtype=jnp.int32)
    offset = (dir_ids[:, None] - dir_ids[None, :]) % NDIR
    nearest = jnp.minimum(offset, NDIR - offset)
    spread = jnp.where(
        4 * nearest < NDIR, jnp.cos(offset.astype(jnp.float32) * (2.0 * math.pi / NDIR)) ** 2, 0.0
    )
    spread = spread / jnp.sum(spread, axis=1, keepdims=True)
    sat_level = jnp.einsum("de,efp->dfp", spread, spectra, precision=lax.Precision.HIGHEST)
    excess = jnp.maximum(sat_level / SATURATION_LEVEL - 1.0, 0.0)
    excess_sq = excess * excess
    freq_ids = jnp.arange(NFREQ, dtype=jnp.int32)
    below_mask = (freq_ids[None, :] < freq_ids[:, None]).astype(jnp.float32)
    running = (
        jnp.einsum("fg,dgp->dfp", below_mask, excess_sq, precision=lax.Precision.HIGHEST) / NFREQ
    )
    ang_freq = freq_values(freq_ids)
    weights = (ang_freq / ang_freq[NFREQ - 1]) ** 2
    steepness = jnp.einsum("dfp,f->p", spectra, weights, precision=lax.Precision.HIGHEST) / (
        NDIR * NFREQ
    )
    headings = dir_ids.astype(jnp.float32) * (2.0 * math.pi / NDIR)
    alignment = (
        jnp.cos(headings)[:, None, None] * jnp.cos(wind_angle)[None, None, :]
        + jnp.sin(headings)[:, None, None] * jnp.sin(wind_angle)[None, None, :]
    )
    forcing = WIND_FACTOR / GRAVITY * friction[None, None, :] * ang_freq[None, :, None] * alignment
    growth = WIND_GROWTH * ang_freq[None, :, None] * jnp.maximum(forcing - 1.0, 0.0)
    losses = ang_freq[None, :, None] * (
        SATURATION_LOSS * excess_sq
        + CUMULATIVE_LOSS * running
        + STEEPNESS_LOSS * (steepness * steepness)[None, None, :]
    )
    return spectra * (1.0 + TIME_STEP * growth) / (1.0 + TIME_STEP * losses)


def shards(spectrum, sea_mask, owner_list, owner_count, slopes, friction, wind_angle):
    comp_size = lax.axis_size("comp")
    local_comps = spectrum.shape[0]
    cell_count = spectrum.shape[1] * spectrum.shape[2]
    sea_cells = sea_mask.astype(jnp.float32)
    masked = spectrum * sea_cells[None]
    headings, ang_freq = wave_tables(lax.axis_index("comp") * local_comps, local_comps)
    padded_lon = padded(masked, (("tx", 1),), 1, True)
    padded_lat = padded(masked, (("ty", 2),), 1, False)
    padded_dir = padded(masked, (("comp", 0),), NFREQ, True)
    advected = (
        advect(
            masked,
            padded_lon[:, :-2],
            padded_lon[:, 2:],
            padded_lat[:, :, :-2],
            padded_lat[:, :, 2:],
            padded_dir[:local_comps],
            padded_dir[2 * NFREQ :],
            headings,
            ang_freq,
            slopes,
        )
        * sea_cells[None]
    )
    moved_flat = advected.reshape(local_comps, cell_count)
    cell_names = owner_list[0, 0]
    slot_ids = jnp.arange(cell_names.shape[1], dtype=jnp.int32)
    in_use = slot_ids[None, :] < owner_count[0, 0][:, None]
    target = jnp.where(in_use, cell_names, cell_count).reshape(-1)
    owners = cell_names.shape[0]
    capacity = cell_names.shape[1]
    tiles_x = lax.axis_size("tx")
    cell_ids = jnp.arange(cell_count, dtype=jnp.int32)
    selector = (cell_ids[:, None] == target[None, :]).astype(jnp.float32)
    outgoing = jnp.dot(moved_flat, selector, precision=lax.Precision.HIGHEST).reshape(
        local_comps, owners, capacity
    )
    wind_rows = jnp.stack([friction.reshape(-1), wind_angle.reshape(-1)])
    point_data = jnp.dot(wind_rows, selector, precision=lax.Precision.HIGHEST).reshape(
        2, owners, capacity
    )
    spectra = lax.all_to_all(outgoing, ("comp", "tx"), split_axis=1, concat_axis=1, tiled=True)
    extras = lax.all_to_all(point_data, ("comp", "tx"), split_axis=1, concat_axis=1, tiled=True)
    batch_size = spectra.shape[2]
    full_spec = (
        spectra.reshape(local_comps, comp_size, tiles_x * batch_size)
        .transpose(1, 0, 2)
        .reshape(NDIR, NFREQ, tiles_x * batch_size)
    )
    extra_rows = extras.reshape(2, comp_size, tiles_x * batch_size)[:, 0]
    result = source_terms(full_spec, extra_rows[0], extra_rows[1])
    homeward = (
        result.reshape(comp_size, local_comps, tiles_x * batch_size)
        .transpose(1, 0, 2)
        .reshape(local_comps, comp_size * tiles_x, batch_size)
    )
    returned = lax.all_to_all(homeward, ("comp", "tx"), split_axis=1, concat_axis=1, tiled=True)
    gathered = lax.dot_general(
        returned.reshape(local_comps, owners * capacity),
        selector,
        (((1,), (1,)), ((), ())),
        precision=lax.Precision.HIGHEST,
    )
    listed = jnp.sum(selector, axis=1) > 0.5
    updated = jnp.where(listed[None], gathered, moved_flat)
    return updated.reshape(spectrum.shape)


def chunk_bounds():
    return [(5 * i, 5 * i + 5) for i in range(10)]


HALO_GROUPS = ((0, 5), (5, 50))
HALF_DIRS = NDIR // 2
SIDE_DIRS = 8
LEAD_DIRS = 9
VMEM_BYTES = 24 * 1024 * 1024


def freq_table():
    freqs = np.arange(NFREQ, dtype=np.float64)
    return 2.0 * math.pi * LOW_FREQ * np.exp(freqs * (math.log(HIGH_FREQ / LOW_FREQ) / (NFREQ - 1)))


def heading(index):
    return 2.0 * math.pi * index / NDIR


def pack_kernel(first, count, half_ref, sea_ref, spec_ref, lead_ref, trail_ref, lat_ref, raw_ref, held, sems, raw_sems):
    copies = []
    for d in range(HALF_DIRS):
        for h in range(2):
            copy = pltpu.make_async_copy(
                spec_ref.at[d, pl.ds(first, count), :, pl.ds(128 * h, 128)], held.at[h, d], sems.at[h, d]
            )
            copy.start()
            copies.append(copy)
    raw_copies = []
    for i, d in enumerate((0, HALF_DIRS - 1)):
        copy = pltpu.make_async_copy(spec_ref.at[d, pl.ds(first, count)], raw_ref.at[i], raw_sems.at[i])
        copy.start()
        raw_copies.append(copy)
    lanes = lax.broadcasted_iota(jnp.int32, (8, 128), 1)

    def body(flipped):
        lead_row, trail_row = (0, 7) if flipped else (7, 0)
        lane = 0 if flipped else 127
        part = 0 if flipped else 1
        sea_part = sea_ref[:, 128 * part : 128 * part + 128]
        rows = held.reshape(2 * HALF_DIRS * count * 8, 128)
        for d in range(HALF_DIRS):
            for h in range(2):
                copies[2 * d + h].wait()
                lanes_here = slice(128 * h, 128 * h + 128)
                start = (h * HALF_DIRS + d) * count * 8
                if d < LEAD_DIRS:
                    column = rows[pl.ds(start + lead_row, count, stride=8), :]
                    lead_ref[d * count : (d + 1) * count, lanes_here] = column * sea_ref[lead_row : lead_row + 1, lanes_here]
                elif d > LEAD_DIRS:
                    t = d - LEAD_DIRS - 1
                    column = rows[pl.ds(start + trail_row, count, stride=8), :]
                    trail_ref[t * count : (t + 1) * count, lanes_here] = column * sea_ref[trail_row : trail_row + 1, lanes_here]

            def one(f, kept):
                value = held[part, d, f] * sea_part
                value = jnp.broadcast_to(value[:, lane : lane + 1], (8, 128))
                return jnp.where(lanes == f, value, kept)

            lat_ref[d] = lax.fori_loop(0, count, one, jnp.zeros((8, 128), jnp.float32), unroll=5)

    @pl.when(half_ref[0] == 0)
    def _():
        body(False)

    @pl.when(half_ref[0] != 0)
    def _():
        body(True)

    for copy in raw_copies:
        copy.wait()


def pack(first, count, half, sea, spec):
    return pl.pallas_call(
        functools.partial(pack_kernel, first, count),
        out_shape=(
            jax.ShapeDtypeStruct((LEAD_DIRS * count, 256), jnp.float32),
            jax.ShapeDtypeStruct(((HALF_DIRS - LEAD_DIRS - 1) * count, 256), jnp.float32),
            jax.ShapeDtypeStruct((HALF_DIRS, 8, 128), jnp.float32),
            jax.ShapeDtypeStruct((2, count, 8, 256), jnp.float32),
        ),
        in_specs=[
            pl.BlockSpec(memory_space=pltpu.SMEM),
            pl.BlockSpec(memory_space=pltpu.VMEM),
            pl.BlockSpec(memory_space=pl.ANY),
        ],
        out_specs=(
            pl.BlockSpec(memory_space=pltpu.VMEM),
            pl.BlockSpec(memory_space=pltpu.VMEM),
            pl.BlockSpec(memory_space=pltpu.VMEM),
            pl.BlockSpec(memory_space=pl.ANY),
        ),
        scratch_shapes=[
            pltpu.VMEM((2, HALF_DIRS, count, 8, 128), jnp.float32),
            pltpu.SemaphoreType.DMA((2, HALF_DIRS)),
            pltpu.SemaphoreType.DMA((2,)),
        ],
        compiler_params=pltpu.CompilerParams(vmem_limit_bytes=VMEM_BYTES),
        cost_estimate=pl.CostEstimate(flops=count * 18 * 2048, bytes_accessed=count * 18 * 8192, transcendentals=0),
    )(half, sea, spec)


def advect_kernel(
    first, count, group_first, group_count,
    half_ref, table_ref, sea_ref, slope_ref, spec_ref, lead_ref, trail_ref, lat_ref, raw_ref, steep_ref,
    send_ref, keep_ref, steep_out_ref, held, turn, sem,
):
    copy = pltpu.make_async_copy(spec_ref.at[:, pl.ds(first, count)], held, sem)
    copy.start()
    for d in range(HALF_DIRS):
        turn[d] = math.sin(heading(d)) * slope_ref[0] - math.cos(heading(d)) * slope_ref[1]
    steep_out_ref[...] = steep_ref[...]
    copy.wait()
    offset = first - group_first
    rows_at = lax.broadcasted_iota(jnp.int32, (8, 256), 0)
    lanes_at = lax.broadcasted_iota(jnp.int32, (8, 256), 1)
    per_cell = TIME_STEP / CELL_SIZE * GRAVITY / 2.0
    bending = TIME_STEP * NDIR / (2.0 * math.pi) * (2.0 * math.pi * LOW_FREQ)

    def body(flipped):
        lead_row, lead_shift = (7, 7) if flipped else (0, 1)
        trail_row, trail_shift = (0, 1) if flipped else (7, 7)
        lat_lane, lat_shift = (255, 255) if flipped else (0, 1)

        def one(f, nothing):
            sea = sea_ref[...]
            inverse = table_ref[0, first + f]
            weight = table_ref[1, first + f]
            total = jnp.zeros((8, 256), jnp.float32)
            prev = raw_ref[1, offset + f] * sea
            here = held[0, f] * sea
            for d in range(HALF_DIRS):
                after = (held[d + 1, f] if d < HALF_DIRS - 1 else raw_ref[0, offset + f]) * sea
                rate = turn[d]
                size = jnp.abs(rate) * bending
                moved = size * jnp.where(rate > 0.0, prev, after)
                along_x = per_cell * abs(math.cos(heading(d)))
                along_y = per_cell * abs(math.sin(heading(d)))
                fixed = 0.0
                if d != LEAD_DIRS:
                    if d < LEAD_DIRS:
                        row = lead_ref[pl.ds(d * group_count + offset + f, 1), :]
                        edge, shift = lead_row, lead_shift
                    else:
                        row = trail_ref[pl.ds((d - LEAD_DIRS - 1) * group_count + offset + f, 1), :]
                        edge, shift = trail_row, trail_shift
                    side = jnp.where(rows_at == edge, jnp.broadcast_to(row, (8, 256)), pltpu.roll(here, shift, 0))
                    moved = moved + along_x * side
                    fixed += along_x
                if d != 0:
                    halo = pltpu.roll(lat_ref[d], (lat_lane % 128) + 128 - (offset + f), 1)
                    halo = jnp.concatenate([halo, halo], axis=1)
                    side = jnp.where(lanes_at == lat_lane, halo, pltpu.roll(here, lat_shift, 1))
                    moved = moved + along_y * side
                    fixed += along_y
                result = (here - inverse * ((size + fixed) * here - moved)) * sea
                if d < SIDE_DIRS:
                    send_ref[d, f] = result
                elif d < HALF_DIRS - SIDE_DIRS:
                    keep_ref[d - SIDE_DIRS, f] = result
                else:
                    send_ref[d - 2, f] = result
                total = total + result
                prev, here = here, after
            steep_out_ref[...] += weight * total
            return nothing

        lax.fori_loop(0, count, one, 0)

    @pl.when(half_ref[0] == 0)
    def _():
        body(False)

    @pl.when(half_ref[0] != 0)
    def _():
        body(True)


def advect_chunk(first, count, group, half, table, sea, slopes, spec, halos, steep):
    vmem = pl.BlockSpec(memory_space=pltpu.VMEM)
    smem = pl.BlockSpec(memory_space=pltpu.SMEM)
    return pl.pallas_call(
        functools.partial(advect_kernel, first, count, group[0], group[1] - group[0]),
        out_shape=(
            jax.ShapeDtypeStruct((2 * SIDE_DIRS, count, 8, 256), jnp.float32),
            jax.ShapeDtypeStruct((HALF_DIRS - 2 * SIDE_DIRS, count, 8, 256), jnp.float32),
            jax.ShapeDtypeStruct((8, 256), jnp.float32),
        ),
        in_specs=[smem, smem, vmem, vmem, pl.BlockSpec(memory_space=pl.ANY), vmem, vmem, vmem, vmem, vmem],
        out_specs=(vmem, vmem, vmem),
        scratch_shapes=[
            pltpu.VMEM((HALF_DIRS, count, 8, 256), jnp.float32),
            pltpu.VMEM((HALF_DIRS, 8, 256), jnp.float32),
            pltpu.SemaphoreType.DMA,
        ],
        compiler_params=pltpu.CompilerParams(vmem_limit_bytes=VMEM_BYTES),
        cost_estimate=pl.CostEstimate(flops=count * 18 * 2048 * 25, bytes_accessed=count * 18 * 8192 * 2, transcendentals=0),
    )(half, table, sea, slopes, spec, *halos, steep)


def source_kernel(first, count, chained, table_ref, wind_ref, steep_a_ref, steep_b_ref, cum_ref, own_ref, keep_ref, other_ref, *rest):
    out_ref, cum_out_ref, result, align, sem = rest[1:] if chained else rest
    weights = [math.cos(heading(m)) ** 2 / (9.0 * SATURATION_LEVEL) for m in range(SIDE_DIRS + 1)]
    steep = (steep_a_ref[...] + steep_b_ref[...]) * (1.0 / (NDIR * NFREQ))
    steep_sq = steep * steep
    for d in range(HALF_DIRS):
        align[d] = math.cos(heading(d)) * wind_ref[0] + math.sin(heading(d)) * wind_ref[1]
    cum_out_ref[...] = cum_ref[...]

    def one(f, nothing):
        omega = table_ref[2, first + f]
        gain = TIME_STEP * WIND_GROWTH * omega
        loss_sat = TIME_STEP * SATURATION_LOSS * omega
        loss_cum = TIME_STEP * CUMULATIVE_LOSS / NFREQ * omega
        loss_steep = TIME_STEP * STEEPNESS_LOSS * omega
        for half in range(2):
            lanes = slice(128 * half, 128 * half + 128)
            line = [other_ref[SIDE_DIRS + i, f, :, lanes] for i in range(SIDE_DIRS)]
            line += [own_ref[i, f, :, lanes] for i in range(SIDE_DIRS)]
            line += [keep_ref[i, f, :, lanes] for i in range(HALF_DIRS - 2 * SIDE_DIRS)]
            line += [own_ref[SIDE_DIRS + i, f, :, lanes] for i in range(SIDE_DIRS)]
            line += [other_ref[i, f, :, lanes] for i in range(SIDE_DIRS)]
            base = 1.0 + loss_steep * steep_sq[:, lanes]
            for d in range(HALF_DIRS):
                at = d + SIDE_DIRS
                level = weights[0] * line[at] - 1.0
                for m in range(1, SIDE_DIRS + 1):
                    level = level + weights[m] * (line[at - m] + line[at + m])
                excess = jnp.maximum(level, 0.0)
                square = excess * excess
                cum = cum_out_ref[d, :, lanes]
                cum_out_ref[d, :, lanes] = cum + square
                grown = 1.0 + gain * jnp.maximum(align[d, :, lanes] * omega - 1.0, 0.0)
                lost = base + loss_sat * square + loss_cum * cum
                result[d, f, :, lanes] = line[at] * grown / lost
        return nothing

    lax.fori_loop(0, count, one, 0)
    copy = pltpu.make_async_copy(result, out_ref.at[:, pl.ds(first, count)], sem)
    copy.start()
    copy.wait()


def source_chunk(first, count, table, wind, steep_own, steep_other, cum, own, keep, other, out):
    vmem = pl.BlockSpec(memory_space=pltpu.VMEM)
    chained = out is not None
    operands = (table, wind, steep_own, steep_other, cum, own, keep, other) + ((out,) if chained else ())
    return pl.pallas_call(
        functools.partial(source_kernel, first, count, chained),
        out_shape=(
            jax.ShapeDtypeStruct((HALF_DIRS, NFREQ, 8, 256), jnp.float32),
            jax.ShapeDtypeStruct((HALF_DIRS, 8, 256), jnp.float32),
        ),
        in_specs=[pl.BlockSpec(memory_space=pltpu.SMEM)]
        + [vmem] * 7
        + ([pl.BlockSpec(memory_space=pl.ANY)] if chained else []),
        out_specs=(pl.BlockSpec(memory_space=pl.ANY), vmem),
        scratch_shapes=[
            pltpu.VMEM((HALF_DIRS, count, 8, 256), jnp.float32),
            pltpu.VMEM((HALF_DIRS, 8, 256), jnp.float32),
            pltpu.SemaphoreType.DMA,
        ],
        input_output_aliases={8: 0} if chained else {},
        compiler_params=pltpu.CompilerParams(vmem_limit_bytes=VMEM_BYTES),
        cost_estimate=pl.CostEstimate(flops=count * 18 * 2048 * 55, bytes_accessed=count * 18 * 8192 * 3, transcendentals=0),
    )(*operands)


def ring_pairs(size, step, wrap):
    return [(i, (i + step) % size) for i in range(size) if wrap or 0 <= i + step < size]


def paired_shards(spectrum, sea_mask, owner_list, owner_count, slopes, friction, wind_angle):
    tiles_x, tiles_y = lax.axis_size("tx"), lax.axis_size("ty")
    half = lax.axis_index("comp")
    sign = 1.0 - 2.0 * half.astype(jnp.float32)
    half = half.astype(jnp.int32).reshape(1)
    spec = spectrum.reshape(HALF_DIRS, NFREQ, 8, 256)
    sea = sea_mask.astype(jnp.float32)
    turn = slopes * sign
    wind = (sign * WIND_FACTOR / GRAVITY) * friction * jnp.stack([jnp.cos(wind_angle), jnp.sin(wind_angle)])
    omega = freq_table()
    table = jnp.asarray(np.stack([1.0 / omega, (omega / omega[-1]) ** 2, omega]).astype(np.float32))

    def joined(axis_size, step, wrap):
        ahead = ring_pairs(axis_size, step, wrap)
        back = ring_pairs(axis_size, -step, wrap)
        return ahead + [(axis_size + i, axis_size + j) for i, j in back]

    swap = [(0, 1), (1, 0)]
    lead_pairs = joined(tiles_x, 1, True)
    trail_pairs = joined(tiles_x, -1, True)
    lat_pairs = joined(tiles_y, 1, False)

    halos = []
    for begin, end in HALO_GROUPS:
        lead, trail, lat, raw = pack(begin, end - begin, half, sea, spec)
        halos.append(
            (
                lax.ppermute(lead, ("comp", "tx"), lead_pairs),
                lax.ppermute(trail, ("comp", "tx"), trail_pairs),
                lax.ppermute(lat, ("comp", "ty"), lat_pairs),
                lax.ppermute(raw, "comp", swap),
            )
        )
    steep = jnp.zeros((8, 256), jnp.float32)
    sent, kept, received = [], [], []
    for begin, end in chunk_bounds():
        which = [i for i, group in enumerate(HALO_GROUPS) if group[0] <= begin and end <= group[1]][0]
        send, keep, steep = advect_chunk(
            begin, end - begin, HALO_GROUPS[which], half, table, sea, turn, spec, halos[which], steep
        )
        sent.append(send)
        kept.append(keep)
        received.append(lax.ppermute(send, "comp", swap))
    steep_other = lax.ppermute(steep, "comp", swap)
    out, cum = None, jnp.zeros((HALF_DIRS, 8, 256), jnp.float32)
    for i, (begin, end) in enumerate(chunk_bounds()):
        out, cum = source_chunk(
            begin, end - begin, table, wind, steep, steep_other, cum, sent[i], kept[i], received[i], out
        )
    return out.reshape(spectrum.shape)


def fits_pairs(mesh, spectrum):
    return (
        mesh.shape["comp"] == 2
        and spectrum.shape[0] == NDIR * NFREQ
        and spectrum.shape[1] == 8 * mesh.shape["tx"]
        and spectrum.shape[2] == 256 * mesh.shape["ty"]
    )


def solution(mesh):
    in_specs = (
        P("comp", "tx", "ty"),
        P("tx", "ty"),
        P("tx", "ty", None, None),
        P("tx", "ty", None),
        P(None, "tx", "ty"),
        P("tx", "ty"),
        P("tx", "ty"),
    )
    out_specs = P("comp", "tx", "ty")

    def step(spectrum, *others):
        body = paired_shards if fits_pairs(mesh, spectrum) else shards
        mapped = jax.shard_map(body, mesh=mesh, in_specs=in_specs, out_specs=out_specs, check_vma=False)
        return mapped(spectrum, *others)

    return step
```

```python
import functools
import math

import jax
import jax.numpy as jnp
import numpy as np
from jax import lax
from jax.experimental import pallas as pl
from jax.experimental.pallas import tpu as pltpu
from jax.sharding import PartitionSpec as P

NDIR = 36
NFREQ = 50


TIME_STEP = 240.0
CELL_SIZE = 11100.0
GRAVITY = 9.81
LOW_FREQ = 0.0373
HIGH_FREQ = 1.0
WIND_GROWTH = 0.0001
WIND_FACTOR = 28.0
SATURATION_LOSS = 0.0005
CUMULATIVE_LOSS = 0.001
STEEPNESS_LOSS = 0.005
SATURATION_LEVEL = 0.6


def padded(value, sides, width, wrap):
    for axis, dim in sides:
        size, length = (lax.axis_size(axis), value.shape[dim])
        up = [(i, (i + 1) % size) for i in range(size if wrap else size - 1)]
        down = [(j, i) for i, j in up]
        last = lax.slice_in_dim(value, length - width, length, axis=dim)
        first = lax.slice_in_dim(value, 0, width, axis=dim)
        before = lax.ppermute(last, axis, up)
        after = lax.ppermute(first, axis, down)
        value = jnp.concatenate([before, value, after], axis=dim)
    return value


def freq_values(freq_ids):
    return (
        2.0
        * math.pi
        * LOW_FREQ
        * jnp.exp(freq_ids.astype(jnp.float32) * (math.log(HIGH_FREQ / LOW_FREQ) / (NFREQ - 1)))
    )


def wave_tables(first_comp, comp_count):
    comp_ids = first_comp + jnp.arange(comp_count, dtype=jnp.int32)
    headings = (comp_ids // NFREQ).astype(jnp.float32) * (2.0 * math.pi / NDIR)
    return (headings, freq_values(comp_ids % NFREQ))


def advect(
    energy,
    west_side,
    east_side,
    south_side,
    north_side,
    prev_dir,
    next_dir,
    headings,
    ang_freq,
    slopes,
):
    group_speed = GRAVITY / (2.0 * ang_freq)
    along_x = (TIME_STEP / CELL_SIZE * group_speed * jnp.cos(headings))[:, None, None]
    along_y = (TIME_STEP / CELL_SIZE * group_speed * jnp.sin(headings))[:, None, None]
    bending = TIME_STEP * NDIR / (2.0 * math.pi) * (2.0 * math.pi * LOW_FREQ) / ang_freq
    turning = bending[:, None, None] * (
        jnp.sin(headings)[:, None, None] * slopes[0][None]
        - jnp.cos(headings)[:, None, None] * slopes[1][None]
    )
    change = jnp.maximum(along_x, 0.0) * (energy - west_side) + jnp.minimum(along_x, 0.0) * (
        east_side - energy
    )
    change = (
        change
        + jnp.maximum(along_y, 0.0) * (energy - south_side)
        + jnp.minimum(along_y, 0.0) * (north_side - energy)
    )
    change = (
        change
        + jnp.maximum(turning, 0.0) * (energy - prev_dir)
        + jnp.minimum(turning, 0.0) * (next_dir - energy)
    )
    return energy - change


def source_terms(spectra, friction, wind_angle):
    dir_ids = jnp.arange(NDIR, dtype=jnp.int32)
    offset = (dir_ids[:, None] - dir_ids[None, :]) % NDIR
    nearest = jnp.minimum(offset, NDIR - offset)
    spread = jnp.where(
        4 * nearest < NDIR, jnp.cos(offset.astype(jnp.float32) * (2.0 * math.pi / NDIR)) ** 2, 0.0
    )
    spread = spread / jnp.sum(spread, axis=1, keepdims=True)
    sat_level = jnp.einsum("de,efp->dfp", spread, spectra, precision=lax.Precision.HIGHEST)
    excess = jnp.maximum(sat_level / SATURATION_LEVEL - 1.0, 0.0)
    excess_sq = excess * excess
    freq_ids = jnp.arange(NFREQ, dtype=jnp.int32)
    below_mask = (freq_ids[None, :] < freq_ids[:, None]).astype(jnp.float32)
    running = (
        jnp.einsum("fg,dgp->dfp", below_mask, excess_sq, precision=lax.Precision.HIGHEST) / NFREQ
    )
    ang_freq = freq_values(freq_ids)
    weights = (ang_freq / ang_freq[NFREQ - 1]) ** 2
    steepness = jnp.einsum("dfp,f->p", spectra, weights, precision=lax.Precision.HIGHEST) / (
        NDIR * NFREQ
    )
    headings = dir_ids.astype(jnp.float32) * (2.0 * math.pi / NDIR)
    alignment = (
        jnp.cos(headings)[:, None, None] * jnp.cos(wind_angle)[None, None, :]
        + jnp.sin(headings)[:, None, None] * jnp.sin(wind_angle)[None, None, :]
    )
    forcing = WIND_FACTOR / GRAVITY * friction[None, None, :] * ang_freq[None, :, None] * alignment
    growth = WIND_GROWTH * ang_freq[None, :, None] * jnp.maximum(forcing - 1.0, 0.0)
    losses = ang_freq[None, :, None] * (
        SATURATION_LOSS * excess_sq
        + CUMULATIVE_LOSS * running
        + STEEPNESS_LOSS * (steepness * steepness)[None, None, :]
    )
    return spectra * (1.0 + TIME_STEP * growth) / (1.0 + TIME_STEP * losses)


def shards(spectrum, sea_mask, owner_list, owner_count, slopes, friction, wind_angle):
    comp_size = lax.axis_size("comp")
    local_comps = spectrum.shape[0]
    cell_count = spectrum.shape[1] * spectrum.shape[2]
    sea_cells = sea_mask.astype(jnp.float32)
    masked = spectrum * sea_cells[None]
    headings, ang_freq = wave_tables(lax.axis_index("comp") * local_comps, local_comps)
    padded_lon = padded(masked, (("tx", 1),), 1, True)
    padded_lat = padded(masked, (("ty", 2),), 1, False)
    padded_dir = padded(masked, (("comp", 0),), NFREQ, True)
    advected = (
        advect(
            masked,
            padded_lon[:, :-2],
            padded_lon[:, 2:],
            padded_lat[:, :, :-2],
            padded_lat[:, :, 2:],
            padded_dir[:local_comps],
            padded_dir[2 * NFREQ :],
            headings,
            ang_freq,
            slopes,
        )
        * sea_cells[None]
    )
    moved_flat = advected.reshape(local_comps, cell_count)
    cell_names = owner_list[0, 0]
    slot_ids = jnp.arange(cell_names.shape[1], dtype=jnp.int32)
    in_use = slot_ids[None, :] < owner_count[0, 0][:, None]
    target = jnp.where(in_use, cell_names, cell_count).reshape(-1)
    owners = cell_names.shape[0]
    capacity = cell_names.shape[1]
    tiles_x = lax.axis_size("tx")
    cell_ids = jnp.arange(cell_count, dtype=jnp.int32)
    selector = (cell_ids[:, None] == target[None, :]).astype(jnp.float32)
    outgoing = jnp.dot(moved_flat, selector, precision=lax.Precision.HIGHEST).reshape(
        local_comps, owners, capacity
    )
    wind_rows = jnp.stack([friction.reshape(-1), wind_angle.reshape(-1)])
    point_data = jnp.dot(wind_rows, selector, precision=lax.Precision.HIGHEST).reshape(
        2, owners, capacity
    )
    spectra = lax.all_to_all(outgoing, ("comp", "tx"), split_axis=1, concat_axis=1, tiled=True)
    extras = lax.all_to_all(point_data, ("comp", "tx"), split_axis=1, concat_axis=1, tiled=True)
    batch_size = spectra.shape[2]
    full_spec = (
        spectra.reshape(local_comps, comp_size, tiles_x * batch_size)
        .transpose(1, 0, 2)
        .reshape(NDIR, NFREQ, tiles_x * batch_size)
    )
    extra_rows = extras.reshape(2, comp_size, tiles_x * batch_size)[:, 0]
    result = source_terms(full_spec, extra_rows[0], extra_rows[1])
    homeward = (
        result.reshape(comp_size, local_comps, tiles_x * batch_size)
        .transpose(1, 0, 2)
        .reshape(local_comps, comp_size * tiles_x, batch_size)
    )
    returned = lax.all_to_all(homeward, ("comp", "tx"), split_axis=1, concat_axis=1, tiled=True)
    gathered = lax.dot_general(
        returned.reshape(local_comps, owners * capacity),
        selector,
        (((1,), (1,)), ((), ())),
        precision=lax.Precision.HIGHEST,
    )
    listed = jnp.sum(selector, axis=1) > 0.5
    updated = jnp.where(listed[None], gathered, moved_flat)
    return updated.reshape(spectrum.shape)


def chunk_bounds():
    return [(5 * i, 5 * i + 5) for i in range(10)]


HALO_GROUPS = ((0, 15), (15, 50))
HALF_DIRS = NDIR // 2
SIDE_DIRS = 8
LEAD_DIRS = 9
VMEM_BYTES = 24 * 1024 * 1024


def freq_table():
    freqs = np.arange(NFREQ, dtype=np.float64)
    return 2.0 * math.pi * LOW_FREQ * np.exp(freqs * (math.log(HIGH_FREQ / LOW_FREQ) / (NFREQ - 1)))


def heading(index):
    return 2.0 * math.pi * index / NDIR


def raw_kernel(spec_ref, raw_ref, sems):
    copies = []
    for i, d in enumerate((0, HALF_DIRS - 1)):
        copy = pltpu.make_async_copy(spec_ref.at[d], raw_ref.at[i], sems.at[i])
        copy.start()
        copies.append(copy)
    for copy in copies:
        copy.wait()


def raw_edges(spec):
    return pl.pallas_call(
        raw_kernel,
        out_shape=jax.ShapeDtypeStruct((2, NFREQ, 8, 256), jnp.float32),
        in_specs=[pl.BlockSpec(memory_space=pl.ANY)],
        out_specs=pl.BlockSpec(memory_space=pl.ANY),
        scratch_shapes=[pltpu.SemaphoreType.DMA((2,))],
        cost_estimate=pl.CostEstimate(flops=0, bytes_accessed=4 * NFREQ * 8192, transcendentals=0),
    )(spec)


def pack_kernel(first, count, with_lat, half_ref, sea_ref, spec_ref, after_ref, lead_ref, trail_ref, *rest):
    if with_lat:
        lat_ref, held, line, sems, line_sems = rest
    else:
        held, sems = rest

    def body(flipped):
        lead_row, trail_row = (0, 7) if flipped else (7, 0)
        part = 0 if flipped else 1
        copies = []
        for d in range(HALF_DIRS):
            for h in range(2):
                copy = pltpu.make_async_copy(
                    spec_ref.at[d, pl.ds(first, count), :, pl.ds(128 * h, 128)], held.at[h, d], sems.at[h, d]
                )
                copy.start()
                copies.append(copy)
        if with_lat:
            line_copies = []
            for d in range(HALF_DIRS):
                copy = pltpu.make_async_copy(spec_ref.at[d, :, :, pl.ds(128 * part, 128)], line.at[d], line_sems.at[d])
                copy.start()
                line_copies.append(copy)
        rows = held.reshape(2 * HALF_DIRS * count * 8, 128)
        for d in range(HALF_DIRS):
            for h in range(2):
                copies[2 * d + h].wait()
                lanes_here = slice(128 * h, 128 * h + 128)
                start = (h * HALF_DIRS + d) * count * 8
                if d < LEAD_DIRS:
                    column = rows[pl.ds(start + lead_row, count, stride=8), :]
                    lead_ref[d * count : (d + 1) * count, lanes_here] = column * sea_ref[lead_row : lead_row + 1, lanes_here]
                elif d > LEAD_DIRS:
                    t = d - LEAD_DIRS - 1
                    column = rows[pl.ds(start + trail_row, count, stride=8), :]
                    trail_ref[t * count : (t + 1) * count, lanes_here] = column * sea_ref[trail_row : trail_row + 1, lanes_here]
        if with_lat:
            lane = 0 if flipped else 127
            lanes = lax.broadcasted_iota(jnp.int32, (8, 128), 1)
            sea_line = jnp.broadcast_to(sea_ref[:, 128 * part + lane : 128 * part + lane + 1], (8, 128))
            for copy in line_copies:
                copy.wait()

            def one(f, kept):
                here = lanes == f
                return tuple(
                    jnp.where(here, jnp.broadcast_to(line[d, f][:, lane : lane + 1], (8, 128)), kept[d])
                    for d in range(HALF_DIRS)
                )

            zeros = jnp.zeros((8, 128), jnp.float32)
            kept = lax.fori_loop(0, NFREQ, one, (zeros,) * HALF_DIRS, unroll=2)
            for d in range(HALF_DIRS):
                lat_ref[d] = kept[d] * sea_line

    @pl.when(half_ref[0] == 0)
    def _():
        body(False)

    @pl.when(half_ref[0] != 0)
    def _():
        body(True)


def pack(first, count, with_lat, half, sea, spec, after):
    vmem = pl.BlockSpec(memory_space=pltpu.VMEM)
    out_shape = [
        jax.ShapeDtypeStruct((LEAD_DIRS * count, 256), jnp.float32),
        jax.ShapeDtypeStruct(((HALF_DIRS - LEAD_DIRS - 1) * count, 256), jnp.float32),
    ]
    scratch = [pltpu.VMEM((2, HALF_DIRS, count, 8, 128), jnp.float32), pltpu.SemaphoreType.DMA((2, HALF_DIRS))]
    if with_lat:
        out_shape.append(jax.ShapeDtypeStruct((HALF_DIRS, 8, 128), jnp.float32))
        scratch.insert(1, pltpu.VMEM((HALF_DIRS, NFREQ, 8, 128), jnp.float32))
        scratch.append(pltpu.SemaphoreType.DMA((HALF_DIRS,)))
    return pl.pallas_call(
        functools.partial(pack_kernel, first, count, with_lat),
        out_shape=out_shape,
        in_specs=[
            pl.BlockSpec(memory_space=pltpu.SMEM),
            vmem,
            pl.BlockSpec(memory_space=pl.ANY),
            pl.BlockSpec(memory_space=pl.ANY),
        ],
        out_specs=[vmem] * len(out_shape),
        scratch_shapes=scratch,
        compiler_params=pltpu.CompilerParams(vmem_limit_bytes=VMEM_BYTES),
        cost_estimate=pl.CostEstimate(flops=count * 18 * 2048, bytes_accessed=count * 18 * 8192, transcendentals=0),
    )(half, sea, spec, after)


def advect_kernel(
    first, count, group_first, group_count, stores, sums, carries, waits,
    half_ref, table_ref, sea_ref, slope_ref, spec_ref, lead_ref, trail_ref, lat_ref, raw_ref, steep_ref, *rest,
):
    rest = rest[waits:]
    held, turn, sem = rest[-3:]
    if stores:
        send_ref, keep_ref = rest[:2]
    if sums:
        steep_out_ref = rest[-4]
    copy = pltpu.make_async_copy(spec_ref.at[:, pl.ds(first, count)], held, sem)
    copy.start()
    for d in range(HALF_DIRS):
        turn[d] = math.sin(heading(d)) * slope_ref[0] - math.cos(heading(d)) * slope_ref[1]
    if sums:
        steep_out_ref[...] = steep_ref[...]
    if carries:
        send_ref[2 * SIDE_DIRS * count] = steep_ref[...]
    copy.wait()
    offset = first - group_first
    rows_at = lax.broadcasted_iota(jnp.int32, (8, 256), 0)
    lanes_at = lax.broadcasted_iota(jnp.int32, (8, 256), 1)
    per_cell = TIME_STEP / CELL_SIZE * GRAVITY / 2.0
    bending = TIME_STEP * NDIR / (2.0 * math.pi) * (2.0 * math.pi * LOW_FREQ)

    def body(flipped):
        lead_row, lead_shift = (7, 7) if flipped else (0, 1)
        trail_row, trail_shift = (0, 1) if flipped else (7, 7)
        lat_lane, lat_shift = (255, 255) if flipped else (0, 1)

        def one(f, nothing):
            sea = sea_ref[...]
            inverse = table_ref[0, first + f]
            weight = table_ref[1, first + f]
            total = jnp.zeros((8, 256), jnp.float32)
            prev = raw_ref[1, first + f] * sea
            here = held[0, f] * sea
            for d in range(HALF_DIRS):
                after = (held[d + 1, f] if d < HALF_DIRS - 1 else raw_ref[0, first + f]) * sea
                rate = turn[d]
                size = jnp.abs(rate) * bending
                moved = size * jnp.where(rate > 0.0, prev, after)
                along_x = per_cell * abs(math.cos(heading(d)))
                along_y = per_cell * abs(math.sin(heading(d)))
                fixed = 0.0
                if d != LEAD_DIRS:
                    if d < LEAD_DIRS:
                        row = lead_ref[pl.ds(d * group_count + offset + f, 1), :]
                        edge, shift = lead_row, lead_shift
                    else:
                        row = trail_ref[pl.ds((d - LEAD_DIRS - 1) * group_count + offset + f, 1), :]
                        edge, shift = trail_row, trail_shift
                    side = jnp.where(rows_at == edge, jnp.broadcast_to(row, (8, 256)), pltpu.roll(here, shift, 0))
                    moved = moved + along_x * side
                    fixed += along_x
                if d != 0:
                    halo = pltpu.roll(lat_ref[d], (lat_lane % 128) + 128 - (first + f), 1)
                    halo = jnp.concatenate([halo, halo], axis=1)
                    side = jnp.where(lanes_at == lat_lane, halo, pltpu.roll(here, lat_shift, 1))
                    moved = moved + along_y * side
                    fixed += along_y
                result = (here - inverse * ((size + fixed) * here - moved)) * sea
                if stores and d < SIDE_DIRS:
                    send_ref[d * count + f] = result
                elif stores and d < HALF_DIRS - SIDE_DIRS:
                    keep_ref[d - SIDE_DIRS, f] = result
                elif stores:
                    send_ref[(d - 2) * count + f] = result
                total = total + result
                prev, here = here, after
            if sums:
                steep_out_ref[...] += weight * total
            return nothing

        lax.fori_loop(0, count, one, 0)

    @pl.when(half_ref[0] == 0)
    def _():
        body(False)

    @pl.when(half_ref[0] != 0)
    def _():
        body(True)


def advect_chunk(first, count, group, stores, sums, carries, half, table, sea, slopes, spec, halos, steep, after):
    vmem = pl.BlockSpec(memory_space=pltpu.VMEM)
    smem = pl.BlockSpec(memory_space=pltpu.SMEM)
    hold = pl.BlockSpec(memory_space=pl.ANY)
    out_shape = []
    if stores:
        out_shape.append(jax.ShapeDtypeStruct((2 * SIDE_DIRS * count + carries, 8, 256), jnp.float32))
        out_shape.append(jax.ShapeDtypeStruct((HALF_DIRS - 2 * SIDE_DIRS, count, 8, 256), jnp.float32))
    if sums:
        out_shape.append(jax.ShapeDtypeStruct((8, 256), jnp.float32))
    return pl.pallas_call(
        functools.partial(advect_kernel, first, count, group[0], group[1] - group[0], stores, sums, carries, len(after)),
        out_shape=out_shape,
        in_specs=[smem, smem, vmem, vmem, hold, vmem, vmem, vmem, vmem, vmem] + [hold] * len(after),
        out_specs=[vmem] * len(out_shape),
        scratch_shapes=[
            pltpu.VMEM((HALF_DIRS, count, 8, 256), jnp.float32),
            pltpu.VMEM((HALF_DIRS, 8, 256), jnp.float32),
            pltpu.SemaphoreType.DMA,
        ],
        compiler_params=pltpu.CompilerParams(vmem_limit_bytes=VMEM_BYTES),
        cost_estimate=pl.CostEstimate(flops=count * 18 * 2048 * 25, bytes_accessed=count * 18 * 8192 * 2, transcendentals=0),
    )(half, table, sea, slopes, spec, *halos, steep, *after)


def source_kernel(first, count, chained, table_ref, wind_ref, steep_a_ref, steep_b_ref, cum_ref, own_ref, keep_ref, other_ref, *rest):
    out_ref, cum_out_ref, result, align, sem = rest[1:] if chained else rest
    weights = [math.cos(heading(m)) ** 2 / (9.0 * SATURATION_LEVEL) for m in range(SIDE_DIRS + 1)]
    steep = (steep_a_ref[...] + steep_b_ref[...]) * (1.0 / (NDIR * NFREQ))
    steep_sq = steep * steep
    for d in range(HALF_DIRS):
        align[d] = math.cos(heading(d)) * wind_ref[0] + math.sin(heading(d)) * wind_ref[1]
    cum_out_ref[...] = cum_ref[...]

    def one(f, nothing):
        omega = table_ref[2, first + f]
        gain = TIME_STEP * WIND_GROWTH * omega
        loss_sat = TIME_STEP * SATURATION_LOSS * omega
        loss_cum = TIME_STEP * CUMULATIVE_LOSS / NFREQ * omega
        loss_steep = TIME_STEP * STEEPNESS_LOSS * omega
        for half in range(2):
            lanes = slice(128 * half, 128 * half + 128)
            line = [other_ref[(SIDE_DIRS + i) * count + f, :, lanes] for i in range(SIDE_DIRS)]
            line += [own_ref[i * count + f, :, lanes] for i in range(SIDE_DIRS)]
            line += [keep_ref[i, f, :, lanes] for i in range(HALF_DIRS - 2 * SIDE_DIRS)]
            line += [own_ref[(SIDE_DIRS + i) * count + f, :, lanes] for i in range(SIDE_DIRS)]
            line += [other_ref[i * count + f, :, lanes] for i in range(SIDE_DIRS)]
            base = 1.0 + loss_steep * steep_sq[:, lanes]
            for d in range(HALF_DIRS):
                at = d + SIDE_DIRS
                level = weights[0] * line[at] - 1.0
                for m in range(1, SIDE_DIRS + 1):
                    level = level + weights[m] * (line[at - m] + line[at + m])
                excess = jnp.maximum(level, 0.0)
                square = excess * excess
                cum = cum_out_ref[d, :, lanes]
                cum_out_ref[d, :, lanes] = cum + square
                grown = 1.0 + gain * jnp.maximum(align[d, :, lanes] * omega - 1.0, 0.0)
                lost = base + loss_sat * square + loss_cum * cum
                result[d, f, :, lanes] = line[at] * grown / lost
        return nothing

    lax.fori_loop(0, count, one, 0)
    copy = pltpu.make_async_copy(result, out_ref.at[:, pl.ds(first, count)], sem)
    copy.start()
    copy.wait()


def source_chunk(first, count, table, wind, steep_own, steep_other, cum, own, keep, other, out):
    vmem = pl.BlockSpec(memory_space=pltpu.VMEM)
    chained = out is not None
    operands = (table, wind, steep_own, steep_other, cum, own, keep, other) + ((out,) if chained else ())
    return pl.pallas_call(
        functools.partial(source_kernel, first, count, chained),
        out_shape=(
            jax.ShapeDtypeStruct((HALF_DIRS, NFREQ, 8, 256), jnp.float32),
            jax.ShapeDtypeStruct((HALF_DIRS, 8, 256), jnp.float32),
        ),
        in_specs=[pl.BlockSpec(memory_space=pltpu.SMEM)]
        + [vmem] * 7
        + ([pl.BlockSpec(memory_space=pl.ANY)] if chained else []),
        out_specs=(pl.BlockSpec(memory_space=pl.ANY), vmem),
        scratch_shapes=[
            pltpu.VMEM((HALF_DIRS, count, 8, 256), jnp.float32),
            pltpu.VMEM((HALF_DIRS, 8, 256), jnp.float32),
            pltpu.SemaphoreType.DMA,
        ],
        input_output_aliases={8: 0} if chained else {},
        compiler_params=pltpu.CompilerParams(vmem_limit_bytes=VMEM_BYTES),
        cost_estimate=pl.CostEstimate(flops=count * 18 * 2048 * 55, bytes_accessed=count * 18 * 8192 * 3, transcendentals=0),
    )(*operands)


def ring_pairs(size, step, wrap):
    return [(i, (i + step) % size) for i in range(size) if wrap or 0 <= i + step < size]


def paired_shards(spectrum, sea_mask, owner_list, owner_count, slopes, friction, wind_angle):
    tiles_x, tiles_y = lax.axis_size("tx"), lax.axis_size("ty")
    half = lax.axis_index("comp")
    sign = 1.0 - 2.0 * half.astype(jnp.float32)
    half = half.astype(jnp.int32).reshape(1)
    spec = spectrum.reshape(HALF_DIRS, NFREQ, 8, 256)
    sea = sea_mask.astype(jnp.float32)
    turn = slopes * sign
    wind = (sign * WIND_FACTOR / GRAVITY) * friction * jnp.stack([jnp.cos(wind_angle), jnp.sin(wind_angle)])
    omega = freq_table()
    table = jnp.asarray(np.stack([1.0 / omega, (omega / omega[-1]) ** 2, omega]).astype(np.float32))

    def joined(axis_size, step, wrap):
        ahead = ring_pairs(axis_size, step, wrap)
        back = ring_pairs(axis_size, -step, wrap)
        return ahead + [(axis_size + i, axis_size + j) for i, j in back]

    swap = [(0, 1), (1, 0)]
    lead_pairs = joined(tiles_x, 1, True)
    trail_pairs = joined(tiles_x, -1, True)
    lat_pairs = joined(tiles_y, 1, False)

    spec = pltpu.with_memory_space_constraint(spec, pltpu.HBM)
    raw = raw_edges(spec)
    bounds = chunk_bounds()

    def halo(g, after):
        begin, end = HALO_GROUPS[g]
        edges = pack(begin, end - begin, g == 0, half, sea, spec, after)
        lead = lax.ppermute(edges[0], ("comp", "tx"), lead_pairs)
        trail = lax.ppermute(edges[1], ("comp", "tx"), trail_pairs)
        return lead, trail, edges[2] if g == 0 else None

    first_sides = halo(0, raw)
    lat = lax.ppermute(first_sides[2], ("comp", "ty"), lat_pairs)
    raw = lax.ppermute(raw, "comp", swap)

    def advect(begin, end, sides, stores, sums, carries, steep, after):
        group = HALO_GROUPS[0] if sides is first_sides else HALO_GROUPS[1]
        halos = (*sides[:2], lat, raw)
        return advect_chunk(
            begin, end - begin, group, stores, sums, carries, half, table, sea, turn, spec, halos, steep, after
        )

    sent, kept, received, sums = [], [], [], []

    def send(result):
        sent.append(result[0])
        kept.append(result[1])
        received.append(lax.ppermute(result[0], "comp", swap))

    def source(upto):
        for j in range(len(sums), upto):
            begin, end = bounds[j]
            state[:] = source_chunk(
                begin, end - begin, table, wind, steep, steep_other, state[1], sent[j], kept[j], received[j], state[0]
            )
            sums.append(state[1])

    steep = jnp.zeros((8, 256), jnp.float32)
    early = sum(end <= HALO_GROUPS[0][1] for _, end in bounds)
    for begin, end in bounds[:early]:
        result = advect(begin, end, first_sides, True, True, False, steep, ())
        send(result)
        steep = result[2]
    later_sides = halo(1, steep)
    state = [None, jnp.zeros((HALF_DIRS, 8, 256), jnp.float32)]
    for i in range(early, len(bounds)):
        after = (received[i - 2], received[i - 3])
        if i >= early + 4:
            source(min(i - 2, 2 * (i - early - 3)))
            after += (sums[-1],)
        send(advect(*bounds[i], later_sides, True, False, i == early + 1, steep, after))
        if i == early:
            (steep,) = advect(*HALO_GROUPS[1], later_sides, False, True, False, steep, (sent[i],))
        if i == early + 1:
            steep_other = received[i][-1]
    source(len(bounds))
    out = state[0]
    return out.reshape(spectrum.shape)


def fits_pairs(mesh, spectrum):
    return (
        mesh.shape["comp"] == 2
        and spectrum.shape[0] == NDIR * NFREQ
        and spectrum.shape[1] == 8 * mesh.shape["tx"]
        and spectrum.shape[2] == 256 * mesh.shape["ty"]
    )


def solution(mesh):
    in_specs = (
        P("comp", "tx", "ty"),
        P("tx", "ty"),
        P("tx", "ty", None, None),
        P("tx", "ty", None),
        P(None, "tx", "ty"),
        P("tx", "ty"),
        P("tx", "ty"),
    )
    out_specs = P("comp", "tx", "ty")

    def step(spectrum, *others):
        body = paired_shards if fits_pairs(mesh, spectrum) else shards
        mapped = jax.shard_map(body, mesh=mesh, in_specs=in_specs, out_specs=out_specs, check_vma=False)
        return mapped(spectrum, *others)

    return step
```

```python
import functools
import math

import jax
import jax.numpy as jnp
import numpy as np
from jax import lax
from jax.experimental import pallas as pl
from jax.experimental.pallas import tpu as pltpu
from jax.sharding import PartitionSpec as P

NDIR = 36
NFREQ = 50


TIME_STEP = 240.0
CELL_SIZE = 11100.0
GRAVITY = 9.81
LOW_FREQ = 0.0373
HIGH_FREQ = 1.0
WIND_GROWTH = 0.0001
WIND_FACTOR = 28.0
SATURATION_LOSS = 0.0005
CUMULATIVE_LOSS = 0.001
STEEPNESS_LOSS = 0.005
SATURATION_LEVEL = 0.6


def padded(value, sides, width, wrap):
    for axis, dim in sides:
        size, length = (lax.axis_size(axis), value.shape[dim])
        up = [(i, (i + 1) % size) for i in range(size if wrap else size - 1)]
        down = [(j, i) for i, j in up]
        last = lax.slice_in_dim(value, length - width, length, axis=dim)
        first = lax.slice_in_dim(value, 0, width, axis=dim)
        before = lax.ppermute(last, axis, up)
        after = lax.ppermute(first, axis, down)
        value = jnp.concatenate([before, value, after], axis=dim)
    return value


def freq_values(freq_ids):
    return (
        2.0
        * math.pi
        * LOW_FREQ
        * jnp.exp(freq_ids.astype(jnp.float32) * (math.log(HIGH_FREQ / LOW_FREQ) / (NFREQ - 1)))
    )


def wave_tables(first_comp, comp_count):
    comp_ids = first_comp + jnp.arange(comp_count, dtype=jnp.int32)
    headings = (comp_ids // NFREQ).astype(jnp.float32) * (2.0 * math.pi / NDIR)
    return (headings, freq_values(comp_ids % NFREQ))


def advect(
    energy,
    west_side,
    east_side,
    south_side,
    north_side,
    prev_dir,
    next_dir,
    headings,
    ang_freq,
    slopes,
):
    group_speed = GRAVITY / (2.0 * ang_freq)
    along_x = (TIME_STEP / CELL_SIZE * group_speed * jnp.cos(headings))[:, None, None]
    along_y = (TIME_STEP / CELL_SIZE * group_speed * jnp.sin(headings))[:, None, None]
    bending = TIME_STEP * NDIR / (2.0 * math.pi) * (2.0 * math.pi * LOW_FREQ) / ang_freq
    turning = bending[:, None, None] * (
        jnp.sin(headings)[:, None, None] * slopes[0][None]
        - jnp.cos(headings)[:, None, None] * slopes[1][None]
    )
    change = jnp.maximum(along_x, 0.0) * (energy - west_side) + jnp.minimum(along_x, 0.0) * (
        east_side - energy
    )
    change = (
        change
        + jnp.maximum(along_y, 0.0) * (energy - south_side)
        + jnp.minimum(along_y, 0.0) * (north_side - energy)
    )
    change = (
        change
        + jnp.maximum(turning, 0.0) * (energy - prev_dir)
        + jnp.minimum(turning, 0.0) * (next_dir - energy)
    )
    return energy - change


def source_terms(spectra, friction, wind_angle):
    dir_ids = jnp.arange(NDIR, dtype=jnp.int32)
    offset = (dir_ids[:, None] - dir_ids[None, :]) % NDIR
    nearest = jnp.minimum(offset, NDIR - offset)
    spread = jnp.where(
        4 * nearest < NDIR, jnp.cos(offset.astype(jnp.float32) * (2.0 * math.pi / NDIR)) ** 2, 0.0
    )
    spread = spread / jnp.sum(spread, axis=1, keepdims=True)
    sat_level = jnp.einsum("de,efp->dfp", spread, spectra, precision=lax.Precision.HIGHEST)
    excess = jnp.maximum(sat_level / SATURATION_LEVEL - 1.0, 0.0)
    excess_sq = excess * excess
    freq_ids = jnp.arange(NFREQ, dtype=jnp.int32)
    below_mask = (freq_ids[None, :] < freq_ids[:, None]).astype(jnp.float32)
    running = (
        jnp.einsum("fg,dgp->dfp", below_mask, excess_sq, precision=lax.Precision.HIGHEST) / NFREQ
    )
    ang_freq = freq_values(freq_ids)
    weights = (ang_freq / ang_freq[NFREQ - 1]) ** 2
    steepness = jnp.einsum("dfp,f->p", spectra, weights, precision=lax.Precision.HIGHEST) / (
        NDIR * NFREQ
    )
    headings = dir_ids.astype(jnp.float32) * (2.0 * math.pi / NDIR)
    alignment = (
        jnp.cos(headings)[:, None, None] * jnp.cos(wind_angle)[None, None, :]
        + jnp.sin(headings)[:, None, None] * jnp.sin(wind_angle)[None, None, :]
    )
    forcing = WIND_FACTOR / GRAVITY * friction[None, None, :] * ang_freq[None, :, None] * alignment
    growth = WIND_GROWTH * ang_freq[None, :, None] * jnp.maximum(forcing - 1.0, 0.0)
    losses = ang_freq[None, :, None] * (
        SATURATION_LOSS * excess_sq
        + CUMULATIVE_LOSS * running
        + STEEPNESS_LOSS * (steepness * steepness)[None, None, :]
    )
    return spectra * (1.0 + TIME_STEP * growth) / (1.0 + TIME_STEP * losses)


def shards(spectrum, sea_mask, owner_list, owner_count, slopes, friction, wind_angle):
    comp_size = lax.axis_size("comp")
    local_comps = spectrum.shape[0]
    cell_count = spectrum.shape[1] * spectrum.shape[2]
    sea_cells = sea_mask.astype(jnp.float32)
    masked = spectrum * sea_cells[None]
    headings, ang_freq = wave_tables(lax.axis_index("comp") * local_comps, local_comps)
    padded_lon = padded(masked, (("tx", 1),), 1, True)
    padded_lat = padded(masked, (("ty", 2),), 1, False)
    padded_dir = padded(masked, (("comp", 0),), NFREQ, True)
    advected = (
        advect(
            masked,
            padded_lon[:, :-2],
            padded_lon[:, 2:],
            padded_lat[:, :, :-2],
            padded_lat[:, :, 2:],
            padded_dir[:local_comps],
            padded_dir[2 * NFREQ :],
            headings,
            ang_freq,
            slopes,
        )
        * sea_cells[None]
    )
    moved_flat = advected.reshape(local_comps, cell_count)
    cell_names = owner_list[0, 0]
    slot_ids = jnp.arange(cell_names.shape[1], dtype=jnp.int32)
    in_use = slot_ids[None, :] < owner_count[0, 0][:, None]
    target = jnp.where(in_use, cell_names, cell_count).reshape(-1)
    owners = cell_names.shape[0]
    capacity = cell_names.shape[1]
    tiles_x = lax.axis_size("tx")
    cell_ids = jnp.arange(cell_count, dtype=jnp.int32)
    selector = (cell_ids[:, None] == target[None, :]).astype(jnp.float32)
    outgoing = jnp.dot(moved_flat, selector, precision=lax.Precision.HIGHEST).reshape(
        local_comps, owners, capacity
    )
    wind_rows = jnp.stack([friction.reshape(-1), wind_angle.reshape(-1)])
    point_data = jnp.dot(wind_rows, selector, precision=lax.Precision.HIGHEST).reshape(
        2, owners, capacity
    )
    spectra = lax.all_to_all(outgoing, ("comp", "tx"), split_axis=1, concat_axis=1, tiled=True)
    extras = lax.all_to_all(point_data, ("comp", "tx"), split_axis=1, concat_axis=1, tiled=True)
    batch_size = spectra.shape[2]
    full_spec = (
        spectra.reshape(local_comps, comp_size, tiles_x * batch_size)
        .transpose(1, 0, 2)
        .reshape(NDIR, NFREQ, tiles_x * batch_size)
    )
    extra_rows = extras.reshape(2, comp_size, tiles_x * batch_size)[:, 0]
    result = source_terms(full_spec, extra_rows[0], extra_rows[1])
    homeward = (
        result.reshape(comp_size, local_comps, tiles_x * batch_size)
        .transpose(1, 0, 2)
        .reshape(local_comps, comp_size * tiles_x, batch_size)
    )
    returned = lax.all_to_all(homeward, ("comp", "tx"), split_axis=1, concat_axis=1, tiled=True)
    gathered = lax.dot_general(
        returned.reshape(local_comps, owners * capacity),
        selector,
        (((1,), (1,)), ((), ())),
        precision=lax.Precision.HIGHEST,
    )
    listed = jnp.sum(selector, axis=1) > 0.5
    updated = jnp.where(listed[None], gathered, moved_flat)
    return updated.reshape(spectrum.shape)


def chunk_bounds():
    return [(5 * i, 5 * i + 5) for i in range(9)] + [(45, 48), (48, 50)]


HALO_GROUPS = ((0, 15), (15, 50))
HALF_DIRS = NDIR // 2
SIDE_DIRS = 8
LEAD_DIRS = 9
VMEM_BYTES = 24 * 1024 * 1024
SMALL_COST = pl.CostEstimate(flops=1024, bytes_accessed=1024, transcendentals=0)


def freq_table():
    freqs = np.arange(NFREQ, dtype=np.float64)
    return 2.0 * math.pi * LOW_FREQ * np.exp(freqs * (math.log(HIGH_FREQ / LOW_FREQ) / (NFREQ - 1)))


def heading(index):
    return 2.0 * math.pi * index / NDIR


def raw_kernel(spec_ref, raw_ref, sems):
    copies = []
    for i, d in enumerate((0, HALF_DIRS - 1)):
        copy = pltpu.make_async_copy(spec_ref.at[d], raw_ref.at[i], sems.at[i])
        copy.start()
        copies.append(copy)
    for copy in copies:
        copy.wait()


def raw_edges(spec):
    return pl.pallas_call(
        raw_kernel,
        out_shape=jax.ShapeDtypeStruct((2, NFREQ, 8, 256), jnp.float32),
        in_specs=[pl.BlockSpec(memory_space=pl.ANY)],
        out_specs=pl.BlockSpec(memory_space=pltpu.VMEM),
        scratch_shapes=[pltpu.SemaphoreType.DMA((2,))],
        compiler_params=pltpu.CompilerParams(vmem_limit_bytes=VMEM_BYTES),
        cost_estimate=SMALL_COST,
    )(spec)


def pack_kernel(first, count, half_ref, sea_ref, spec_ref, after_ref, lead_ref, trail_ref, lat_ref, held, sems):
    def body(flipped):
        lead_row, trail_row = (0, 7) if flipped else (7, 0)
        part = 0 if flipped else 1
        copies = []
        for d in range(HALF_DIRS):
            for h in range(2):
                copy = pltpu.make_async_copy(
                    spec_ref.at[d, pl.ds(first, count), :, pl.ds(128 * h, 128)], held.at[h, d], sems.at[h, d]
                )
                copy.start()
                copies.append(copy)
        rows = held.reshape(2 * HALF_DIRS * count * 8, 128)
        for d in range(HALF_DIRS):
            for h in range(2):
                copies[2 * d + h].wait()
                lanes_here = slice(128 * h, 128 * h + 128)
                start = (h * HALF_DIRS + d) * count * 8
                if d < LEAD_DIRS:
                    column = rows[pl.ds(start + lead_row, count, stride=8), :]
                    lead_ref[d * count : (d + 1) * count, lanes_here] = column * sea_ref[lead_row : lead_row + 1, lanes_here]
                elif d > LEAD_DIRS:
                    t = d - LEAD_DIRS - 1
                    column = rows[pl.ds(start + trail_row, count, stride=8), :]
                    trail_ref[t * count : (t + 1) * count, lanes_here] = column * sea_ref[trail_row : trail_row + 1, lanes_here]
        lane = 0 if flipped else 127
        lanes = lax.broadcasted_iota(jnp.int32, (8, 128), 1)
        sea_line = jnp.broadcast_to(sea_ref[:, 128 * part + lane : 128 * part + lane + 1], (8, 128))

        def one(f, kept):
            here = lanes == f
            return tuple(
                jnp.where(here, jnp.broadcast_to(held[part, d, f][:, lane : lane + 1], (8, 128)), kept[d])
                for d in range(HALF_DIRS)
            )

        zeros = jnp.zeros((8, 128), jnp.float32)
        kept = lax.fori_loop(0, count, one, (zeros,) * HALF_DIRS, unroll=5)
        for d in range(HALF_DIRS):
            lat_ref[d] = kept[d] * sea_line

    @pl.when(half_ref[0] == 0)
    def _():
        body(False)

    @pl.when(half_ref[0] != 0)
    def _():
        body(True)


def pack(first, count, half, sea, spec, after):
    vmem = pl.BlockSpec(memory_space=pltpu.VMEM)
    hold = pl.BlockSpec(memory_space=pl.ANY)
    return pl.pallas_call(
        functools.partial(pack_kernel, first, count),
        out_shape=[
            jax.ShapeDtypeStruct((LEAD_DIRS * count, 256), jnp.float32),
            jax.ShapeDtypeStruct(((HALF_DIRS - LEAD_DIRS - 1) * count, 256), jnp.float32),
            jax.ShapeDtypeStruct((HALF_DIRS, 8, 128), jnp.float32),
        ],
        in_specs=[pl.BlockSpec(memory_space=pltpu.SMEM), vmem, hold, hold],
        out_specs=[vmem] * 3,
        scratch_shapes=[
            pltpu.VMEM((2, HALF_DIRS, count, 8, 128), jnp.float32),
            pltpu.SemaphoreType.DMA((2, HALF_DIRS)),
        ],
        compiler_params=pltpu.CompilerParams(vmem_limit_bytes=VMEM_BYTES),
        cost_estimate=SMALL_COST,
    )(half, sea, spec, after)


ALL_DIRS = tuple(range(HALF_DIRS))
INNER_DIRS = ALL_DIRS[1:-1]
OUTER_DIRS = (0, HALF_DIRS - 1)


def is_sent(d):
    return d < SIDE_DIRS or d >= HALF_DIRS - SIDE_DIRS


def slab_index(dirs, count, base=0):
    return {d: base + count * n for n, d in enumerate(d for d in dirs if is_sent(d))}


def advect_kernel(
    load, group, passes, sums, carries, waits, has_raw,
    half_ref, table_ref, sea_ref, slope_ref, spec_ref, lead_ref, trail_ref, lat_ref, steep_ref, *rest,
):
    raw_ref = rest[0] if has_raw else None
    rest = rest[has_raw + waits :]
    held, turn, sem = rest[-3:]
    stores = any(slabs is not None for _, _, _, slabs in passes)
    if stores:
        send_ref, keep_ref = rest[:2]
    if sums:
        steep_out_ref = rest[-4]
    copy = pltpu.make_async_copy(spec_ref.at[:, pl.ds(load[0], load[1] - load[0])], held, sem)
    copy.start()
    for d in range(HALF_DIRS):
        turn[d] = math.sin(heading(d)) * slope_ref[0] - math.cos(heading(d)) * slope_ref[1]
    if sums:
        steep_out_ref[...] = steep_ref[...]
    if carries:
        send_ref[send_ref.shape[0] - 1] = steep_ref[...]
    copy.wait()
    rows_at = lax.broadcasted_iota(jnp.int32, (8, 256), 0)
    lanes_at = lax.broadcasted_iota(jnp.int32, (8, 256), 1)
    per_cell = TIME_STEP / CELL_SIZE * GRAVITY / 2.0
    bending = TIME_STEP * NDIR / (2.0 * math.pi) * (2.0 * math.pi * LOW_FREQ)
    group_count = group[1] - group[0]

    def body(flipped):
        lead_row, lead_shift = (7, 7) if flipped else (0, 1)
        trail_row, trail_shift = (0, 1) if flipped else (7, 7)
        lat_lane, lat_shift = (255, 255) if flipped else (0, 1)

        def one(first, dirs, slabs, f, nothing):
            sea = sea_ref[...]
            inverse = table_ref[0, first + f]
            weight = table_ref[1, first + f]
            total = jnp.zeros((8, 256), jnp.float32)
            offset = first - group[0]

            def energy(d):
                if d < 0:
                    return raw_ref[1, first + f] * sea
                if d >= HALF_DIRS:
                    return raw_ref[0, first + f] * sea
                return held[d, first - load[0] + f] * sea

            known = {}
            for d in dirs:
                known = {e: known[e] if e in known else energy(e) for e in (d - 1, d, d + 1)}
                prev, here, after = known[d - 1], known[d], known[d + 1]
                rate = turn[d]
                size = jnp.abs(rate) * bending
                moved = size * jnp.where(rate > 0.0, prev, after)
                along_x = per_cell * abs(math.cos(heading(d)))
                along_y = per_cell * abs(math.sin(heading(d)))
                fixed = 0.0
                if d != LEAD_DIRS:
                    if d < LEAD_DIRS:
                        row = lead_ref[pl.ds(d * group_count + offset + f, 1), :]
                        edge, shift = lead_row, lead_shift
                    else:
                        row = trail_ref[pl.ds((d - LEAD_DIRS - 1) * group_count + offset + f, 1), :]
                        edge, shift = trail_row, trail_shift
                    side = jnp.where(rows_at == edge, jnp.broadcast_to(row, (8, 256)), pltpu.roll(here, shift, 0))
                    moved = moved + along_x * side
                    fixed += along_x
                if d != 0:
                    halo = pltpu.roll(lat_ref[d], (lat_lane % 128) + 128 - (offset + f), 1)
                    halo = jnp.concatenate([halo, halo], axis=1)
                    side = jnp.where(lanes_at == lat_lane, halo, pltpu.roll(here, lat_shift, 1))
                    moved = moved + along_y * side
                    fixed += along_y
                result = (here - inverse * ((size + fixed) * here - moved)) * sea
                if slabs is not None and is_sent(d):
                    send_ref[slabs[d] + f] = result
                elif slabs is not None:
                    keep_ref[d - SIDE_DIRS, f] = result
                total = total + result
            if sums:
                steep_out_ref[...] += weight * total
            return nothing

        for first, count, dirs, slabs in passes:
            lax.fori_loop(0, count, functools.partial(one, first, dirs, slabs), 0)

    @pl.when(half_ref[0] == 0)
    def _():
        body(False)

    @pl.when(half_ref[0] != 0)
    def _():
        body(True)


def advect_chunk(passes, group, sums, carries, half, table, sea, slopes, spec, sides, steep, raw, after):
    vmem = pl.BlockSpec(memory_space=pltpu.VMEM)
    smem = pl.BlockSpec(memory_space=pltpu.SMEM)
    hold = pl.BlockSpec(memory_space=pl.ANY)
    load = (min(p[0] for p in passes), max(p[0] + p[1] for p in passes))
    slabs = sum(count * len(place) for _, count, _, place in passes if place is not None)
    raw = () if raw is None else (raw,)
    out_shape = []
    if slabs:
        out_shape.append(jax.ShapeDtypeStruct((slabs + carries, 8, 256), jnp.float32))
        out_shape.append(jax.ShapeDtypeStruct((HALF_DIRS - 2 * SIDE_DIRS, passes[0][1], 8, 256), jnp.float32))
    if sums:
        out_shape.append(jax.ShapeDtypeStruct((8, 256), jnp.float32))
    return pl.pallas_call(
        functools.partial(advect_kernel, load, group, passes, sums, carries, len(after), len(raw)),
        out_shape=out_shape,
        in_specs=[smem, smem, vmem, vmem, hold, vmem, vmem, vmem, vmem] + [vmem] * len(raw) + [hold] * len(after),
        out_specs=[vmem] * len(out_shape),
        scratch_shapes=[
            pltpu.VMEM((HALF_DIRS, load[1] - load[0], 8, 256), jnp.float32),
            pltpu.VMEM((HALF_DIRS, 8, 256), jnp.float32),
            pltpu.SemaphoreType.DMA,
        ],
        compiler_params=pltpu.CompilerParams(vmem_limit_bytes=VMEM_BYTES),
        cost_estimate=SMALL_COST,
    )(half, table, sea, slopes, spec, *sides, steep, *raw, *after)


def source_kernel(
    first, count, inner, outer, chained,
    table_ref, wind_ref, steep_a_ref, steep_b_ref, cum_ref, own_ref, keep_ref, other_ref, *rest,
):
    edge_own_ref, edge_other_ref = rest[:2] if outer else (None, None)
    rest = rest[(2 if outer else 0) + chained :]
    out_ref, cum_out_ref, result, align, sem = rest
    weights = [math.cos(heading(m)) ** 2 / (9.0 * SATURATION_LEVEL) for m in range(SIDE_DIRS + 1)]
    steep = (steep_a_ref[...] + steep_b_ref[...]) * (1.0 / (NDIR * NFREQ))
    steep_sq = steep * steep
    for d in range(HALF_DIRS):
        align[d] = math.cos(heading(d)) * wind_ref[0] + math.sin(heading(d)) * wind_ref[1]
    cum_out_ref[...] = cum_ref[...]

    def one(f, nothing):
        omega = table_ref[2, first + f]
        gain = TIME_STEP * WIND_GROWTH * omega
        loss_sat = TIME_STEP * SATURATION_LOSS * omega
        loss_cum = TIME_STEP * CUMULATIVE_LOSS / NFREQ * omega
        loss_steep = TIME_STEP * STEEPNESS_LOSS * omega
        for half in range(2):
            lanes = slice(128 * half, 128 * half + 128)

            def slab(d, main, edge):
                return main[inner[d] + f, :, lanes] if d in inner else edge[outer[d] + f, :, lanes]

            first_dirs, last_dirs = ALL_DIRS[:SIDE_DIRS], ALL_DIRS[-SIDE_DIRS:]
            line = [slab(d, other_ref, edge_other_ref) for d in last_dirs]
            line += [slab(d, own_ref, edge_own_ref) for d in first_dirs]
            line += [keep_ref[i, f, :, lanes] for i in range(HALF_DIRS - 2 * SIDE_DIRS)]
            line += [slab(d, own_ref, edge_own_ref) for d in last_dirs]
            line += [slab(d, other_ref, edge_other_ref) for d in first_dirs]
            base = 1.0 + loss_steep * steep_sq[:, lanes]
            for d in range(HALF_DIRS):
                at = d + SIDE_DIRS
                level = weights[0] * line[at] - 1.0
                for m in range(1, SIDE_DIRS + 1):
                    level = level + weights[m] * (line[at - m] + line[at + m])
                excess = jnp.maximum(level, 0.0)
                square = excess * excess
                cum = cum_out_ref[d, :, lanes]
                cum_out_ref[d, :, lanes] = cum + square
                grown = 1.0 + gain * jnp.maximum(align[d, :, lanes] * omega - 1.0, 0.0)
                lost = base + loss_sat * square + loss_cum * cum
                result[d, f, :, lanes] = line[at] * grown / lost
        return nothing

    lax.fori_loop(0, count, one, 0)
    copy = pltpu.make_async_copy(result, out_ref.at[:, pl.ds(first, count)], sem)
    copy.start()
    copy.wait()


def source_chunk(first, count, inner, outer, table, wind, steep_own, steep_other, cum, own, keep, other, edges, out):
    vmem = pl.BlockSpec(memory_space=pltpu.VMEM)
    hold = pl.BlockSpec(memory_space=pl.ANY)
    chained = out is not None
    operands = (table, wind, steep_own, steep_other, cum, own, keep, other, *edges) + ((out,) if chained else ())
    return pl.pallas_call(
        functools.partial(source_kernel, first, count, inner, outer, chained),
        out_shape=(
            jax.ShapeDtypeStruct((HALF_DIRS, NFREQ, 8, 256), jnp.float32),
            jax.ShapeDtypeStruct((HALF_DIRS, 8, 256), jnp.float32),
        ),
        in_specs=[pl.BlockSpec(memory_space=pltpu.SMEM)] + [vmem] * (7 + len(edges)) + [hold] * chained,
        out_specs=(hold, vmem),
        scratch_shapes=[
            pltpu.VMEM((HALF_DIRS, count, 8, 256), jnp.float32),
            pltpu.VMEM((HALF_DIRS, 8, 256), jnp.float32),
            pltpu.SemaphoreType.DMA,
        ],
        input_output_aliases={len(operands) - 1: 0} if chained else {},
        compiler_params=pltpu.CompilerParams(vmem_limit_bytes=VMEM_BYTES),
        cost_estimate=SMALL_COST,
    )(*operands)


def ring_pairs(size, step, wrap):
    return [(i, (i + step) % size) for i in range(size) if wrap or 0 <= i + step < size]


def paired_shards(spectrum, sea_mask, owner_list, owner_count, slopes, friction, wind_angle):
    tiles_x, tiles_y = lax.axis_size("tx"), lax.axis_size("ty")
    half = lax.axis_index("comp")
    sign = 1.0 - 2.0 * half.astype(jnp.float32)
    half = half.astype(jnp.int32).reshape(1)
    spec = spectrum.reshape(HALF_DIRS, NFREQ, 8, 256)
    sea = sea_mask.astype(jnp.float32)
    turn = slopes * sign
    wind = (sign * WIND_FACTOR / GRAVITY) * friction * jnp.stack([jnp.cos(wind_angle), jnp.sin(wind_angle)])
    omega = freq_table()
    table = jnp.asarray(np.stack([1.0 / omega, (omega / omega[-1]) ** 2, omega]).astype(np.float32))

    def joined(axis_size, step, wrap):
        ahead = ring_pairs(axis_size, step, wrap)
        back = ring_pairs(axis_size, -step, wrap)
        return ahead + [(axis_size + i, axis_size + j) for i, j in back]

    swap = [(0, 1), (1, 0)]
    lead_pairs = joined(tiles_x, 1, True)
    trail_pairs = joined(tiles_x, -1, True)
    lat_pairs = joined(tiles_y, 1, False)

    spec = pltpu.with_memory_space_constraint(spec, pltpu.HBM)
    bounds = chunk_bounds()
    raw = raw_edges(spec)

    def halo(g, after):
        begin, end = HALO_GROUPS[g]
        lead, trail, lat = pack(begin, end - begin, half, sea, spec, after)
        return (
            lax.ppermute(lead, ("comp", "tx"), lead_pairs),
            lax.ppermute(trail, ("comp", "tx"), trail_pairs),
            lax.ppermute(lat, ("comp", "ty"), lat_pairs),
        )

    first_sides = halo(0, raw)
    raw = lax.ppermute(raw, "comp", swap)
    early = sum(end <= HALO_GROUPS[0][1] for _, end in bounds)
    counts = [end - begin for begin, end in bounds]
    places = [slab_index(INNER_DIRS if i == 0 else ALL_DIRS, counts[i]) for i in range(len(bounds))]
    edge_place = slab_index(OUTER_DIRS, counts[0], base=2 * SIDE_DIRS * counts[1])

    def advect(passes, sides, sums, carries, steep, raw, after):
        group = HALO_GROUPS[0] if sides is first_sides else HALO_GROUPS[1]
        return advect_chunk(passes, group, sums, carries, half, table, sea, turn, spec, sides, steep, raw, after)

    sent, kept, received, sums = [], [], [], []

    def send(result):
        sent.append(result[0])
        kept.append(result[1])
        received.append(lax.ppermute(result[0], "comp", swap))

    def source(upto):
        for j in range(len(sums), upto):
            outer, edges = (edge_place, (sent[1], received[1])) if j == 0 else (None, ())
            state[:] = source_chunk(
                bounds[j][0], counts[j], places[j], outer, table, wind, steep, steep_other,
                state[1], sent[j], kept[j], received[j], edges, state[0],
            )
            sums.append(state[1])

    steep = jnp.zeros((8, 256), jnp.float32)
    for i in range(early):
        passes = [(bounds[i][0], counts[i], INNER_DIRS if i == 0 else ALL_DIRS, places[i])]
        if i == 1:
            passes.append((bounds[0][0], counts[0], OUTER_DIRS, edge_place))
        result = advect(passes, first_sides, True, False, steep, raw if i else None, tuple(received[: max(i - 1, 0)]))
        send(result)
        steep = result[2]
        if i == 1:
            later_sides = halo(1, steep)
    state = [None, jnp.zeros((HALF_DIRS, 8, 256), jnp.float32)]
    for i in range(early, len(bounds)):
        after = (received[i - 2],)
        if i >= early + 4:
            source(min(i - 2, 2 * (i - early - 3)))
            after += (sums[-1],)
        passes = [(bounds[i][0], counts[i], ALL_DIRS, places[i])]
        send(advect(passes, later_sides, False, i == early + 1, steep, raw, after))
        if i == early:
            rest = [(HALO_GROUPS[1][0], NFREQ - HALO_GROUPS[1][0], ALL_DIRS, None)]
            (steep,) = advect(rest, later_sides, True, False, steep, raw, (sent[i],))
        if i == early + 1:
            steep_other = received[i][-1]
    source(len(bounds))
    out = state[0]
    return out.reshape(spectrum.shape)


def fits_pairs(mesh, spectrum):
    return (
        mesh.shape["comp"] == 2
        and spectrum.shape[0] == NDIR * NFREQ
        and spectrum.shape[1] == 8 * mesh.shape["tx"]
        and spectrum.shape[2] == 256 * mesh.shape["ty"]
    )


def solution(mesh):
    in_specs = (
        P("comp", "tx", "ty"),
        P("tx", "ty"),
        P("tx", "ty", None, None),
        P("tx", "ty", None),
        P(None, "tx", "ty"),
        P("tx", "ty"),
        P("tx", "ty"),
    )
    out_specs = P("comp", "tx", "ty")

    def step(spectrum, *others):
        body = paired_shards if fits_pairs(mesh, spectrum) else shards
        mapped = jax.shard_map(body, mesh=mesh, in_specs=in_specs, out_specs=out_specs, check_vma=False)
        return mapped(spectrum, *others)

    return step
```

```python
import functools
import math

import jax
import jax.numpy as jnp
import numpy as np
from jax import lax
from jax.experimental import pallas as pl
from jax.experimental.pallas import tpu as pltpu
from jax.sharding import PartitionSpec as P

NDIR = 36
NFREQ = 50


TIME_STEP = 240.0
CELL_SIZE = 11100.0
GRAVITY = 9.81
LOW_FREQ = 0.0373
HIGH_FREQ = 1.0
WIND_GROWTH = 0.0001
WIND_FACTOR = 28.0
SATURATION_LOSS = 0.0005
CUMULATIVE_LOSS = 0.001
STEEPNESS_LOSS = 0.005
SATURATION_LEVEL = 0.6


def padded(value, sides, width, wrap):
    for axis, dim in sides:
        size, length = (lax.axis_size(axis), value.shape[dim])
        up = [(i, (i + 1) % size) for i in range(size if wrap else size - 1)]
        down = [(j, i) for i, j in up]
        last = lax.slice_in_dim(value, length - width, length, axis=dim)
        first = lax.slice_in_dim(value, 0, width, axis=dim)
        before = lax.ppermute(last, axis, up)
        after = lax.ppermute(first, axis, down)
        value = jnp.concatenate([before, value, after], axis=dim)
    return value


def freq_values(freq_ids):
    return (
        2.0
        * math.pi
        * LOW_FREQ
        * jnp.exp(freq_ids.astype(jnp.float32) * (math.log(HIGH_FREQ / LOW_FREQ) / (NFREQ - 1)))
    )


def wave_tables(first_comp, comp_count):
    comp_ids = first_comp + jnp.arange(comp_count, dtype=jnp.int32)
    headings = (comp_ids // NFREQ).astype(jnp.float32) * (2.0 * math.pi / NDIR)
    return (headings, freq_values(comp_ids % NFREQ))


def advect(
    energy,
    west_side,
    east_side,
    south_side,
    north_side,
    prev_dir,
    next_dir,
    headings,
    ang_freq,
    slopes,
):
    group_speed = GRAVITY / (2.0 * ang_freq)
    along_x = (TIME_STEP / CELL_SIZE * group_speed * jnp.cos(headings))[:, None, None]
    along_y = (TIME_STEP / CELL_SIZE * group_speed * jnp.sin(headings))[:, None, None]
    bending = TIME_STEP * NDIR / (2.0 * math.pi) * (2.0 * math.pi * LOW_FREQ) / ang_freq
    turning = bending[:, None, None] * (
        jnp.sin(headings)[:, None, None] * slopes[0][None]
        - jnp.cos(headings)[:, None, None] * slopes[1][None]
    )
    change = jnp.maximum(along_x, 0.0) * (energy - west_side) + jnp.minimum(along_x, 0.0) * (
        east_side - energy
    )
    change = (
        change
        + jnp.maximum(along_y, 0.0) * (energy - south_side)
        + jnp.minimum(along_y, 0.0) * (north_side - energy)
    )
    change = (
        change
        + jnp.maximum(turning, 0.0) * (energy - prev_dir)
        + jnp.minimum(turning, 0.0) * (next_dir - energy)
    )
    return energy - change


def source_terms(spectra, friction, wind_angle):
    dir_ids = jnp.arange(NDIR, dtype=jnp.int32)
    offset = (dir_ids[:, None] - dir_ids[None, :]) % NDIR
    nearest = jnp.minimum(offset, NDIR - offset)
    spread = jnp.where(
        4 * nearest < NDIR, jnp.cos(offset.astype(jnp.float32) * (2.0 * math.pi / NDIR)) ** 2, 0.0
    )
    spread = spread / jnp.sum(spread, axis=1, keepdims=True)
    sat_level = jnp.einsum("de,efp->dfp", spread, spectra, precision=lax.Precision.HIGHEST)
    excess = jnp.maximum(sat_level / SATURATION_LEVEL - 1.0, 0.0)
    excess_sq = excess * excess
    freq_ids = jnp.arange(NFREQ, dtype=jnp.int32)
    below_mask = (freq_ids[None, :] < freq_ids[:, None]).astype(jnp.float32)
    running = (
        jnp.einsum("fg,dgp->dfp", below_mask, excess_sq, precision=lax.Precision.HIGHEST) / NFREQ
    )
    ang_freq = freq_values(freq_ids)
    weights = (ang_freq / ang_freq[NFREQ - 1]) ** 2
    steepness = jnp.einsum("dfp,f->p", spectra, weights, precision=lax.Precision.HIGHEST) / (
        NDIR * NFREQ
    )
    headings = dir_ids.astype(jnp.float32) * (2.0 * math.pi / NDIR)
    alignment = (
        jnp.cos(headings)[:, None, None] * jnp.cos(wind_angle)[None, None, :]
        + jnp.sin(headings)[:, None, None] * jnp.sin(wind_angle)[None, None, :]
    )
    forcing = WIND_FACTOR / GRAVITY * friction[None, None, :] * ang_freq[None, :, None] * alignment
    growth = WIND_GROWTH * ang_freq[None, :, None] * jnp.maximum(forcing - 1.0, 0.0)
    losses = ang_freq[None, :, None] * (
        SATURATION_LOSS * excess_sq
        + CUMULATIVE_LOSS * running
        + STEEPNESS_LOSS * (steepness * steepness)[None, None, :]
    )
    return spectra * (1.0 + TIME_STEP * growth) / (1.0 + TIME_STEP * losses)


def shards(spectrum, sea_mask, owner_list, owner_count, slopes, friction, wind_angle):
    comp_size = lax.axis_size("comp")
    local_comps = spectrum.shape[0]
    cell_count = spectrum.shape[1] * spectrum.shape[2]
    sea_cells = sea_mask.astype(jnp.float32)
    masked = spectrum * sea_cells[None]
    headings, ang_freq = wave_tables(lax.axis_index("comp") * local_comps, local_comps)
    padded_lon = padded(masked, (("tx", 1),), 1, True)
    padded_lat = padded(masked, (("ty", 2),), 1, False)
    padded_dir = padded(masked, (("comp", 0),), NFREQ, True)
    advected = (
        advect(
            masked,
            padded_lon[:, :-2],
            padded_lon[:, 2:],
            padded_lat[:, :, :-2],
            padded_lat[:, :, 2:],
            padded_dir[:local_comps],
            padded_dir[2 * NFREQ :],
            headings,
            ang_freq,
            slopes,
        )
        * sea_cells[None]
    )
    moved_flat = advected.reshape(local_comps, cell_count)
    cell_names = owner_list[0, 0]
    slot_ids = jnp.arange(cell_names.shape[1], dtype=jnp.int32)
    in_use = slot_ids[None, :] < owner_count[0, 0][:, None]
    target = jnp.where(in_use, cell_names, cell_count).reshape(-1)
    owners = cell_names.shape[0]
    capacity = cell_names.shape[1]
    tiles_x = lax.axis_size("tx")
    cell_ids = jnp.arange(cell_count, dtype=jnp.int32)
    selector = (cell_ids[:, None] == target[None, :]).astype(jnp.float32)
    outgoing = jnp.dot(moved_flat, selector, precision=lax.Precision.HIGHEST).reshape(
        local_comps, owners, capacity
    )
    wind_rows = jnp.stack([friction.reshape(-1), wind_angle.reshape(-1)])
    point_data = jnp.dot(wind_rows, selector, precision=lax.Precision.HIGHEST).reshape(
        2, owners, capacity
    )
    spectra = lax.all_to_all(outgoing, ("comp", "tx"), split_axis=1, concat_axis=1, tiled=True)
    extras = lax.all_to_all(point_data, ("comp", "tx"), split_axis=1, concat_axis=1, tiled=True)
    batch_size = spectra.shape[2]
    full_spec = (
        spectra.reshape(local_comps, comp_size, tiles_x * batch_size)
        .transpose(1, 0, 2)
        .reshape(NDIR, NFREQ, tiles_x * batch_size)
    )
    extra_rows = extras.reshape(2, comp_size, tiles_x * batch_size)[:, 0]
    result = source_terms(full_spec, extra_rows[0], extra_rows[1])
    homeward = (
        result.reshape(comp_size, local_comps, tiles_x * batch_size)
        .transpose(1, 0, 2)
        .reshape(local_comps, comp_size * tiles_x, batch_size)
    )
    returned = lax.all_to_all(homeward, ("comp", "tx"), split_axis=1, concat_axis=1, tiled=True)
    gathered = lax.dot_general(
        returned.reshape(local_comps, owners * capacity),
        selector,
        (((1,), (1,)), ((), ())),
        precision=lax.Precision.HIGHEST,
    )
    listed = jnp.sum(selector, axis=1) > 0.5
    updated = jnp.where(listed[None], gathered, moved_flat)
    return updated.reshape(spectrum.shape)


def chunk_bounds():
    return [(5 * i, 5 * i + 5) for i in range(9)] + [(45, 48), (48, 50)]


HALO_GROUPS = ((0, 15), (15, 50))
SUM_CHUNKS = 3
SOURCES_DONE = {8: 2, 9: 5, 10: 7}
HALF_DIRS = NDIR // 2
SIDE_DIRS = 8
LEAD_DIRS = 9
VMEM_BYTES = 24 * 1024 * 1024
SMALL_COST = pl.CostEstimate(flops=1024, bytes_accessed=1024, transcendentals=0)


def freq_table():
    freqs = np.arange(NFREQ, dtype=np.float64)
    return 2.0 * math.pi * LOW_FREQ * np.exp(freqs * (math.log(HIGH_FREQ / LOW_FREQ) / (NFREQ - 1)))


def heading(index):
    return 2.0 * math.pi * index / NDIR


def raw_kernel(spec_ref, raw_ref, sems):
    copies = []
    for i, d in enumerate((0, HALF_DIRS - 1)):
        copy = pltpu.make_async_copy(spec_ref.at[d], raw_ref.at[i], sems.at[i])
        copy.start()
        copies.append(copy)
    for copy in copies:
        copy.wait()


def raw_edges(spec):
    return pl.pallas_call(
        raw_kernel,
        out_shape=jax.ShapeDtypeStruct((2, NFREQ, 8, 256), jnp.float32),
        in_specs=[pl.BlockSpec(memory_space=pl.ANY)],
        out_specs=pl.BlockSpec(memory_space=pltpu.VMEM),
        scratch_shapes=[pltpu.SemaphoreType.DMA((2,))],
        compiler_params=pltpu.CompilerParams(vmem_limit_bytes=VMEM_BYTES),
        cost_estimate=SMALL_COST,
    )(spec)


def pack_kernel(first, count, half_ref, sea_ref, spec_ref, after_ref, lead_ref, trail_ref, lat_ref, held, sems):
    def body(flipped):
        lead_row, trail_row = (0, 7) if flipped else (7, 0)
        part = 0 if flipped else 1
        copies = []
        for d in range(HALF_DIRS):
            for h in range(2):
                copy = pltpu.make_async_copy(
                    spec_ref.at[d, pl.ds(first, count), :, pl.ds(128 * h, 128)], held.at[h, d], sems.at[h, d]
                )
                copy.start()
                copies.append(copy)
        rows = held.reshape(2 * HALF_DIRS * count * 8, 128)
        for d in range(HALF_DIRS):
            for h in range(2):
                copies[2 * d + h].wait()
                lanes_here = slice(128 * h, 128 * h + 128)
                start = (h * HALF_DIRS + d) * count * 8
                if d < LEAD_DIRS:
                    column = rows[pl.ds(start + lead_row, count, stride=8), :]
                    lead_ref[d * count : (d + 1) * count, lanes_here] = column * sea_ref[lead_row : lead_row + 1, lanes_here]
                elif d > LEAD_DIRS:
                    t = d - LEAD_DIRS - 1
                    column = rows[pl.ds(start + trail_row, count, stride=8), :]
                    trail_ref[t * count : (t + 1) * count, lanes_here] = column * sea_ref[trail_row : trail_row + 1, lanes_here]
        lane = 0 if flipped else 127
        lanes = lax.broadcasted_iota(jnp.int32, (8, 128), 1)
        sea_line = jnp.broadcast_to(sea_ref[:, 128 * part + lane : 128 * part + lane + 1], (8, 128))

        def one(f, kept):
            here = lanes == f
            return tuple(
                jnp.where(here, jnp.broadcast_to(held[part, d, f][:, lane : lane + 1], (8, 128)), kept[d])
                for d in range(HALF_DIRS)
            )

        zeros = jnp.zeros((8, 128), jnp.float32)
        kept = lax.fori_loop(0, count, one, (zeros,) * HALF_DIRS, unroll=5)
        for d in range(HALF_DIRS):
            lat_ref[d] = kept[d] * sea_line

    @pl.when(half_ref[0] == 0)
    def _():
        body(False)

    @pl.when(half_ref[0] != 0)
    def _():
        body(True)


def pack(first, count, half, sea, spec, after):
    vmem = pl.BlockSpec(memory_space=pltpu.VMEM)
    hold = pl.BlockSpec(memory_space=pl.ANY)
    return pl.pallas_call(
        functools.partial(pack_kernel, first, count),
        out_shape=[
            jax.ShapeDtypeStruct((LEAD_DIRS * count, 256), jnp.float32),
            jax.ShapeDtypeStruct(((HALF_DIRS - LEAD_DIRS - 1) * count, 256), jnp.float32),
            jax.ShapeDtypeStruct((HALF_DIRS, 8, 128), jnp.float32),
        ],
        in_specs=[pl.BlockSpec(memory_space=pltpu.SMEM), vmem, hold, hold],
        out_specs=[vmem] * 3,
        scratch_shapes=[
            pltpu.VMEM((2, HALF_DIRS, count, 8, 128), jnp.float32),
            pltpu.SemaphoreType.DMA((2, HALF_DIRS)),
        ],
        compiler_params=pltpu.CompilerParams(vmem_limit_bytes=VMEM_BYTES),
        cost_estimate=SMALL_COST,
    )(half, sea, spec, after)


ALL_DIRS = tuple(range(HALF_DIRS))
INNER_DIRS = ALL_DIRS[1:-1]
OUTER_DIRS = (0, HALF_DIRS - 1)


def is_sent(d):
    return d < SIDE_DIRS or d >= HALF_DIRS - SIDE_DIRS


def slab_index(dirs, count, base=0):
    return {d: base + count * n for n, d in enumerate(d for d in dirs if is_sent(d))}


def advect_kernel(
    group, passes, carries, waits, has_raw,
    half_ref, table_ref, sea_ref, slope_ref, spec_ref, lead_ref, trail_ref, lat_ref, steep_ref, *rest,
):
    sums = any(summed for *_, summed in passes)
    raw_ref = rest[0] if has_raw else None
    rest = rest[has_raw + waits :]
    held, turn, sem = rest[-3:]
    send_ref, keep_ref = rest[:2]
    if sums:
        steep_out_ref = rest[-4]
    copies, base = [], 0
    for i, (first, count, *_) in enumerate(passes):
        copy = pltpu.make_async_copy(spec_ref.at[:, pl.ds(first, count)], held.at[:, pl.ds(base, count)], sem.at[i])
        copy.start()
        copies.append(copy)
        base += count
    for d in range(HALF_DIRS):
        turn[d] = math.sin(heading(d)) * slope_ref[0] - math.cos(heading(d)) * slope_ref[1]
    if sums:
        steep_out_ref[...] = steep_ref[...]
    for copy in copies:
        copy.wait()
    rows_at = lax.broadcasted_iota(jnp.int32, (8, 256), 0)
    lanes_at = lax.broadcasted_iota(jnp.int32, (8, 256), 1)
    per_cell = TIME_STEP / CELL_SIZE * GRAVITY / 2.0
    bending = TIME_STEP * NDIR / (2.0 * math.pi) * (2.0 * math.pi * LOW_FREQ)
    group_count = group[1] - group[0]

    def body(flipped):
        lead_row, lead_shift = (7, 7) if flipped else (0, 1)
        trail_row, trail_shift = (0, 1) if flipped else (7, 7)
        lat_lane, lat_shift = (255, 255) if flipped else (0, 1)

        def one(first, dirs, slabs, summed, base, f, nothing):
            sea = sea_ref[...]
            inverse = table_ref[0, first + f]
            weight = table_ref[1, first + f]
            total = jnp.zeros((8, 256), jnp.float32)
            offset = first - group[0]

            def energy(d):
                if d < 0:
                    return raw_ref[1, first + f] * sea
                if d >= HALF_DIRS:
                    return raw_ref[0, first + f] * sea
                return held[d, base + f] * sea

            known = {}
            for d in dirs:
                known = {e: known[e] if e in known else energy(e) for e in (d - 1, d, d + 1)}
                prev, here, after = known[d - 1], known[d], known[d + 1]
                rate = turn[d]
                size = jnp.abs(rate) * bending
                moved = size * jnp.where(rate > 0.0, prev, after)
                along_x = per_cell * abs(math.cos(heading(d)))
                along_y = per_cell * abs(math.sin(heading(d)))
                fixed = 0.0
                if d != LEAD_DIRS:
                    if d < LEAD_DIRS:
                        row = lead_ref[pl.ds(d * group_count + offset + f, 1), :]
                        edge, shift = lead_row, lead_shift
                    else:
                        row = trail_ref[pl.ds((d - LEAD_DIRS - 1) * group_count + offset + f, 1), :]
                        edge, shift = trail_row, trail_shift
                    side = jnp.where(rows_at == edge, jnp.broadcast_to(row, (8, 256)), pltpu.roll(here, shift, 0))
                    moved = moved + along_x * side
                    fixed += along_x
                if d != 0:
                    halo = pltpu.roll(lat_ref[d], (lat_lane % 128) + 128 - (offset + f), 1)
                    halo = jnp.concatenate([halo, halo], axis=1)
                    side = jnp.where(lanes_at == lat_lane, halo, pltpu.roll(here, lat_shift, 1))
                    moved = moved + along_y * side
                    fixed += along_y
                result = (here - inverse * ((size + fixed) * here - moved)) * sea
                if slabs is not None and is_sent(d):
                    send_ref[slabs[d] + f] = result
                elif slabs is not None:
                    keep_ref[d - SIDE_DIRS, f] = result
                total = total + result
            if summed:
                steep_out_ref[...] += weight * total
            return nothing

        base = 0
        for first, count, dirs, slabs, summed in passes:
            lax.fori_loop(0, count, functools.partial(one, first, dirs, slabs, summed, base), 0)
            base += count

    @pl.when(half_ref[0] == 0)
    def _():
        body(False)

    @pl.when(half_ref[0] != 0)
    def _():
        body(True)

    if carries:
        send_ref[send_ref.shape[0] - 1] = steep_out_ref[...]


def advect_chunk(passes, group, carries, half, table, sea, slopes, spec, sides, steep, raw, after):
    vmem = pl.BlockSpec(memory_space=pltpu.VMEM)
    smem = pl.BlockSpec(memory_space=pltpu.SMEM)
    hold = pl.BlockSpec(memory_space=pl.ANY)
    slabs = sum(count * len(place) for _, count, _, place, _ in passes if place is not None)
    raw = () if raw is None else (raw,)
    out_shape = [
        jax.ShapeDtypeStruct((slabs + carries, 8, 256), jnp.float32),
        jax.ShapeDtypeStruct((HALF_DIRS - 2 * SIDE_DIRS, passes[0][1], 8, 256), jnp.float32),
    ]
    if any(summed for *_, summed in passes):
        out_shape.append(jax.ShapeDtypeStruct((8, 256), jnp.float32))
    return pl.pallas_call(
        functools.partial(advect_kernel, group, passes, carries, len(after), len(raw)),
        out_shape=out_shape,
        in_specs=[smem, smem, vmem, vmem, hold, vmem, vmem, vmem, vmem] + [vmem] * len(raw) + [hold] * len(after),
        out_specs=[vmem] * len(out_shape),
        scratch_shapes=[
            pltpu.VMEM((HALF_DIRS, sum(p[1] for p in passes), 8, 256), jnp.float32),
            pltpu.VMEM((HALF_DIRS, 8, 256), jnp.float32),
            pltpu.SemaphoreType.DMA((len(passes),)),
        ],
        compiler_params=pltpu.CompilerParams(vmem_limit_bytes=VMEM_BYTES),
        cost_estimate=SMALL_COST,
    )(half, table, sea, slopes, spec, *sides, steep, *raw, *after)


def source_kernel(
    first, count, inner, outer, chained,
    table_ref, wind_ref, steep_a_ref, steep_b_ref, cum_ref, own_ref, keep_ref, other_ref, *rest,
):
    edge_own_ref, edge_other_ref = rest[:2] if outer else (None, None)
    rest = rest[(2 if outer else 0) + chained :]
    out_ref, cum_out_ref, result, align, sem = rest
    weights = [math.cos(heading(m)) ** 2 / (9.0 * SATURATION_LEVEL) for m in range(SIDE_DIRS + 1)]
    steep = (steep_a_ref[...] + steep_b_ref[...]) * (1.0 / (NDIR * NFREQ))
    steep_sq = steep * steep
    for d in range(HALF_DIRS):
        align[d] = math.cos(heading(d)) * wind_ref[0] + math.sin(heading(d)) * wind_ref[1]
    cum_out_ref[...] = cum_ref[...]

    def one(f, nothing):
        omega = table_ref[2, first + f]
        gain = TIME_STEP * WIND_GROWTH * omega
        loss_sat = TIME_STEP * SATURATION_LOSS * omega
        loss_cum = TIME_STEP * CUMULATIVE_LOSS / NFREQ * omega
        loss_steep = TIME_STEP * STEEPNESS_LOSS * omega
        for half in range(2):
            lanes = slice(128 * half, 128 * half + 128)

            def slab(d, main, edge):
                return main[inner[d] + f, :, lanes] if d in inner else edge[outer[d] + f, :, lanes]

            first_dirs, last_dirs = ALL_DIRS[:SIDE_DIRS], ALL_DIRS[-SIDE_DIRS:]
            line = [slab(d, other_ref, edge_other_ref) for d in last_dirs]
            line += [slab(d, own_ref, edge_own_ref) for d in first_dirs]
            line += [keep_ref[i, f, :, lanes] for i in range(HALF_DIRS - 2 * SIDE_DIRS)]
            line += [slab(d, own_ref, edge_own_ref) for d in last_dirs]
            line += [slab(d, other_ref, edge_other_ref) for d in first_dirs]
            base = 1.0 + loss_steep * steep_sq[:, lanes]
            for d in range(HALF_DIRS):
                at = d + SIDE_DIRS
                level = weights[0] * line[at] - 1.0
                for m in range(1, SIDE_DIRS + 1):
                    level = level + weights[m] * (line[at - m] + line[at + m])
                excess = jnp.maximum(level, 0.0)
                square = excess * excess
                cum = cum_out_ref[d, :, lanes]
                cum_out_ref[d, :, lanes] = cum + square
                grown = 1.0 + gain * jnp.maximum(align[d, :, lanes] * omega - 1.0, 0.0)
                lost = base + loss_sat * square + loss_cum * cum
                result[d, f, :, lanes] = line[at] * grown / lost
        return nothing

    lax.fori_loop(0, count, one, 0)
    copy = pltpu.make_async_copy(result, out_ref.at[:, pl.ds(first, count)], sem)
    copy.start()
    copy.wait()


def source_chunk(first, count, inner, outer, table, wind, steep_own, steep_other, cum, own, keep, other, edges, out):
    vmem = pl.BlockSpec(memory_space=pltpu.VMEM)
    hold = pl.BlockSpec(memory_space=pl.ANY)
    chained = out is not None
    operands = (table, wind, steep_own, steep_other, cum, own, keep, other, *edges) + ((out,) if chained else ())
    return pl.pallas_call(
        functools.partial(source_kernel, first, count, inner, outer, chained),
        out_shape=(
            jax.ShapeDtypeStruct((HALF_DIRS, NFREQ, 8, 256), jnp.float32),
            jax.ShapeDtypeStruct((HALF_DIRS, 8, 256), jnp.float32),
        ),
        in_specs=[pl.BlockSpec(memory_space=pltpu.SMEM)] + [vmem] * (7 + len(edges)) + [hold] * chained,
        out_specs=(hold, vmem),
        scratch_shapes=[
            pltpu.VMEM((HALF_DIRS, count, 8, 256), jnp.float32),
            pltpu.VMEM((HALF_DIRS, 8, 256), jnp.float32),
            pltpu.SemaphoreType.DMA,
        ],
        input_output_aliases={len(operands) - 1: 0} if chained else {},
        compiler_params=pltpu.CompilerParams(vmem_limit_bytes=VMEM_BYTES),
        cost_estimate=SMALL_COST,
    )(*operands)


def ring_pairs(size, step, wrap):
    return [(i, (i + step) % size) for i in range(size) if wrap or 0 <= i + step < size]


def paired_shards(spectrum, sea_mask, owner_list, owner_count, slopes, friction, wind_angle):
    tiles_x, tiles_y = lax.axis_size("tx"), lax.axis_size("ty")
    half = lax.axis_index("comp")
    sign = 1.0 - 2.0 * half.astype(jnp.float32)
    half = half.astype(jnp.int32).reshape(1)
    spec = spectrum.reshape(HALF_DIRS, NFREQ, 8, 256)
    sea = sea_mask.astype(jnp.float32)
    turn = slopes * sign
    wind = (sign * WIND_FACTOR / GRAVITY) * friction * jnp.stack([jnp.cos(wind_angle), jnp.sin(wind_angle)])
    omega = freq_table()
    table = jnp.asarray(np.stack([1.0 / omega, (omega / omega[-1]) ** 2, omega]).astype(np.float32))

    def joined(axis_size, step, wrap):
        ahead = ring_pairs(axis_size, step, wrap)
        back = ring_pairs(axis_size, -step, wrap)
        return ahead + [(axis_size + i, axis_size + j) for i, j in back]

    swap = [(0, 1), (1, 0)]
    lead_pairs = joined(tiles_x, 1, True)
    trail_pairs = joined(tiles_x, -1, True)
    lat_pairs = joined(tiles_y, 1, False)

    spec = pltpu.with_memory_space_constraint(spec, pltpu.HBM)
    bounds = chunk_bounds()
    raw = raw_edges(spec)

    def halo(g, after):
        begin, end = HALO_GROUPS[g]
        lead, trail, lat = pack(begin, end - begin, half, sea, spec, after)
        sides = (
            lax.ppermute(lead, ("comp", "tx"), lead_pairs),
            lax.ppermute(trail, ("comp", "tx"), trail_pairs),
            lax.ppermute(lat, ("comp", "ty"), lat_pairs),
        )
        return sides, lead

    first_sides, _ = halo(0, raw)
    raw = lax.ppermute(raw, "comp", swap)
    early = sum(end <= HALO_GROUPS[0][1] for _, end in bounds)
    counts = [end - begin for begin, end in bounds]
    places = [slab_index(INNER_DIRS if i == 0 else ALL_DIRS, counts[i]) for i in range(len(bounds))]
    edge_place = slab_index(OUTER_DIRS, counts[0], base=2 * SIDE_DIRS * counts[1])

    def advect(passes, sides, carries, steep, raw, after):
        group = HALO_GROUPS[0] if sides is first_sides else HALO_GROUPS[1]
        return advect_chunk(passes, group, carries, half, table, sea, turn, spec, sides, steep, raw, after)

    sent, kept, received, sums = [], [], [], []

    def send(result):
        sent.append(result[0])
        kept.append(result[1])
        received.append(lax.ppermute(result[0], "comp", swap))

    def source(upto):
        for j in range(len(sums), upto):
            outer, edges = (edge_place, (sent[1], received[1])) if j == 0 else (None, ())
            state[:] = source_chunk(
                bounds[j][0], counts[j], places[j], outer, table, wind, steep, steep_other,
                state[1], sent[j], kept[j], received[j], edges, state[0],
            )
            sums.append(state[1])

    steep = jnp.zeros((8, 256), jnp.float32)
    for i in range(early):
        passes = [(bounds[i][0], counts[i], INNER_DIRS if i == 0 else ALL_DIRS, places[i], True)]
        after = ()
        if i == 1:
            passes.append((bounds[0][0], counts[0], OUTER_DIRS, edge_place, True))
        if i >= 2:
            after = (received[i - 2], packed)
        result = advect(passes, first_sides, False, steep, raw if i else None, after)
        send(result)
        steep = result[2]
        if i == 1:
            later_sides, packed = halo(1, steep)
    state = [None, jnp.zeros((HALF_DIRS, 8, 256), jnp.float32)]
    summing = SUM_CHUNKS
    ahead = bounds[early + summing][0]
    cuts = [ahead + (NFREQ - ahead) * n // summing for n in range(summing + 1)]
    for i in range(early, len(bounds)):
        after = (received[i - 2],)
        if i in SOURCES_DONE:
            source(SOURCES_DONE[i])
            after += (sums[-1],)
        n = i - early
        passes = [(bounds[i][0], counts[i], ALL_DIRS, places[i], n < summing)]
        if n < summing:
            passes.append((cuts[n], cuts[n + 1] - cuts[n], ALL_DIRS, None, True))
        result = advect(passes, later_sides, n == summing - 1, steep, raw, after)
        send(result)
        if n < summing:
            steep = result[2]
        if n == summing - 1:
            steep_other = received[i][-1]
    source(len(bounds))
    out = state[0]
    return out.reshape(spectrum.shape)


def fits_pairs(mesh, spectrum):
    return (
        mesh.shape["comp"] == 2
        and spectrum.shape[0] == NDIR * NFREQ
        and spectrum.shape[1] == 8 * mesh.shape["tx"]
        and spectrum.shape[2] == 256 * mesh.shape["ty"]
    )


def solution(mesh):
    in_specs = (
        P("comp", "tx", "ty"),
        P("tx", "ty"),
        P("tx", "ty", None, None),
        P("tx", "ty", None),
        P(None, "tx", "ty"),
        P("tx", "ty"),
        P("tx", "ty"),
    )
    out_specs = P("comp", "tx", "ty")

    def step(spectrum, *others):
        body = paired_shards if fits_pairs(mesh, spectrum) else shards
        mapped = jax.shard_map(body, mesh=mesh, in_specs=in_specs, out_specs=out_specs, check_vma=False)
        return mapped(spectrum, *others)

    return step
```

```python
import functools
import math

import jax
import jax.numpy as jnp
import numpy as np
from jax import lax
from jax.experimental import pallas as pl
from jax.experimental.pallas import tpu as pltpu
from jax.sharding import PartitionSpec as P

NDIR = 36
NFREQ = 50


TIME_STEP = 240.0
CELL_SIZE = 11100.0
GRAVITY = 9.81
LOW_FREQ = 0.0373
HIGH_FREQ = 1.0
WIND_GROWTH = 0.0001
WIND_FACTOR = 28.0
SATURATION_LOSS = 0.0005
CUMULATIVE_LOSS = 0.001
STEEPNESS_LOSS = 0.005
SATURATION_LEVEL = 0.6


def padded(value, sides, width, wrap):
    for axis, dim in sides:
        size, length = (lax.axis_size(axis), value.shape[dim])
        up = [(i, (i + 1) % size) for i in range(size if wrap else size - 1)]
        down = [(j, i) for i, j in up]
        last = lax.slice_in_dim(value, length - width, length, axis=dim)
        first = lax.slice_in_dim(value, 0, width, axis=dim)
        before = lax.ppermute(last, axis, up)
        after = lax.ppermute(first, axis, down)
        value = jnp.concatenate([before, value, after], axis=dim)
    return value


def freq_values(freq_ids):
    return (
        2.0
        * math.pi
        * LOW_FREQ
        * jnp.exp(freq_ids.astype(jnp.float32) * (math.log(HIGH_FREQ / LOW_FREQ) / (NFREQ - 1)))
    )


def wave_tables(first_comp, comp_count):
    comp_ids = first_comp + jnp.arange(comp_count, dtype=jnp.int32)
    headings = (comp_ids // NFREQ).astype(jnp.float32) * (2.0 * math.pi / NDIR)
    return (headings, freq_values(comp_ids % NFREQ))


def advect(
    energy,
    west_side,
    east_side,
    south_side,
    north_side,
    prev_dir,
    next_dir,
    headings,
    ang_freq,
    slopes,
):
    group_speed = GRAVITY / (2.0 * ang_freq)
    along_x = (TIME_STEP / CELL_SIZE * group_speed * jnp.cos(headings))[:, None, None]
    along_y = (TIME_STEP / CELL_SIZE * group_speed * jnp.sin(headings))[:, None, None]
    bending = TIME_STEP * NDIR / (2.0 * math.pi) * (2.0 * math.pi * LOW_FREQ) / ang_freq
    turning = bending[:, None, None] * (
        jnp.sin(headings)[:, None, None] * slopes[0][None]
        - jnp.cos(headings)[:, None, None] * slopes[1][None]
    )
    change = jnp.maximum(along_x, 0.0) * (energy - west_side) + jnp.minimum(along_x, 0.0) * (
        east_side - energy
    )
    change = (
        change
        + jnp.maximum(along_y, 0.0) * (energy - south_side)
        + jnp.minimum(along_y, 0.0) * (north_side - energy)
    )
    change = (
        change
        + jnp.maximum(turning, 0.0) * (energy - prev_dir)
        + jnp.minimum(turning, 0.0) * (next_dir - energy)
    )
    return energy - change


def source_terms(spectra, friction, wind_angle):
    dir_ids = jnp.arange(NDIR, dtype=jnp.int32)
    offset = (dir_ids[:, None] - dir_ids[None, :]) % NDIR
    nearest = jnp.minimum(offset, NDIR - offset)
    spread = jnp.where(
        4 * nearest < NDIR, jnp.cos(offset.astype(jnp.float32) * (2.0 * math.pi / NDIR)) ** 2, 0.0
    )
    spread = spread / jnp.sum(spread, axis=1, keepdims=True)
    sat_level = jnp.einsum("de,efp->dfp", spread, spectra, precision=lax.Precision.HIGHEST)
    excess = jnp.maximum(sat_level / SATURATION_LEVEL - 1.0, 0.0)
    excess_sq = excess * excess
    freq_ids = jnp.arange(NFREQ, dtype=jnp.int32)
    below_mask = (freq_ids[None, :] < freq_ids[:, None]).astype(jnp.float32)
    running = (
        jnp.einsum("fg,dgp->dfp", below_mask, excess_sq, precision=lax.Precision.HIGHEST) / NFREQ
    )
    ang_freq = freq_values(freq_ids)
    weights = (ang_freq / ang_freq[NFREQ - 1]) ** 2
    steepness = jnp.einsum("dfp,f->p", spectra, weights, precision=lax.Precision.HIGHEST) / (
        NDIR * NFREQ
    )
    headings = dir_ids.astype(jnp.float32) * (2.0 * math.pi / NDIR)
    alignment = (
        jnp.cos(headings)[:, None, None] * jnp.cos(wind_angle)[None, None, :]
        + jnp.sin(headings)[:, None, None] * jnp.sin(wind_angle)[None, None, :]
    )
    forcing = WIND_FACTOR / GRAVITY * friction[None, None, :] * ang_freq[None, :, None] * alignment
    growth = WIND_GROWTH * ang_freq[None, :, None] * jnp.maximum(forcing - 1.0, 0.0)
    losses = ang_freq[None, :, None] * (
        SATURATION_LOSS * excess_sq
        + CUMULATIVE_LOSS * running
        + STEEPNESS_LOSS * (steepness * steepness)[None, None, :]
    )
    return spectra * (1.0 + TIME_STEP * growth) / (1.0 + TIME_STEP * losses)


def shards(spectrum, sea_mask, owner_list, owner_count, slopes, friction, wind_angle):
    comp_size = lax.axis_size("comp")
    local_comps = spectrum.shape[0]
    cell_count = spectrum.shape[1] * spectrum.shape[2]
    sea_cells = sea_mask.astype(jnp.float32)
    masked = spectrum * sea_cells[None]
    headings, ang_freq = wave_tables(lax.axis_index("comp") * local_comps, local_comps)
    padded_lon = padded(masked, (("tx", 1),), 1, True)
    padded_lat = padded(masked, (("ty", 2),), 1, False)
    padded_dir = padded(masked, (("comp", 0),), NFREQ, True)
    advected = (
        advect(
            masked,
            padded_lon[:, :-2],
            padded_lon[:, 2:],
            padded_lat[:, :, :-2],
            padded_lat[:, :, 2:],
            padded_dir[:local_comps],
            padded_dir[2 * NFREQ :],
            headings,
            ang_freq,
            slopes,
        )
        * sea_cells[None]
    )
    moved_flat = advected.reshape(local_comps, cell_count)
    cell_names = owner_list[0, 0]
    slot_ids = jnp.arange(cell_names.shape[1], dtype=jnp.int32)
    in_use = slot_ids[None, :] < owner_count[0, 0][:, None]
    target = jnp.where(in_use, cell_names, cell_count).reshape(-1)
    owners = cell_names.shape[0]
    capacity = cell_names.shape[1]
    tiles_x = lax.axis_size("tx")
    cell_ids = jnp.arange(cell_count, dtype=jnp.int32)
    selector = (cell_ids[:, None] == target[None, :]).astype(jnp.float32)
    outgoing = jnp.dot(moved_flat, selector, precision=lax.Precision.HIGHEST).reshape(
        local_comps, owners, capacity
    )
    wind_rows = jnp.stack([friction.reshape(-1), wind_angle.reshape(-1)])
    point_data = jnp.dot(wind_rows, selector, precision=lax.Precision.HIGHEST).reshape(
        2, owners, capacity
    )
    spectra = lax.all_to_all(outgoing, ("comp", "tx"), split_axis=1, concat_axis=1, tiled=True)
    extras = lax.all_to_all(point_data, ("comp", "tx"), split_axis=1, concat_axis=1, tiled=True)
    batch_size = spectra.shape[2]
    full_spec = (
        spectra.reshape(local_comps, comp_size, tiles_x * batch_size)
        .transpose(1, 0, 2)
        .reshape(NDIR, NFREQ, tiles_x * batch_size)
    )
    extra_rows = extras.reshape(2, comp_size, tiles_x * batch_size)[:, 0]
    result = source_terms(full_spec, extra_rows[0], extra_rows[1])
    homeward = (
        result.reshape(comp_size, local_comps, tiles_x * batch_size)
        .transpose(1, 0, 2)
        .reshape(local_comps, comp_size * tiles_x, batch_size)
    )
    returned = lax.all_to_all(homeward, ("comp", "tx"), split_axis=1, concat_axis=1, tiled=True)
    gathered = lax.dot_general(
        returned.reshape(local_comps, owners * capacity),
        selector,
        (((1,), (1,)), ((), ())),
        precision=lax.Precision.HIGHEST,
    )
    listed = jnp.sum(selector, axis=1) > 0.5
    updated = jnp.where(listed[None], gathered, moved_flat)
    return updated.reshape(spectrum.shape)


def chunk_bounds():
    return [(5 * i, 5 * i + 5) for i in range(9)] + [(45, 48), (48, 50)]


HALO_GROUPS = ((0, 15), (15, 50))
SUM_CHUNKS = 3
SOURCES_DONE = {8: 2, 9: 5, 10: 7}
HALF_DIRS = NDIR // 2
SIDE_DIRS = 8
LEAD_DIRS = 9
VMEM_BYTES = 63 * 1024 * 1024
SMALL_COST = pl.CostEstimate(flops=1024, bytes_accessed=1024, transcendentals=0)


def freq_table():
    freqs = np.arange(NFREQ, dtype=np.float64)
    return 2.0 * math.pi * LOW_FREQ * np.exp(freqs * (math.log(HIGH_FREQ / LOW_FREQ) / (NFREQ - 1)))


def heading(index):
    return 2.0 * math.pi * index / NDIR


def raw_kernel(spec_ref, raw_ref, sems):
    copies = []
    for i, d in enumerate((0, HALF_DIRS - 1)):
        copy = pltpu.make_async_copy(spec_ref.at[d], raw_ref.at[i], sems.at[i])
        copy.start()
        copies.append(copy)
    for copy in copies:
        copy.wait()


def raw_edges(spec):
    return pl.pallas_call(
        raw_kernel,
        out_shape=jax.ShapeDtypeStruct((2, NFREQ, 8, 256), jnp.float32),
        in_specs=[pl.BlockSpec(memory_space=pl.ANY)],
        out_specs=pl.BlockSpec(memory_space=pltpu.VMEM),
        scratch_shapes=[pltpu.SemaphoreType.DMA((2,))],
        compiler_params=pltpu.CompilerParams(vmem_limit_bytes=VMEM_BYTES),
        cost_estimate=SMALL_COST,
    )(spec)


def pack_kernel(first, count, half_ref, sea_ref, spec_ref, after_ref, lead_ref, trail_ref, lat_ref, held, sems):
    def body(flipped):
        lead_row, trail_row = (0, 7) if flipped else (7, 0)
        part = 0 if flipped else 1
        copies = []
        for d in range(HALF_DIRS):
            for h in range(2):
                copy = pltpu.make_async_copy(
                    spec_ref.at[d, pl.ds(first, count), :, pl.ds(128 * h, 128)], held.at[h, d], sems.at[h, d]
                )
                copy.start()
                copies.append(copy)
        rows = held.reshape(2 * HALF_DIRS * count * 8, 128)
        for d in range(HALF_DIRS):
            for h in range(2):
                copies[2 * d + h].wait()
                lanes_here = slice(128 * h, 128 * h + 128)
                start = (h * HALF_DIRS + d) * count * 8
                if d < LEAD_DIRS:
                    column = rows[pl.ds(start + lead_row, count, stride=8), :]
                    lead_ref[d * count : (d + 1) * count, lanes_here] = column * sea_ref[lead_row : lead_row + 1, lanes_here]
                elif d > LEAD_DIRS:
                    t = d - LEAD_DIRS - 1
                    column = rows[pl.ds(start + trail_row, count, stride=8), :]
                    trail_ref[t * count : (t + 1) * count, lanes_here] = column * sea_ref[trail_row : trail_row + 1, lanes_here]
        lane = 0 if flipped else 127
        lanes = lax.broadcasted_iota(jnp.int32, (8, 128), 1)
        sea_line = jnp.broadcast_to(sea_ref[:, 128 * part + lane : 128 * part + lane + 1], (8, 128))

        def one(f, kept):
            here = lanes == f
            return tuple(
                jnp.where(here, jnp.broadcast_to(held[part, d, f][:, lane : lane + 1], (8, 128)), kept[d])
                for d in range(HALF_DIRS)
            )

        zeros = jnp.zeros((8, 128), jnp.float32)
        kept = lax.fori_loop(0, count, one, (zeros,) * HALF_DIRS, unroll=5)
        for d in range(HALF_DIRS):
            lat_ref[d] = kept[d] * sea_line

    @pl.when(half_ref[0] == 0)
    def _():
        body(False)

    @pl.when(half_ref[0] != 0)
    def _():
        body(True)


def pack(first, count, half, sea, spec, after):
    vmem = pl.BlockSpec(memory_space=pltpu.VMEM)
    hold = pl.BlockSpec(memory_space=pl.ANY)
    return pl.pallas_call(
        functools.partial(pack_kernel, first, count),
        out_shape=[
            jax.ShapeDtypeStruct((LEAD_DIRS * count, 256), jnp.float32),
            jax.ShapeDtypeStruct(((HALF_DIRS - LEAD_DIRS - 1) * count, 256), jnp.float32),
            jax.ShapeDtypeStruct((HALF_DIRS, 8, 128), jnp.float32),
        ],
        in_specs=[pl.BlockSpec(memory_space=pltpu.SMEM), vmem, hold, hold],
        out_specs=[vmem] * 3,
        scratch_shapes=[
            pltpu.VMEM((2, HALF_DIRS, count, 8, 128), jnp.float32),
            pltpu.SemaphoreType.DMA((2, HALF_DIRS)),
        ],
        compiler_params=pltpu.CompilerParams(vmem_limit_bytes=VMEM_BYTES),
        cost_estimate=SMALL_COST,
    )(half, sea, spec, after)


ALL_DIRS = tuple(range(HALF_DIRS))
INNER_DIRS = ALL_DIRS[1:-1]
OUTER_DIRS = (0, HALF_DIRS - 1)


def is_sent(d):
    return d < SIDE_DIRS or d >= HALF_DIRS - SIDE_DIRS


def slab_index(dirs, count, base=0):
    return {d: base + count * n for n, d in enumerate(d for d in dirs if is_sent(d))}


def advect_kernel(
    group, passes, carries, waits, has_raw,
    half_ref, table_ref, sea_ref, slope_ref, spec_ref, lead_ref, trail_ref, lat_ref, steep_ref, *rest,
):
    sums = any(summed for *_, summed in passes)
    raw_ref = rest[0] if has_raw else None
    rest = rest[has_raw + waits :]
    held, turn, sem = rest[-3:]
    send_ref, keep_ref = rest[:2]
    if sums:
        steep_out_ref = rest[-4]
    copies, base = [], 0
    for i, (first, count, *_) in enumerate(passes):
        copy = pltpu.make_async_copy(spec_ref.at[:, pl.ds(first, count)], held.at[:, pl.ds(base, count)], sem.at[i])
        copy.start()
        copies.append(copy)
        base += count
    for d in range(HALF_DIRS):
        turn[d] = math.sin(heading(d)) * slope_ref[0] - math.cos(heading(d)) * slope_ref[1]
    if sums:
        steep_out_ref[...] = steep_ref[...]
    for copy in copies:
        copy.wait()
    rows_at = lax.broadcasted_iota(jnp.int32, (8, 256), 0)
    lanes_at = lax.broadcasted_iota(jnp.int32, (8, 256), 1)
    per_cell = TIME_STEP / CELL_SIZE * GRAVITY / 2.0
    bending = TIME_STEP * NDIR / (2.0 * math.pi) * (2.0 * math.pi * LOW_FREQ)
    group_count = group[1] - group[0]

    def body(flipped):
        lead_row, lead_shift = (7, 7) if flipped else (0, 1)
        trail_row, trail_shift = (0, 1) if flipped else (7, 7)
        lat_lane, lat_shift = (255, 255) if flipped else (0, 1)

        def one(first, dirs, slabs, summed, base, f, nothing):
            sea = sea_ref[...]
            inverse = table_ref[0, first + f]
            weight = table_ref[1, first + f]
            total = jnp.zeros((8, 256), jnp.float32)
            offset = first - group[0]

            def energy(d):
                if d < 0:
                    return raw_ref[1, first + f] * sea
                if d >= HALF_DIRS:
                    return raw_ref[0, first + f] * sea
                return held[d, base + f] * sea

            known = {}
            for d in dirs:
                known = {e: known[e] if e in known else energy(e) for e in (d - 1, d, d + 1)}
                prev, here, after = known[d - 1], known[d], known[d + 1]
                rate = turn[d]
                size = jnp.abs(rate) * bending
                moved = size * jnp.where(rate > 0.0, prev, after)
                along_x = per_cell * abs(math.cos(heading(d)))
                along_y = per_cell * abs(math.sin(heading(d)))
                fixed = 0.0
                if d != LEAD_DIRS:
                    if d < LEAD_DIRS:
                        row = lead_ref[pl.ds(d * group_count + offset + f, 1), :]
                        edge, shift = lead_row, lead_shift
                    else:
                        row = trail_ref[pl.ds((d - LEAD_DIRS - 1) * group_count + offset + f, 1), :]
                        edge, shift = trail_row, trail_shift
                    side = jnp.where(rows_at == edge, jnp.broadcast_to(row, (8, 256)), pltpu.roll(here, shift, 0))
                    moved = moved + along_x * side
                    fixed += along_x
                if d != 0:
                    halo = pltpu.roll(lat_ref[d], (lat_lane % 128) + 128 - (offset + f), 1)
                    halo = jnp.concatenate([halo, halo], axis=1)
                    side = jnp.where(lanes_at == lat_lane, halo, pltpu.roll(here, lat_shift, 1))
                    moved = moved + along_y * side
                    fixed += along_y
                result = (here - inverse * ((size + fixed) * here - moved)) * sea
                if slabs is not None and is_sent(d):
                    send_ref[slabs[d] + f] = result
                elif slabs is not None:
                    keep_ref[d - SIDE_DIRS, f] = result
                total = total + result
            if summed:
                steep_out_ref[...] += weight * total
            return nothing

        base = 0
        for first, count, dirs, slabs, summed in passes:
            lax.fori_loop(0, count, functools.partial(one, first, dirs, slabs, summed, base), 0)
            base += count

    @pl.when(half_ref[0] == 0)
    def _():
        body(False)

    @pl.when(half_ref[0] != 0)
    def _():
        body(True)

    if carries:
        send_ref[send_ref.shape[0] - 1] = steep_out_ref[...]


def advect_chunk(passes, group, carries, half, table, sea, slopes, spec, sides, steep, raw, after):
    vmem = pl.BlockSpec(memory_space=pltpu.VMEM)
    smem = pl.BlockSpec(memory_space=pltpu.SMEM)
    hold = pl.BlockSpec(memory_space=pl.ANY)
    slabs = sum(count * len(place) for _, count, _, place, _ in passes if place is not None)
    raw = () if raw is None else (raw,)
    out_shape = [
        jax.ShapeDtypeStruct((slabs + carries, 8, 256), jnp.float32),
        jax.ShapeDtypeStruct((HALF_DIRS - 2 * SIDE_DIRS, passes[0][1], 8, 256), jnp.float32),
    ]
    if any(summed for *_, summed in passes):
        out_shape.append(jax.ShapeDtypeStruct((8, 256), jnp.float32))
    return pl.pallas_call(
        functools.partial(advect_kernel, group, passes, carries, len(after), len(raw)),
        out_shape=out_shape,
        in_specs=[smem, smem, vmem, vmem, hold, vmem, vmem, vmem, vmem] + [vmem] * len(raw) + [hold] * len(after),
        out_specs=[vmem] * len(out_shape),
        scratch_shapes=[
            pltpu.VMEM((HALF_DIRS, sum(p[1] for p in passes), 8, 256), jnp.float32),
            pltpu.VMEM((HALF_DIRS, 8, 256), jnp.float32),
            pltpu.SemaphoreType.DMA((len(passes),)),
        ],
        compiler_params=pltpu.CompilerParams(vmem_limit_bytes=VMEM_BYTES),
        cost_estimate=SMALL_COST,
    )(half, table, sea, slopes, spec, *sides, steep, *raw, *after)


def source_kernel(
    first, count, inner, outer, chained,
    table_ref, wind_ref, steep_a_ref, steep_b_ref, cum_ref, own_ref, keep_ref, other_ref, *rest,
):
    edge_own_ref, edge_other_ref = rest[:2] if outer else (None, None)
    rest = rest[(2 if outer else 0) + chained :]
    out_ref, cum_out_ref, result, align, sem = rest
    weights = [math.cos(heading(m)) ** 2 / (9.0 * SATURATION_LEVEL) for m in range(SIDE_DIRS + 1)]
    steep = (steep_a_ref[...] + steep_b_ref[...]) * (1.0 / (NDIR * NFREQ))
    steep_sq = steep * steep
    for d in range(HALF_DIRS):
        align[d] = math.cos(heading(d)) * wind_ref[0] + math.sin(heading(d)) * wind_ref[1]
    cum_out_ref[...] = cum_ref[...]

    def one(f, nothing):
        omega = table_ref[2, first + f]
        gain = TIME_STEP * WIND_GROWTH * omega
        loss_sat = TIME_STEP * SATURATION_LOSS * omega
        loss_cum = TIME_STEP * CUMULATIVE_LOSS / NFREQ * omega
        loss_steep = TIME_STEP * STEEPNESS_LOSS * omega
        for half in range(2):
            lanes = slice(128 * half, 128 * half + 128)

            def slab(d, main, edge):
                return main[inner[d] + f, :, lanes] if d in inner else edge[outer[d] + f, :, lanes]

            first_dirs, last_dirs = ALL_DIRS[:SIDE_DIRS], ALL_DIRS[-SIDE_DIRS:]
            line = [slab(d, other_ref, edge_other_ref) for d in last_dirs]
            line += [slab(d, own_ref, edge_own_ref) for d in first_dirs]
            line += [keep_ref[i, f, :, lanes] for i in range(HALF_DIRS - 2 * SIDE_DIRS)]
            line += [slab(d, own_ref, edge_own_ref) for d in last_dirs]
            line += [slab(d, other_ref, edge_other_ref) for d in first_dirs]
            base = 1.0 + loss_steep * steep_sq[:, lanes]
            for d in range(HALF_DIRS):
                at = d + SIDE_DIRS
                level = weights[0] * line[at] - 1.0
                for m in range(1, SIDE_DIRS + 1):
                    level = level + weights[m] * (line[at - m] + line[at + m])
                excess = jnp.maximum(level, 0.0)
                square = excess * excess
                cum = cum_out_ref[d, :, lanes]
                cum_out_ref[d, :, lanes] = cum + square
                grown = 1.0 + gain * jnp.maximum(align[d, :, lanes] * omega - 1.0, 0.0)
                lost = base + loss_sat * square + loss_cum * cum
                result[d, f, :, lanes] = line[at] * grown / lost
        return nothing

    lax.fori_loop(0, count, one, 0)
    copy = pltpu.make_async_copy(result, out_ref.at[:, pl.ds(first, count)], sem)
    copy.start()
    copy.wait()


def source_chunk(first, count, inner, outer, table, wind, steep_own, steep_other, cum, own, keep, other, edges, out):
    vmem = pl.BlockSpec(memory_space=pltpu.VMEM)
    hold = pl.BlockSpec(memory_space=pl.ANY)
    chained = out is not None
    operands = (table, wind, steep_own, steep_other, cum, own, keep, other, *edges) + ((out,) if chained else ())
    return pl.pallas_call(
        functools.partial(source_kernel, first, count, inner, outer, chained),
        out_shape=(
            jax.ShapeDtypeStruct((HALF_DIRS, NFREQ, 8, 256), jnp.float32),
            jax.ShapeDtypeStruct((HALF_DIRS, 8, 256), jnp.float32),
        ),
        in_specs=[pl.BlockSpec(memory_space=pltpu.SMEM)] + [vmem] * (7 + len(edges)) + [hold] * chained,
        out_specs=(hold, vmem),
        scratch_shapes=[
            pltpu.VMEM((HALF_DIRS, count, 8, 256), jnp.float32),
            pltpu.VMEM((HALF_DIRS, 8, 256), jnp.float32),
            pltpu.SemaphoreType.DMA,
        ],
        input_output_aliases={len(operands) - 1: 0} if chained else {},
        compiler_params=pltpu.CompilerParams(vmem_limit_bytes=VMEM_BYTES),
        cost_estimate=SMALL_COST,
    )(*operands)


def ring_pairs(size, step, wrap):
    return [(i, (i + step) % size) for i in range(size) if wrap or 0 <= i + step < size]


def paired_shards(spectrum, sea_mask, owner_list, owner_count, slopes, friction, wind_angle):
    tiles_x, tiles_y = lax.axis_size("tx"), lax.axis_size("ty")
    half = lax.axis_index("comp")
    sign = 1.0 - 2.0 * half.astype(jnp.float32)
    half = half.astype(jnp.int32).reshape(1)
    spec = spectrum.reshape(HALF_DIRS, NFREQ, 8, 256)
    sea = sea_mask.astype(jnp.float32)
    turn = slopes * sign
    wind = (sign * WIND_FACTOR / GRAVITY) * friction * jnp.stack([jnp.cos(wind_angle), jnp.sin(wind_angle)])
    omega = freq_table()
    table = jnp.asarray(np.stack([1.0 / omega, (omega / omega[-1]) ** 2, omega]).astype(np.float32))

    def joined(axis_size, step, wrap):
        ahead = ring_pairs(axis_size, step, wrap)
        back = ring_pairs(axis_size, -step, wrap)
        return ahead + [(axis_size + i, axis_size + j) for i, j in back]

    swap = [(0, 1), (1, 0)]
    lead_pairs = joined(tiles_x, 1, True)
    trail_pairs = joined(tiles_x, -1, True)
    lat_pairs = joined(tiles_y, 1, False)

    spec = pltpu.with_memory_space_constraint(spec, pltpu.HBM)
    bounds = chunk_bounds()
    raw = raw_edges(spec)

    def halo(g, after):
        begin, end = HALO_GROUPS[g]
        lead, trail, lat = pack(begin, end - begin, half, sea, spec, after)
        sides = (
            lax.ppermute(lead, ("comp", "tx"), lead_pairs),
            lax.ppermute(trail, ("comp", "tx"), trail_pairs),
            lax.ppermute(lat, ("comp", "ty"), lat_pairs),
        )
        return sides, lead

    first_sides, _ = halo(0, raw)
    raw = lax.ppermute(raw, "comp", swap)
    early = sum(end <= HALO_GROUPS[0][1] for _, end in bounds)
    counts = [end - begin for begin, end in bounds]
    places = [slab_index(INNER_DIRS if i == 0 else ALL_DIRS, counts[i]) for i in range(len(bounds))]
    edge_place = slab_index(OUTER_DIRS, counts[0], base=2 * SIDE_DIRS * counts[1])

    def advect(passes, sides, carries, steep, raw, after):
        group = HALO_GROUPS[0] if sides is first_sides else HALO_GROUPS[1]
        return advect_chunk(passes, group, carries, half, table, sea, turn, spec, sides, steep, raw, after)

    sent, kept, received, sums = [], [], [], []

    def send(result):
        sent.append(result[0])
        kept.append(result[1])
        received.append(lax.ppermute(result[0], "comp", swap))

    def source(upto):
        for j in range(len(sums), upto):
            outer, edges = (edge_place, (sent[1], received[1])) if j == 0 else (None, ())
            state[:] = source_chunk(
                bounds[j][0], counts[j], places[j], outer, table, wind, steep, steep_other,
                state[1], sent[j], kept[j], received[j], edges, state[0],
            )
            sums.append(state[1])

    steep = jnp.zeros((8, 256), jnp.float32)
    for i in range(early):
        passes = [(bounds[i][0], counts[i], INNER_DIRS if i == 0 else ALL_DIRS, places[i], True)]
        after = ()
        if i == 1:
            passes.append((bounds[0][0], counts[0], OUTER_DIRS, edge_place, True))
        if i >= 2:
            after = (received[i - 2], packed)
        result = advect(passes, first_sides, False, steep, raw if i else None, after)
        send(result)
        steep = result[2]
        if i == 1:
            later_sides, packed = halo(1, steep)
    state = [None, jnp.zeros((HALF_DIRS, 8, 256), jnp.float32)]
    summing = SUM_CHUNKS
    ahead = bounds[early + summing][0]
    cuts = [ahead + (NFREQ - ahead) * n // summing for n in range(summing + 1)]
    for i in range(early, len(bounds)):
        after = (received[i - 2],)
        if i in SOURCES_DONE:
            source(SOURCES_DONE[i])
            after += (sums[-1],)
        n = i - early
        passes = [(bounds[i][0], counts[i], ALL_DIRS, places[i], n < summing)]
        if n < summing:
            passes.append((cuts[n], cuts[n + 1] - cuts[n], ALL_DIRS, None, True))
        result = advect(passes, later_sides, n == summing - 1, steep, raw, after)
        send(result)
        if n < summing:
            steep = result[2]
        if n == summing - 1:
            steep_other = received[i][-1]
    source(len(bounds))
    out = state[0]
    return out.reshape(spectrum.shape)


def fits_pairs(mesh, spectrum):
    return (
        mesh.shape["comp"] == 2
        and spectrum.shape[0] == NDIR * NFREQ
        and spectrum.shape[1] == 8 * mesh.shape["tx"]
        and spectrum.shape[2] == 256 * mesh.shape["ty"]
    )


def solution(mesh):
    in_specs = (
        P("comp", "tx", "ty"),
        P("tx", "ty"),
        P("tx", "ty", None, None),
        P("tx", "ty", None),
        P(None, "tx", "ty"),
        P("tx", "ty"),
        P("tx", "ty"),
    )
    out_specs = P("comp", "tx", "ty")

    def step(spectrum, *others):
        body = paired_shards if fits_pairs(mesh, spectrum) else shards
        mapped = jax.shard_map(body, mesh=mesh, in_specs=in_specs, out_specs=out_specs, check_vma=False)
        return mapped(spectrum, *others)

    return step
```

```python
import functools
import math

import jax
import jax.numpy as jnp
from jax import lax
from jax.experimental import pallas as pl
from jax.experimental.pallas import tpu as pltpu
from jax.sharding import PartitionSpec as P

NDIR = 36
NFREQ = 50


TIME_STEP = 240.0
CELL_SIZE = 11100.0
GRAVITY = 9.81
LOW_FREQ = 0.0373
HIGH_FREQ = 1.0
WIND_GROWTH = 0.0001
WIND_FACTOR = 28.0
SATURATION_LOSS = 0.0005
CUMULATIVE_LOSS = 0.001
STEEPNESS_LOSS = 0.005
SATURATION_LEVEL = 0.6


def padded(value, sides, width, wrap):
    for axis, dim in sides:
        size, length = (lax.axis_size(axis), value.shape[dim])
        up = [(i, (i + 1) % size) for i in range(size if wrap else size - 1)]
        down = [(j, i) for i, j in up]
        last = lax.slice_in_dim(value, length - width, length, axis=dim)
        first = lax.slice_in_dim(value, 0, width, axis=dim)
        before = lax.ppermute(last, axis, up)
        after = lax.ppermute(first, axis, down)
        value = jnp.concatenate([before, value, after], axis=dim)
    return value


def freq_values(freq_ids):
    return (
        2.0
        * math.pi
        * LOW_FREQ
        * jnp.exp(freq_ids.astype(jnp.float32) * (math.log(HIGH_FREQ / LOW_FREQ) / (NFREQ - 1)))
    )


def wave_tables(first_comp, comp_count):
    comp_ids = first_comp + jnp.arange(comp_count, dtype=jnp.int32)
    headings = (comp_ids // NFREQ).astype(jnp.float32) * (2.0 * math.pi / NDIR)
    return (headings, freq_values(comp_ids % NFREQ))


def advect(
    energy,
    west_side,
    east_side,
    south_side,
    north_side,
    prev_dir,
    next_dir,
    headings,
    ang_freq,
    slopes,
):
    group_speed = GRAVITY / (2.0 * ang_freq)
    along_x = (TIME_STEP / CELL_SIZE * group_speed * jnp.cos(headings))[:, None, None]
    along_y = (TIME_STEP / CELL_SIZE * group_speed * jnp.sin(headings))[:, None, None]
    bending = TIME_STEP * NDIR / (2.0 * math.pi) * (2.0 * math.pi * LOW_FREQ) / ang_freq
    turning = bending[:, None, None] * (
        jnp.sin(headings)[:, None, None] * slopes[0][None]
        - jnp.cos(headings)[:, None, None] * slopes[1][None]
    )
    change = jnp.maximum(along_x, 0.0) * (energy - west_side) + jnp.minimum(along_x, 0.0) * (
        east_side - energy
    )
    change = (
        change
        + jnp.maximum(along_y, 0.0) * (energy - south_side)
        + jnp.minimum(along_y, 0.0) * (north_side - energy)
    )
    change = (
        change
        + jnp.maximum(turning, 0.0) * (energy - prev_dir)
        + jnp.minimum(turning, 0.0) * (next_dir - energy)
    )
    return energy - change


def source_terms(spectra, friction, wind_angle):
    dir_ids = jnp.arange(NDIR, dtype=jnp.int32)
    offset = (dir_ids[:, None] - dir_ids[None, :]) % NDIR
    nearest = jnp.minimum(offset, NDIR - offset)
    spread = jnp.where(
        4 * nearest < NDIR, jnp.cos(offset.astype(jnp.float32) * (2.0 * math.pi / NDIR)) ** 2, 0.0
    )
    spread = spread / jnp.sum(spread, axis=1, keepdims=True)
    sat_level = jnp.einsum("de,efp->dfp", spread, spectra, precision=lax.Precision.HIGHEST)
    excess = jnp.maximum(sat_level / SATURATION_LEVEL - 1.0, 0.0)
    excess_sq = excess * excess
    freq_ids = jnp.arange(NFREQ, dtype=jnp.int32)
    below_mask = (freq_ids[None, :] < freq_ids[:, None]).astype(jnp.float32)
    running = (
        jnp.einsum("fg,dgp->dfp", below_mask, excess_sq, precision=lax.Precision.HIGHEST) / NFREQ
    )
    ang_freq = freq_values(freq_ids)
    weights = (ang_freq / ang_freq[NFREQ - 1]) ** 2
    steepness = jnp.einsum("dfp,f->p", spectra, weights, precision=lax.Precision.HIGHEST) / (
        NDIR * NFREQ
    )
    headings = dir_ids.astype(jnp.float32) * (2.0 * math.pi / NDIR)
    alignment = (
        jnp.cos(headings)[:, None, None] * jnp.cos(wind_angle)[None, None, :]
        + jnp.sin(headings)[:, None, None] * jnp.sin(wind_angle)[None, None, :]
    )
    forcing = WIND_FACTOR / GRAVITY * friction[None, None, :] * ang_freq[None, :, None] * alignment
    growth = WIND_GROWTH * ang_freq[None, :, None] * jnp.maximum(forcing - 1.0, 0.0)
    losses = ang_freq[None, :, None] * (
        SATURATION_LOSS * excess_sq
        + CUMULATIVE_LOSS * running
        + STEEPNESS_LOSS * (steepness * steepness)[None, None, :]
    )
    return spectra * (1.0 + TIME_STEP * growth) / (1.0 + TIME_STEP * losses)


def shards(spectrum, sea_mask, owner_list, owner_count, slopes, friction, wind_angle):
    comp_size = lax.axis_size("comp")
    local_comps = spectrum.shape[0]
    cell_count = spectrum.shape[1] * spectrum.shape[2]
    sea_cells = sea_mask.astype(jnp.float32)
    masked = spectrum * sea_cells[None]
    headings, ang_freq = wave_tables(lax.axis_index("comp") * local_comps, local_comps)
    padded_lon = padded(masked, (("tx", 1),), 1, True)
    padded_lat = padded(masked, (("ty", 2),), 1, False)
    padded_dir = padded(masked, (("comp", 0),), NFREQ, True)
    advected = (
        advect(
            masked,
            padded_lon[:, :-2],
            padded_lon[:, 2:],
            padded_lat[:, :, :-2],
            padded_lat[:, :, 2:],
            padded_dir[:local_comps],
            padded_dir[2 * NFREQ :],
            headings,
            ang_freq,
            slopes,
        )
        * sea_cells[None]
    )
    moved_flat = advected.reshape(local_comps, cell_count)
    cell_names = owner_list[0, 0]
    slot_ids = jnp.arange(cell_names.shape[1], dtype=jnp.int32)
    in_use = slot_ids[None, :] < owner_count[0, 0][:, None]
    target = jnp.where(in_use, cell_names, cell_count).reshape(-1)
    owners = cell_names.shape[0]
    capacity = cell_names.shape[1]
    tiles_x = lax.axis_size("tx")
    cell_ids = jnp.arange(cell_count, dtype=jnp.int32)
    selector = (cell_ids[:, None] == target[None, :]).astype(jnp.float32)
    outgoing = jnp.dot(moved_flat, selector, precision=lax.Precision.HIGHEST).reshape(
        local_comps, owners, capacity
    )
    wind_rows = jnp.stack([friction.reshape(-1), wind_angle.reshape(-1)])
    point_data = jnp.dot(wind_rows, selector, precision=lax.Precision.HIGHEST).reshape(
        2, owners, capacity
    )
    spectra = lax.all_to_all(outgoing, ("comp", "tx"), split_axis=1, concat_axis=1, tiled=True)
    extras = lax.all_to_all(point_data, ("comp", "tx"), split_axis=1, concat_axis=1, tiled=True)
    batch_size = spectra.shape[2]
    full_spec = (
        spectra.reshape(local_comps, comp_size, tiles_x * batch_size)
        .transpose(1, 0, 2)
        .reshape(NDIR, NFREQ, tiles_x * batch_size)
    )
    extra_rows = extras.reshape(2, comp_size, tiles_x * batch_size)[:, 0]
    result = source_terms(full_spec, extra_rows[0], extra_rows[1])
    homeward = (
        result.reshape(comp_size, local_comps, tiles_x * batch_size)
        .transpose(1, 0, 2)
        .reshape(local_comps, comp_size * tiles_x, batch_size)
    )
    returned = lax.all_to_all(homeward, ("comp", "tx"), split_axis=1, concat_axis=1, tiled=True)
    gathered = lax.dot_general(
        returned.reshape(local_comps, owners * capacity),
        selector,
        (((1,), (1,)), ((), ())),
        precision=lax.Precision.HIGHEST,
    )
    listed = jnp.sum(selector, axis=1) > 0.5
    updated = jnp.where(listed[None], gathered, moved_flat)
    return updated.reshape(spectrum.shape)


def chunk_bounds():
    return [(5 * i, 5 * i + 5) for i in range(9)] + [(45, 48), (48, 50)]


HALO_GROUPS = ((0, 15), (15, 50))
SUM_CHUNKS = 3
SOURCES_DONE = {8: 2, 9: 5, 10: 7}
HALF_DIRS = NDIR // 2
SIDE_DIRS = 8
LEAD_DIRS = 9
VMEM_BYTES = 24 * 1024 * 1024
SMALL_COST = pl.CostEstimate(flops=1024, bytes_accessed=1024, transcendentals=0)


FREQ_STEP = (HIGH_FREQ / LOW_FREQ) ** (1.0 / (NFREQ - 1))


def frequency(index):
    return 2.0 * math.pi * LOW_FREQ * FREQ_STEP**index


def heading(index):
    return 2.0 * math.pi * index / NDIR


def raw_kernel(spec_ref, raw_ref, sems):
    copies = []
    for i, d in enumerate((0, HALF_DIRS - 1)):
        copy = pltpu.make_async_copy(spec_ref.at[d], raw_ref.at[i], sems.at[i])
        copy.start()
        copies.append(copy)
    for copy in copies:
        copy.wait()


def raw_edges(spec):
    return pl.pallas_call(
        raw_kernel,
        out_shape=jax.ShapeDtypeStruct((2, NFREQ, 8, 256), jnp.float32),
        in_specs=[pl.BlockSpec(memory_space=pl.ANY)],
        out_specs=pl.BlockSpec(memory_space=pltpu.VMEM),
        scratch_shapes=[pltpu.SemaphoreType.DMA((2,))],
        compiler_params=pltpu.CompilerParams(vmem_limit_bytes=VMEM_BYTES),
        cost_estimate=SMALL_COST,
    )(spec)


def pack_kernel(first, count, sea_ref, spec_ref, after_ref, lead_ref, trail_ref, lat_ref, held, sems):
    def body(flipped):
        lead_row, trail_row = (0, 7) if flipped else (7, 0)
        part = 0 if flipped else 1
        copies = []
        for d in range(HALF_DIRS):
            for h in range(2):
                copy = pltpu.make_async_copy(
                    spec_ref.at[d, pl.ds(first, count), :, pl.ds(128 * h, 128)], held.at[h, d], sems.at[h, d]
                )
                copy.start()
                copies.append(copy)
        rows = held.reshape(2 * HALF_DIRS * count * 8, 128)
        for d in range(HALF_DIRS):
            for h in range(2):
                copies[2 * d + h].wait()
                lanes_here = slice(128 * h, 128 * h + 128)
                start = (h * HALF_DIRS + d) * count * 8
                if d < LEAD_DIRS:
                    column = rows[pl.ds(start + lead_row, count, stride=8), :]
                    lead_ref[d * count : (d + 1) * count, lanes_here] = column * sea_ref[lead_row : lead_row + 1, lanes_here]
                elif d > LEAD_DIRS:
                    t = d - LEAD_DIRS - 1
                    column = rows[pl.ds(start + trail_row, count, stride=8), :]
                    trail_ref[t * count : (t + 1) * count, lanes_here] = column * sea_ref[trail_row : trail_row + 1, lanes_here]
        lane = 0 if flipped else 127
        lanes = lax.broadcasted_iota(jnp.int32, (8, 128), 1)
        sea_line = jnp.broadcast_to(sea_ref[:, 128 * part + lane : 128 * part + lane + 1], (8, 128))

        def one(f, kept):
            here = lanes == f
            return tuple(
                jnp.where(here, jnp.broadcast_to(held[part, d, f][:, lane : lane + 1], (8, 128)), kept[d])
                for d in range(HALF_DIRS)
            )

        zeros = jnp.zeros((8, 128), jnp.float32)
        kept = lax.fori_loop(0, count, one, (zeros,) * HALF_DIRS, unroll=5)
        for d in range(HALF_DIRS):
            lat_ref[d] = kept[d] * sea_line

    half = lax.axis_index("comp")

    @pl.when(half == 0)
    def _():
        body(False)

    @pl.when(half != 0)
    def _():
        body(True)


def pack(first, count, sea, spec, after):
    vmem = pl.BlockSpec(memory_space=pltpu.VMEM)
    hold = pl.BlockSpec(memory_space=pl.ANY)
    return pl.pallas_call(
        functools.partial(pack_kernel, first, count),
        out_shape=[
            jax.ShapeDtypeStruct((LEAD_DIRS * count, 256), jnp.float32),
            jax.ShapeDtypeStruct(((HALF_DIRS - LEAD_DIRS - 1) * count, 256), jnp.float32),
            jax.ShapeDtypeStruct((HALF_DIRS, 8, 128), jnp.float32),
        ],
        in_specs=[vmem, hold, hold],
        out_specs=[vmem] * 3,
        scratch_shapes=[
            pltpu.VMEM((2, HALF_DIRS, count, 8, 128), jnp.float32),
            pltpu.SemaphoreType.DMA((2, HALF_DIRS)),
        ],
        compiler_params=pltpu.CompilerParams(vmem_limit_bytes=VMEM_BYTES),
        cost_estimate=SMALL_COST,
    )(sea, spec, after)


ALL_DIRS = tuple(range(HALF_DIRS))
INNER_DIRS = ALL_DIRS[1:-1]
OUTER_DIRS = (0, HALF_DIRS - 1)


def is_sent(d):
    return d < SIDE_DIRS or d >= HALF_DIRS - SIDE_DIRS


def slab_index(dirs, count, base=0):
    return {d: base + count * n for n, d in enumerate(d for d in dirs if is_sent(d))}


def advect_kernel(
    group, passes, carries, waits, has_raw,
    sea_ref, slope_ref, spec_ref, lead_ref, trail_ref, lat_ref, steep_ref, *rest,
):
    sums = any(summed for *_, summed in passes)
    raw_ref = rest[0] if has_raw else None
    rest = rest[has_raw + waits :]
    held, turn, sem = rest[-3:]
    send_ref, keep_ref = rest[:2]
    if sums:
        steep_out_ref = rest[-4]
    copies, base = [], 0
    for i, (first, count, *_) in enumerate(passes):
        copy = pltpu.make_async_copy(spec_ref.at[:, pl.ds(first, count)], held.at[:, pl.ds(base, count)], sem.at[i])
        copy.start()
        copies.append(copy)
        base += count
    for d in range(HALF_DIRS):
        turn[d] = math.sin(heading(d)) * slope_ref[0] - math.cos(heading(d)) * slope_ref[1]
    if sums:
        steep_out_ref[...] = steep_ref[...]
    for copy in copies:
        copy.wait()
    rows_at = lax.broadcasted_iota(jnp.int32, (8, 256), 0)
    lanes_at = lax.broadcasted_iota(jnp.int32, (8, 256), 1)
    per_cell = TIME_STEP / CELL_SIZE * GRAVITY / 2.0
    bending = TIME_STEP * NDIR / (2.0 * math.pi) * (2.0 * math.pi * LOW_FREQ)
    group_count = group[1] - group[0]

    def body(flipped):
        lead_row, lead_shift = (7, 7) if flipped else (0, 1)
        trail_row, trail_shift = (0, 1) if flipped else (7, 7)
        lat_lane, lat_shift = (255, 255) if flipped else (0, 1)

        def one(first, dirs, slabs, summed, base, f, factors):
            sea = sea_ref[...]
            inverse, weight = factors
            total = jnp.zeros((8, 256), jnp.float32)
            offset = first - group[0]

            def energy(d):
                if d < 0:
                    return raw_ref[1, first + f] * sea
                if d >= HALF_DIRS:
                    return raw_ref[0, first + f] * sea
                return held[d, base + f] * sea

            known = {}
            for d in dirs:
                known = {e: known[e] if e in known else energy(e) for e in (d - 1, d, d + 1)}
                prev, here, after = known[d - 1], known[d], known[d + 1]
                rate = turn[d]
                size = jnp.abs(rate) * bending
                moved = size * jnp.where(rate > 0.0, prev, after)
                along_x = per_cell * abs(math.cos(heading(d)))
                along_y = per_cell * abs(math.sin(heading(d)))
                fixed = 0.0
                if d != LEAD_DIRS:
                    if d < LEAD_DIRS:
                        row = lead_ref[pl.ds(d * group_count + offset + f, 1), :]
                        edge, shift = lead_row, lead_shift
                    else:
                        row = trail_ref[pl.ds((d - LEAD_DIRS - 1) * group_count + offset + f, 1), :]
                        edge, shift = trail_row, trail_shift
                    side = jnp.where(rows_at == edge, jnp.broadcast_to(row, (8, 256)), pltpu.roll(here, shift, 0))
                    moved = moved + along_x * side
                    fixed += along_x
                if d != 0:
                    halo = pltpu.roll(lat_ref[d], (lat_lane % 128) + 128 - (offset + f), 1)
                    halo = jnp.concatenate([halo, halo], axis=1)
                    side = jnp.where(lanes_at == lat_lane, halo, pltpu.roll(here, lat_shift, 1))
                    moved = moved + along_y * side
                    fixed += along_y
                result = (here - inverse * ((size + fixed) * here - moved)) * sea
                if slabs is not None and is_sent(d):
                    send_ref[slabs[d] + f] = result
                elif slabs is not None:
                    keep_ref[d - SIDE_DIRS, f] = result
                total = total + result
            if summed:
                steep_out_ref[...] += weight * total
            return inverse * (1.0 / FREQ_STEP), weight * FREQ_STEP**2

        base = 0
        for first, count, dirs, slabs, summed in passes:
            factors = jnp.float32(1.0 / frequency(first)), jnp.float32((frequency(first) / frequency(NFREQ - 1)) ** 2)
            lax.fori_loop(0, count, functools.partial(one, first, dirs, slabs, summed, base), factors)
            base += count

    half = lax.axis_index("comp")

    @pl.when(half == 0)
    def _():
        body(False)

    @pl.when(half != 0)
    def _():
        body(True)

    if carries:
        send_ref[send_ref.shape[0] - 1] = steep_out_ref[...]


def advect_chunk(passes, group, carries, sea, slopes, spec, sides, steep, raw, after):
    vmem = pl.BlockSpec(memory_space=pltpu.VMEM)
    hold = pl.BlockSpec(memory_space=pl.ANY)
    slabs = sum(count * len(place) for _, count, _, place, _ in passes if place is not None)
    raw = () if raw is None else (raw,)
    out_shape = [
        jax.ShapeDtypeStruct((slabs + carries, 8, 256), jnp.float32),
        jax.ShapeDtypeStruct((HALF_DIRS - 2 * SIDE_DIRS, passes[0][1], 8, 256), jnp.float32),
    ]
    if any(summed for *_, summed in passes):
        out_shape.append(jax.ShapeDtypeStruct((8, 256), jnp.float32))
    return pl.pallas_call(
        functools.partial(advect_kernel, group, passes, carries, len(after), len(raw)),
        out_shape=out_shape,
        in_specs=[vmem, vmem, hold, vmem, vmem, vmem, vmem] + [vmem] * len(raw) + [hold] * len(after),
        out_specs=[vmem] * len(out_shape),
        scratch_shapes=[
            pltpu.VMEM((HALF_DIRS, sum(p[1] for p in passes), 8, 256), jnp.float32),
            pltpu.VMEM((HALF_DIRS, 8, 256), jnp.float32),
            pltpu.SemaphoreType.DMA((len(passes),)),
        ],
        compiler_params=pltpu.CompilerParams(vmem_limit_bytes=VMEM_BYTES),
        cost_estimate=SMALL_COST,
    )(sea, slopes, spec, *sides, steep, *raw, *after)


def source_kernel(
    first, count, inner, outer, chained, last,
    wind_ref, steep_a_ref, steep_b_ref, cum_ref, own_ref, keep_ref, other_ref, *rest,
):
    edge_own_ref, edge_other_ref = rest[:2] if outer else (None, None)
    out_ref, cum_out_ref, result, align, sems = rest[(2 if outer else 0) + chained :]
    weights = [math.cos(heading(m)) ** 2 / (9.0 * SATURATION_LEVEL) for m in range(SIDE_DIRS + 1)]
    steep = (steep_a_ref[...] + steep_b_ref[...]) * (1.0 / (NDIR * NFREQ))
    steep_sq = steep * steep
    for d in range(HALF_DIRS):
        align[d] = math.cos(heading(d)) * wind_ref[0] + math.sin(heading(d)) * wind_ref[1]
    cum_out_ref[...] = cum_ref[...]

    def leave(f):
        return pltpu.make_async_copy(result.at[:, f], out_ref.at[:, first + f], sems.at[f])

    def one(f, omega):
        gain = TIME_STEP * WIND_GROWTH * omega
        loss_sat = TIME_STEP * SATURATION_LOSS * omega
        loss_cum = TIME_STEP * CUMULATIVE_LOSS / NFREQ * omega
        loss_steep = TIME_STEP * STEEPNESS_LOSS * omega
        for half in range(2):
            lanes = slice(128 * half, 128 * half + 128)

            def slab(d, main, edge):
                return main[inner[d] + f, :, lanes] if d in inner else edge[outer[d] + f, :, lanes]

            first_dirs, last_dirs = ALL_DIRS[:SIDE_DIRS], ALL_DIRS[-SIDE_DIRS:]
            line = [slab(d, other_ref, edge_other_ref) for d in last_dirs]
            line += [slab(d, own_ref, edge_own_ref) for d in first_dirs]
            line += [keep_ref[i, f, :, lanes] for i in range(HALF_DIRS - 2 * SIDE_DIRS)]
            line += [slab(d, own_ref, edge_own_ref) for d in last_dirs]
            line += [slab(d, other_ref, edge_other_ref) for d in first_dirs]
            base = 1.0 + loss_steep * steep_sq[:, lanes]
            for d in range(HALF_DIRS):
                at = d + SIDE_DIRS
                level = weights[0] * line[at] - 1.0
                for m in range(1, SIDE_DIRS + 1):
                    level = level + weights[m] * (line[at - m] + line[at + m])
                excess = jnp.maximum(level, 0.0)
                square = excess * excess
                cum = cum_out_ref[d, :, lanes]
                cum_out_ref[d, :, lanes] = cum + square
                grown = 1.0 + gain * jnp.maximum(align[d, :, lanes] * omega - 1.0, 0.0)
                lost = base + loss_sat * square + loss_cum * cum
                result[d, f, :, lanes] = line[at] * grown / lost
        leave(f).start()
        return omega * FREQ_STEP

    lax.fori_loop(0, count, one, jnp.float32(frequency(first)))
    for f in range(count):
        leave(f).wait()


def source_chunk(first, count, inner, outer, last, wind, steep_own, steep_other, cum, own, keep, other, edges, out):
    vmem = pl.BlockSpec(memory_space=pltpu.VMEM)
    hold = pl.BlockSpec(memory_space=pl.ANY)
    chained = out is not None
    operands = (wind, steep_own, steep_other, cum, own, keep, other, *edges) + ((out,) if chained else ())
    out_shape = [jax.ShapeDtypeStruct((HALF_DIRS, NFREQ, 8, 256), jnp.float32)]
    running = [] if last else [jax.ShapeDtypeStruct((HALF_DIRS, 8, 256), jnp.float32)]
    result = pl.pallas_call(
        functools.partial(source_kernel, first, count, inner, outer, chained, last),
        out_shape=out_shape + running,
        in_specs=[vmem] * (7 + len(edges)) + [hold] * chained,
        out_specs=[hold] + [vmem] * len(running),
        scratch_shapes=[pltpu.VMEM((HALF_DIRS, 8, 256), jnp.float32)] * last
        + [
            pltpu.VMEM((HALF_DIRS, count, 8, 256), jnp.float32),
            pltpu.VMEM((HALF_DIRS, 8, 256), jnp.float32),
            pltpu.SemaphoreType.DMA((count,)),
        ],
        input_output_aliases={len(operands) - 1: 0} if chained else {},
        compiler_params=pltpu.CompilerParams(vmem_limit_bytes=VMEM_BYTES),
        cost_estimate=SMALL_COST,
    )(*operands)
    return result[0], None if last else result[1]


def ring_pairs(size, step, wrap):
    return [(i, (i + step) % size) for i in range(size) if wrap or 0 <= i + step < size]


def paired_shards(spectrum, sea_mask, owner_list, owner_count, slopes, friction, wind_angle):
    tiles_x, tiles_y = lax.axis_size("tx"), lax.axis_size("ty")
    half = lax.axis_index("comp")
    sign = 1.0 - 2.0 * half.astype(jnp.float32)
    spec = spectrum.reshape(HALF_DIRS, NFREQ, 8, 256)
    sea = sea_mask.astype(jnp.float32)
    turn = slopes * sign
    wind = (sign * WIND_FACTOR / GRAVITY) * friction * jnp.stack([jnp.cos(wind_angle), jnp.sin(wind_angle)])

    def joined(axis_size, step, wrap):
        ahead = ring_pairs(axis_size, step, wrap)
        back = ring_pairs(axis_size, -step, wrap)
        return ahead + [(axis_size + i, axis_size + j) for i, j in back]

    swap = [(0, 1), (1, 0)]
    lead_pairs = joined(tiles_x, 1, True)
    trail_pairs = joined(tiles_x, -1, True)
    lat_pairs = joined(tiles_y, 1, False)

    spec = pltpu.with_memory_space_constraint(spec, pltpu.HBM)
    bounds = chunk_bounds()
    raw = raw_edges(spec)

    def halo(g, after):
        begin, end = HALO_GROUPS[g]
        lead, trail, lat = pack(begin, end - begin, sea, spec, after)
        sides = (
            lax.ppermute(lead, ("comp", "tx"), lead_pairs),
            lax.ppermute(trail, ("comp", "tx"), trail_pairs),
            lax.ppermute(lat, ("comp", "ty"), lat_pairs),
        )
        return sides, lead

    first_sides, _ = halo(0, raw)
    raw = lax.ppermute(raw, "comp", swap)
    early = sum(end <= HALO_GROUPS[0][1] for _, end in bounds)
    counts = [end - begin for begin, end in bounds]
    places = [slab_index(INNER_DIRS if i == 0 else ALL_DIRS, counts[i]) for i in range(len(bounds))]
    edge_place = slab_index(OUTER_DIRS, counts[0], base=2 * SIDE_DIRS * counts[1])

    def advect(passes, sides, carries, steep, raw, after):
        group = HALO_GROUPS[0] if sides is first_sides else HALO_GROUPS[1]
        return advect_chunk(passes, group, carries, sea, turn, spec, sides, steep, raw, after)

    sent, kept, received, sums = [], [], [], []

    def send(result):
        sent.append(result[0])
        kept.append(result[1])
        received.append(lax.ppermute(result[0], "comp", swap))

    def source(upto):
        for j in range(len(sums), upto):
            outer, edges = (edge_place, (sent[1], received[1])) if j == 0 else (None, ())
            state[:] = source_chunk(
                bounds[j][0], counts[j], places[j], outer, j == len(bounds) - 1, wind, steep, steep_other,
                state[1], sent[j], kept[j], received[j], edges, state[0],
            )
            sums.append(state[1])

    steep = jnp.zeros((8, 256), jnp.float32)
    for i in range(early):
        passes = [(bounds[i][0], counts[i], INNER_DIRS if i == 0 else ALL_DIRS, places[i], True)]
        after = ()
        if i == 1:
            passes.append((bounds[0][0], counts[0], OUTER_DIRS, edge_place, True))
        if i >= 2:
            after = (received[i - 2], packed)
        result = advect(passes, first_sides, False, steep, raw if i else None, after)
        send(result)
        steep = result[2]
        if i == 1:
            later_sides, packed = halo(1, steep)
    state = [None, jnp.zeros((HALF_DIRS, 8, 256), jnp.float32)]
    summing = SUM_CHUNKS
    ahead = bounds[early + summing][0]
    cuts = [ahead + (NFREQ - ahead) * n // summing for n in range(summing + 1)]
    for i in range(early, len(bounds)):
        after = (received[i - 2],)
        if i in SOURCES_DONE:
            source(SOURCES_DONE[i])
            after += (sums[-1],)
        n = i - early
        passes = [(bounds[i][0], counts[i], ALL_DIRS, places[i], n < summing)]
        if n < summing:
            passes.append((cuts[n], cuts[n + 1] - cuts[n], ALL_DIRS, None, True))
        result = advect(passes, later_sides, n == summing - 1, steep, raw, after)
        send(result)
        if n < summing:
            steep = result[2]
        if n == summing - 1:
            steep_other = received[i][-1]
    source(len(bounds))
    out = state[0]
    return out.reshape(spectrum.shape)


def fits_pairs(mesh, spectrum):
    return (
        mesh.shape["comp"] == 2
        and spectrum.shape[0] == NDIR * NFREQ
        and spectrum.shape[1] == 8 * mesh.shape["tx"]
        and spectrum.shape[2] == 256 * mesh.shape["ty"]
    )


def solution(mesh):
    in_specs = (
        P("comp", "tx", "ty"),
        P("tx", "ty"),
        P("tx", "ty", None, None),
        P("tx", "ty", None),
        P(None, "tx", "ty"),
        P("tx", "ty"),
        P("tx", "ty"),
    )
    out_specs = P("comp", "tx", "ty")

    def step(spectrum, *others):
        body = paired_shards if fits_pairs(mesh, spectrum) else shards
        mapped = jax.shard_map(body, mesh=mesh, in_specs=in_specs, out_specs=out_specs, check_vma=False)
        return mapped(spectrum, *others)

    return step
```

```python
import functools
import math

import jax
import jax.numpy as jnp
from jax import lax
from jax.experimental import pallas as pl
from jax.experimental.pallas import tpu as pltpu
from jax.sharding import PartitionSpec as P

NDIR = 36
NFREQ = 50


TIME_STEP = 240.0
CELL_SIZE = 11100.0
GRAVITY = 9.81
LOW_FREQ = 0.0373
HIGH_FREQ = 1.0
WIND_GROWTH = 0.0001
WIND_FACTOR = 28.0
SATURATION_LOSS = 0.0005
CUMULATIVE_LOSS = 0.001
STEEPNESS_LOSS = 0.005
SATURATION_LEVEL = 0.6


def padded(value, sides, width, wrap):
    for axis, dim in sides:
        size, length = (lax.axis_size(axis), value.shape[dim])
        up = [(i, (i + 1) % size) for i in range(size if wrap else size - 1)]
        down = [(j, i) for i, j in up]
        last = lax.slice_in_dim(value, length - width, length, axis=dim)
        first = lax.slice_in_dim(value, 0, width, axis=dim)
        before = lax.ppermute(last, axis, up)
        after = lax.ppermute(first, axis, down)
        value = jnp.concatenate([before, value, after], axis=dim)
    return value


def freq_values(freq_ids):
    return (
        2.0
        * math.pi
        * LOW_FREQ
        * jnp.exp(freq_ids.astype(jnp.float32) * (math.log(HIGH_FREQ / LOW_FREQ) / (NFREQ - 1)))
    )


def wave_tables(first_comp, comp_count):
    comp_ids = first_comp + jnp.arange(comp_count, dtype=jnp.int32)
    headings = (comp_ids // NFREQ).astype(jnp.float32) * (2.0 * math.pi / NDIR)
    return (headings, freq_values(comp_ids % NFREQ))


def advect(
    energy,
    west_side,
    east_side,
    south_side,
    north_side,
    prev_dir,
    next_dir,
    headings,
    ang_freq,
    slopes,
):
    group_speed = GRAVITY / (2.0 * ang_freq)
    along_x = (TIME_STEP / CELL_SIZE * group_speed * jnp.cos(headings))[:, None, None]
    along_y = (TIME_STEP / CELL_SIZE * group_speed * jnp.sin(headings))[:, None, None]
    bending = TIME_STEP * NDIR / (2.0 * math.pi) * (2.0 * math.pi * LOW_FREQ) / ang_freq
    turning = bending[:, None, None] * (
        jnp.sin(headings)[:, None, None] * slopes[0][None]
        - jnp.cos(headings)[:, None, None] * slopes[1][None]
    )
    change = jnp.maximum(along_x, 0.0) * (energy - west_side) + jnp.minimum(along_x, 0.0) * (
        east_side - energy
    )
    change = (
        change
        + jnp.maximum(along_y, 0.0) * (energy - south_side)
        + jnp.minimum(along_y, 0.0) * (north_side - energy)
    )
    change = (
        change
        + jnp.maximum(turning, 0.0) * (energy - prev_dir)
        + jnp.minimum(turning, 0.0) * (next_dir - energy)
    )
    return energy - change


def source_terms(spectra, friction, wind_angle):
    dir_ids = jnp.arange(NDIR, dtype=jnp.int32)
    offset = (dir_ids[:, None] - dir_ids[None, :]) % NDIR
    nearest = jnp.minimum(offset, NDIR - offset)
    spread = jnp.where(
        4 * nearest < NDIR, jnp.cos(offset.astype(jnp.float32) * (2.0 * math.pi / NDIR)) ** 2, 0.0
    )
    spread = spread / jnp.sum(spread, axis=1, keepdims=True)
    sat_level = jnp.einsum("de,efp->dfp", spread, spectra, precision=lax.Precision.HIGHEST)
    excess = jnp.maximum(sat_level / SATURATION_LEVEL - 1.0, 0.0)
    excess_sq = excess * excess
    freq_ids = jnp.arange(NFREQ, dtype=jnp.int32)
    below_mask = (freq_ids[None, :] < freq_ids[:, None]).astype(jnp.float32)
    running = (
        jnp.einsum("fg,dgp->dfp", below_mask, excess_sq, precision=lax.Precision.HIGHEST) / NFREQ
    )
    ang_freq = freq_values(freq_ids)
    weights = (ang_freq / ang_freq[NFREQ - 1]) ** 2
    steepness = jnp.einsum("dfp,f->p", spectra, weights, precision=lax.Precision.HIGHEST) / (
        NDIR * NFREQ
    )
    headings = dir_ids.astype(jnp.float32) * (2.0 * math.pi / NDIR)
    alignment = (
        jnp.cos(headings)[:, None, None] * jnp.cos(wind_angle)[None, None, :]
        + jnp.sin(headings)[:, None, None] * jnp.sin(wind_angle)[None, None, :]
    )
    forcing = WIND_FACTOR / GRAVITY * friction[None, None, :] * ang_freq[None, :, None] * alignment
    growth = WIND_GROWTH * ang_freq[None, :, None] * jnp.maximum(forcing - 1.0, 0.0)
    losses = ang_freq[None, :, None] * (
        SATURATION_LOSS * excess_sq
        + CUMULATIVE_LOSS * running
        + STEEPNESS_LOSS * (steepness * steepness)[None, None, :]
    )
    return spectra * (1.0 + TIME_STEP * growth) / (1.0 + TIME_STEP * losses)


def shards(spectrum, sea_mask, owner_list, owner_count, slopes, friction, wind_angle):
    comp_size = lax.axis_size("comp")
    local_comps = spectrum.shape[0]
    cell_count = spectrum.shape[1] * spectrum.shape[2]
    sea_cells = sea_mask.astype(jnp.float32)
    masked = spectrum * sea_cells[None]
    headings, ang_freq = wave_tables(lax.axis_index("comp") * local_comps, local_comps)
    padded_lon = padded(masked, (("tx", 1),), 1, True)
    padded_lat = padded(masked, (("ty", 2),), 1, False)
    padded_dir = padded(masked, (("comp", 0),), NFREQ, True)
    advected = (
        advect(
            masked,
            padded_lon[:, :-2],
            padded_lon[:, 2:],
            padded_lat[:, :, :-2],
            padded_lat[:, :, 2:],
            padded_dir[:local_comps],
            padded_dir[2 * NFREQ :],
            headings,
            ang_freq,
            slopes,
        )
        * sea_cells[None]
    )
    moved_flat = advected.reshape(local_comps, cell_count)
    cell_names = owner_list[0, 0]
    slot_ids = jnp.arange(cell_names.shape[1], dtype=jnp.int32)
    in_use = slot_ids[None, :] < owner_count[0, 0][:, None]
    target = jnp.where(in_use, cell_names, cell_count).reshape(-1)
    owners = cell_names.shape[0]
    capacity = cell_names.shape[1]
    tiles_x = lax.axis_size("tx")
    cell_ids = jnp.arange(cell_count, dtype=jnp.int32)
    selector = (cell_ids[:, None] == target[None, :]).astype(jnp.float32)
    outgoing = jnp.dot(moved_flat, selector, precision=lax.Precision.HIGHEST).reshape(
        local_comps, owners, capacity
    )
    wind_rows = jnp.stack([friction.reshape(-1), wind_angle.reshape(-1)])
    point_data = jnp.dot(wind_rows, selector, precision=lax.Precision.HIGHEST).reshape(
        2, owners, capacity
    )
    spectra = lax.all_to_all(outgoing, ("comp", "tx"), split_axis=1, concat_axis=1, tiled=True)
    extras = lax.all_to_all(point_data, ("comp", "tx"), split_axis=1, concat_axis=1, tiled=True)
    batch_size = spectra.shape[2]
    full_spec = (
        spectra.reshape(local_comps, comp_size, tiles_x * batch_size)
        .transpose(1, 0, 2)
        .reshape(NDIR, NFREQ, tiles_x * batch_size)
    )
    extra_rows = extras.reshape(2, comp_size, tiles_x * batch_size)[:, 0]
    result = source_terms(full_spec, extra_rows[0], extra_rows[1])
    homeward = (
        result.reshape(comp_size, local_comps, tiles_x * batch_size)
        .transpose(1, 0, 2)
        .reshape(local_comps, comp_size * tiles_x, batch_size)
    )
    returned = lax.all_to_all(homeward, ("comp", "tx"), split_axis=1, concat_axis=1, tiled=True)
    gathered = lax.dot_general(
        returned.reshape(local_comps, owners * capacity),
        selector,
        (((1,), (1,)), ((), ())),
        precision=lax.Precision.HIGHEST,
    )
    listed = jnp.sum(selector, axis=1) > 0.5
    updated = jnp.where(listed[None], gathered, moved_flat)
    return updated.reshape(spectrum.shape)


def chunk_bounds():
    return [(5 * i, 5 * i + 5) for i in range(9)] + [(45, 48), (48, 50)]


HALO_GROUPS = ((0, 15), (15, 50))
SUM_CHUNKS = 3
SOURCES_DONE = {8: 2, 9: 5, 10: 7}
HALF_DIRS = NDIR // 2
SIDE_DIRS = 8
LEAD_DIRS = 9
VMEM_BYTES = 24 * 1024 * 1024
SMALL_COST = pl.CostEstimate(flops=1024, bytes_accessed=1024, transcendentals=0)


FREQ_STEP = (HIGH_FREQ / LOW_FREQ) ** (1.0 / (NFREQ - 1))


def frequency(index):
    return 2.0 * math.pi * LOW_FREQ * FREQ_STEP**index


def heading(index):
    return 2.0 * math.pi * index / NDIR


def raw_kernel(spec_ref, raw_ref, sems):
    copies = []
    for i, d in enumerate((0, HALF_DIRS - 1)):
        copy = pltpu.make_async_copy(spec_ref.at[d], raw_ref.at[i], sems.at[i])
        copy.start()
        copies.append(copy)
    for copy in copies:
        copy.wait()


def raw_edges(spec):
    return pl.pallas_call(
        raw_kernel,
        out_shape=jax.ShapeDtypeStruct((2, NFREQ, 8, 256), jnp.float32),
        in_specs=[pl.BlockSpec(memory_space=pl.ANY)],
        out_specs=pl.BlockSpec(memory_space=pltpu.VMEM),
        scratch_shapes=[pltpu.SemaphoreType.DMA((2,))],
        compiler_params=pltpu.CompilerParams(vmem_limit_bytes=VMEM_BYTES),
        cost_estimate=SMALL_COST,
    )(spec)


def pack_kernel(first, count, sea_ref, spec_ref, after_ref, lead_ref, trail_ref, lat_ref, held, sems):
    def body(flipped):
        lead_row, trail_row = (0, 7) if flipped else (7, 0)
        part = 0 if flipped else 1
        copies = []
        for d in range(HALF_DIRS):
            for h in range(2):
                copy = pltpu.make_async_copy(
                    spec_ref.at[d, pl.ds(first, count), :, pl.ds(128 * h, 128)], held.at[h, d], sems.at[h, d]
                )
                copy.start()
                copies.append(copy)
        rows = held.reshape(2 * HALF_DIRS * count * 8, 128)
        for d in range(HALF_DIRS):
            for h in range(2):
                copies[2 * d + h].wait()
                lanes_here = slice(128 * h, 128 * h + 128)
                start = (h * HALF_DIRS + d) * count * 8
                if d < LEAD_DIRS:
                    column = rows[pl.ds(start + lead_row, count, stride=8), :]
                    lead_ref[d * count : (d + 1) * count, lanes_here] = column * sea_ref[lead_row : lead_row + 1, lanes_here]
                elif d > LEAD_DIRS:
                    t = d - LEAD_DIRS - 1
                    column = rows[pl.ds(start + trail_row, count, stride=8), :]
                    trail_ref[t * count : (t + 1) * count, lanes_here] = column * sea_ref[trail_row : trail_row + 1, lanes_here]
        lane = 0 if flipped else 127
        lanes = lax.broadcasted_iota(jnp.int32, (8, 128), 1)
        sea_line = jnp.broadcast_to(sea_ref[:, 128 * part + lane : 128 * part + lane + 1], (8, 128))

        def one(f, kept):
            here = lanes == f
            return tuple(
                jnp.where(here, jnp.broadcast_to(held[part, d, f][:, lane : lane + 1], (8, 128)), kept[d])
                for d in range(HALF_DIRS)
            )

        zeros = jnp.zeros((8, 128), jnp.float32)
        kept = lax.fori_loop(0, count, one, (zeros,) * HALF_DIRS, unroll=5)
        for d in range(HALF_DIRS):
            lat_ref[d] = kept[d] * sea_line

    half = lax.axis_index("comp")

    @pl.when(half == 0)
    def _():
        body(False)

    @pl.when(half != 0)
    def _():
        body(True)


def pack(first, count, sea, spec, after):
    vmem = pl.BlockSpec(memory_space=pltpu.VMEM)
    hold = pl.BlockSpec(memory_space=pl.ANY)
    return pl.pallas_call(
        functools.partial(pack_kernel, first, count),
        out_shape=[
            jax.ShapeDtypeStruct((LEAD_DIRS * count, 256), jnp.float32),
            jax.ShapeDtypeStruct(((HALF_DIRS - LEAD_DIRS - 1) * count, 256), jnp.float32),
            jax.ShapeDtypeStruct((HALF_DIRS, 8, 128), jnp.float32),
        ],
        in_specs=[vmem, hold, hold],
        out_specs=[vmem] * 3,
        scratch_shapes=[
            pltpu.VMEM((2, HALF_DIRS, count, 8, 128), jnp.float32),
            pltpu.SemaphoreType.DMA((2, HALF_DIRS)),
        ],
        compiler_params=pltpu.CompilerParams(vmem_limit_bytes=VMEM_BYTES),
        cost_estimate=SMALL_COST,
    )(sea, spec, after)


ALL_DIRS = tuple(range(HALF_DIRS))
INNER_DIRS = ALL_DIRS[1:-1]
OUTER_DIRS = (0, HALF_DIRS - 1)


def is_sent(d):
    return d < SIDE_DIRS or d >= HALF_DIRS - SIDE_DIRS


def slab_index(dirs, count, base=0):
    return {d: base + count * n for n, d in enumerate(d for d in dirs if is_sent(d))}


def advect_kernel(
    group, passes, carries, waits, has_raw,
    sea_ref, slope_ref, spec_ref, lead_ref, trail_ref, lat_ref, steep_ref, *rest,
):
    sums = any(summed for *_, summed in passes)
    raw_ref = rest[0] if has_raw else None
    rest = rest[has_raw + waits :]
    held, turn, sem = rest[-3:]
    send_ref, keep_ref = rest[:2]
    if sums:
        steep_out_ref = rest[-4]
    copies, base = [], 0
    for i, (first, count, *_) in enumerate(passes):
        copy = pltpu.make_async_copy(spec_ref.at[:, pl.ds(first, count)], held.at[:, pl.ds(base, count)], sem.at[i])
        copy.start()
        copies.append(copy)
        base += count
    for d in range(HALF_DIRS):
        turn[d] = math.sin(heading(d)) * slope_ref[0] - math.cos(heading(d)) * slope_ref[1]
    if sums:
        steep_out_ref[...] = steep_ref[...]
    for copy in copies:
        copy.wait()
    rows_at = lax.broadcasted_iota(jnp.int32, (8, 256), 0)
    lanes_at = lax.broadcasted_iota(jnp.int32, (8, 256), 1)
    per_cell = TIME_STEP / CELL_SIZE * GRAVITY / 2.0
    bending = TIME_STEP * NDIR / (2.0 * math.pi) * (2.0 * math.pi * LOW_FREQ)
    group_count = group[1] - group[0]

    def body(flipped):
        lead_row, lead_shift = (7, 7) if flipped else (0, 1)
        trail_row, trail_shift = (0, 1) if flipped else (7, 7)
        lat_lane, lat_shift = (255, 255) if flipped else (0, 1)

        def one(first, dirs, slabs, summed, base, f, factors):
            sea = sea_ref[...]
            inverse, weight = factors
            total = jnp.zeros((8, 256), jnp.float32)
            offset = first - group[0]

            def energy(d):
                if d < 0:
                    return raw_ref[1, first + f] * sea
                if d >= HALF_DIRS:
                    return raw_ref[0, first + f] * sea
                return held[d, base + f] * sea

            known = {}
            for d in dirs:
                known = {e: known[e] if e in known else energy(e) for e in (d - 1, d, d + 1)}
                prev, here, after = known[d - 1], known[d], known[d + 1]
                rate = turn[d]
                size = jnp.abs(rate) * bending
                moved = size * jnp.where(rate > 0.0, prev, after)
                along_x = per_cell * abs(math.cos(heading(d)))
                along_y = per_cell * abs(math.sin(heading(d)))
                fixed = 0.0
                if d != LEAD_DIRS:
                    if d < LEAD_DIRS:
                        row = lead_ref[pl.ds(d * group_count + offset + f, 1), :]
                        edge, shift = lead_row, lead_shift
                    else:
                        row = trail_ref[pl.ds((d - LEAD_DIRS - 1) * group_count + offset + f, 1), :]
                        edge, shift = trail_row, trail_shift
                    side = jnp.where(rows_at == edge, jnp.broadcast_to(row, (8, 256)), pltpu.roll(here, shift, 0))
                    moved = moved + along_x * side
                    fixed += along_x
                if d != 0:
                    halo = pltpu.roll(lat_ref[d], (lat_lane % 128) + 128 - (offset + f), 1)
                    halo = jnp.concatenate([halo, halo], axis=1)
                    side = jnp.where(lanes_at == lat_lane, halo, pltpu.roll(here, lat_shift, 1))
                    moved = moved + along_y * side
                    fixed += along_y
                result = (here - inverse * ((size + fixed) * here - moved)) * sea
                if slabs is not None and is_sent(d):
                    send_ref[slabs[d] + f] = result
                elif slabs is not None:
                    keep_ref[d - SIDE_DIRS, f] = result
                total = total + result
            if summed:
                steep_out_ref[...] += weight * total
            return inverse * (1.0 / FREQ_STEP), weight * FREQ_STEP**2

        base = 0
        for first, count, dirs, slabs, summed in passes:
            factors = jnp.float32(1.0 / frequency(first)), jnp.float32((frequency(first) / frequency(NFREQ - 1)) ** 2)
            lax.fori_loop(0, count, functools.partial(one, first, dirs, slabs, summed, base), factors)
            base += count

    half = lax.axis_index("comp")

    @pl.when(half == 0)
    def _():
        body(False)

    @pl.when(half != 0)
    def _():
        body(True)

    if carries:
        send_ref[send_ref.shape[0] - 1] = steep_out_ref[...]


def advect_chunk(passes, group, carries, sea, slopes, spec, sides, steep, raw, after):
    vmem = pl.BlockSpec(memory_space=pltpu.VMEM)
    hold = pl.BlockSpec(memory_space=pl.ANY)
    slabs = sum(count * len(place) for _, count, _, place, _ in passes if place is not None)
    raw = () if raw is None else (raw,)
    out_shape = [
        jax.ShapeDtypeStruct((slabs + carries, 8, 256), jnp.float32),
        jax.ShapeDtypeStruct((HALF_DIRS - 2 * SIDE_DIRS, passes[0][1], 8, 256), jnp.float32),
    ]
    if any(summed for *_, summed in passes):
        out_shape.append(jax.ShapeDtypeStruct((8, 256), jnp.float32))
    return pl.pallas_call(
        functools.partial(advect_kernel, group, passes, carries, len(after), len(raw)),
        out_shape=out_shape,
        in_specs=[vmem, vmem, hold, vmem, vmem, vmem, vmem] + [vmem] * len(raw) + [hold] * len(after),
        out_specs=[vmem] * len(out_shape),
        scratch_shapes=[
            pltpu.VMEM((HALF_DIRS, sum(p[1] for p in passes), 8, 256), jnp.float32),
            pltpu.VMEM((HALF_DIRS, 8, 256), jnp.float32),
            pltpu.SemaphoreType.DMA((len(passes),)),
        ],
        compiler_params=pltpu.CompilerParams(vmem_limit_bytes=VMEM_BYTES),
        cost_estimate=SMALL_COST,
    )(sea, slopes, spec, *sides, steep, *raw, *after)


def source_kernel(
    first, count, inner, outer, chained, last,
    wind_ref, steep_a_ref, steep_b_ref, cum_ref, own_ref, keep_ref, other_ref, *rest,
):
    edge_own_ref, edge_other_ref = rest[:2] if outer else (None, None)
    out_ref, cum_out_ref, result, align, sems = rest[(2 if outer else 0) + chained :]
    weights = [math.cos(heading(m)) ** 2 / (9.0 * SATURATION_LEVEL) for m in range(SIDE_DIRS + 1)]
    peer = 1 - lax.axis_index("comp")
    steep = (steep_a_ref[...] + steep_b_ref[...]) * (1.0 / (NDIR * NFREQ))
    steep_sq = steep * steep
    for d in range(HALF_DIRS):
        align[d] = math.cos(heading(d)) * wind_ref[0] + math.sin(heading(d)) * wind_ref[1]
    cum_out_ref[...] = cum_ref[...]

    def leave(f):
        return pltpu.make_async_copy(result.at[:, f], out_ref.at[:, first + f], sems.at[f])

    def one(f, omega):
        gain = TIME_STEP * WIND_GROWTH * omega
        loss_sat = TIME_STEP * SATURATION_LOSS * omega
        loss_cum = TIME_STEP * CUMULATIVE_LOSS / NFREQ * omega
        loss_steep = TIME_STEP * STEEPNESS_LOSS * omega
        for half in range(2):
            lanes = slice(128 * half, 128 * half + 128)

            def slab(d, main, edge):
                place = inner[d] + f if d in inner else outer[d] + f
                source = main if d in inner else edge
                return source[place, :, lanes] if len(source.shape) == 3 else source[peer, place, :, lanes]

            first_dirs, last_dirs = ALL_DIRS[:SIDE_DIRS], ALL_DIRS[-SIDE_DIRS:]
            line = [slab(d, other_ref, edge_other_ref) for d in last_dirs]
            line += [slab(d, own_ref, edge_own_ref) for d in first_dirs]
            line += [keep_ref[i, f, :, lanes] for i in range(HALF_DIRS - 2 * SIDE_DIRS)]
            line += [slab(d, own_ref, edge_own_ref) for d in last_dirs]
            line += [slab(d, other_ref, edge_other_ref) for d in first_dirs]
            base = 1.0 + loss_steep * steep_sq[:, lanes]
            for d in range(HALF_DIRS):
                at = d + SIDE_DIRS
                level = weights[0] * line[at] - 1.0
                for m in range(1, SIDE_DIRS + 1):
                    level = level + weights[m] * (line[at - m] + line[at + m])
                excess = jnp.maximum(level, 0.0)
                square = excess * excess
                cum = cum_out_ref[d, :, lanes]
                cum_out_ref[d, :, lanes] = cum + square
                grown = 1.0 + gain * jnp.maximum(align[d, :, lanes] * omega - 1.0, 0.0)
                lost = base + loss_sat * square + loss_cum * cum
                result[d, f, :, lanes] = line[at] * grown / lost
        leave(f).start()
        return omega * FREQ_STEP

    lax.fori_loop(0, count, one, jnp.float32(frequency(first)))
    for f in range(count):
        leave(f).wait()


def source_chunk(first, count, inner, outer, last, wind, steep_own, steep_other, cum, own, keep, other, edges, out):
    vmem = pl.BlockSpec(memory_space=pltpu.VMEM)
    hold = pl.BlockSpec(memory_space=pl.ANY)
    chained = out is not None
    operands = (wind, steep_own, steep_other, cum, own, keep, other, *edges) + ((out,) if chained else ())
    out_shape = [jax.ShapeDtypeStruct((HALF_DIRS, NFREQ, 8, 256), jnp.float32)]
    running = [] if last else [jax.ShapeDtypeStruct((HALF_DIRS, 8, 256), jnp.float32)]
    result = pl.pallas_call(
        functools.partial(source_kernel, first, count, inner, outer, chained, last),
        out_shape=out_shape + running,
        in_specs=[vmem] * (7 + len(edges)) + [hold] * chained,
        out_specs=[hold] + [vmem] * len(running),
        scratch_shapes=[pltpu.VMEM((HALF_DIRS, 8, 256), jnp.float32)] * last
        + [
            pltpu.VMEM((HALF_DIRS, count, 8, 256), jnp.float32),
            pltpu.VMEM((HALF_DIRS, 8, 256), jnp.float32),
            pltpu.SemaphoreType.DMA((count,)),
        ],
        input_output_aliases={len(operands) - 1: 0} if chained else {},
        compiler_params=pltpu.CompilerParams(vmem_limit_bytes=VMEM_BYTES),
        cost_estimate=SMALL_COST,
    )(*operands)
    return result[0], None if last else result[1]


def ring_pairs(size, step, wrap):
    return [(i, (i + step) % size) for i in range(size) if wrap or 0 <= i + step < size]


def paired_shards(spectrum, sea_mask, owner_list, owner_count, slopes, friction, wind_angle):
    tiles_x, tiles_y = lax.axis_size("tx"), lax.axis_size("ty")
    half = lax.axis_index("comp")
    sign = 1.0 - 2.0 * half.astype(jnp.float32)
    spec = spectrum.reshape(HALF_DIRS, NFREQ, 8, 256)
    sea = sea_mask.astype(jnp.float32)
    turn = slopes * sign
    wind = (sign * WIND_FACTOR / GRAVITY) * friction * jnp.stack([jnp.cos(wind_angle), jnp.sin(wind_angle)])

    def joined(axis_size, step, wrap):
        ahead = ring_pairs(axis_size, step, wrap)
        back = ring_pairs(axis_size, -step, wrap)
        return ahead + [(axis_size + i, axis_size + j) for i, j in back]

    swap = [(0, 1), (1, 0)]
    lead_pairs = joined(tiles_x, 1, True)
    trail_pairs = joined(tiles_x, -1, True)
    lat_pairs = joined(tiles_y, 1, False)

    spec = pltpu.with_memory_space_constraint(spec, pltpu.HBM)
    bounds = chunk_bounds()
    raw = raw_edges(spec)

    def halo(g, after):
        begin, end = HALO_GROUPS[g]
        lead, trail, lat = pack(begin, end - begin, sea, spec, after)
        sides = (
            lax.ppermute(lead, ("comp", "tx"), lead_pairs),
            lax.ppermute(trail, ("comp", "tx"), trail_pairs),
            lax.ppermute(lat, ("comp", "ty"), lat_pairs),
        )
        return sides, lead

    first_sides, _ = halo(0, raw)
    raw = lax.ppermute(raw, "comp", swap)
    early = sum(end <= HALO_GROUPS[0][1] for _, end in bounds)
    counts = [end - begin for begin, end in bounds]
    places = [slab_index(INNER_DIRS if i == 0 else ALL_DIRS, counts[i]) for i in range(len(bounds))]
    edge_place = slab_index(OUTER_DIRS, counts[0], base=2 * SIDE_DIRS * counts[1])

    def advect(passes, sides, carries, steep, raw, after):
        group = HALO_GROUPS[0] if sides is first_sides else HALO_GROUPS[1]
        return advect_chunk(passes, group, carries, sea, turn, spec, sides, steep, raw, after)

    sent, kept, received, sums = [], [], [], []

    def send(result):
        sent.append(result[0])
        kept.append(result[1])
        received.append(lax.all_gather(result[0], "comp"))

    def source(upto):
        for j in range(len(sums), upto):
            outer, edges = (edge_place, (sent[1], received[1])) if j == 0 else (None, ())
            state[:] = source_chunk(
                bounds[j][0], counts[j], places[j], outer, j == len(bounds) - 1, wind, steep, steep_other,
                state[1], sent[j], kept[j], received[j], edges, state[0],
            )
            sums.append(state[1])

    steep = jnp.zeros((8, 256), jnp.float32)
    for i in range(early):
        passes = [(bounds[i][0], counts[i], INNER_DIRS if i == 0 else ALL_DIRS, places[i], True)]
        after = ()
        if i == 1:
            passes.append((bounds[0][0], counts[0], OUTER_DIRS, edge_place, True))
        if i >= 2:
            after = (received[i - 2], packed)
        result = advect(passes, first_sides, False, steep, raw if i else None, after)
        send(result)
        steep = result[2]
        if i == 1:
            later_sides, packed = halo(1, steep)
    state = [None, jnp.zeros((HALF_DIRS, 8, 256), jnp.float32)]
    summing = SUM_CHUNKS
    ahead = bounds[early + summing][0]
    cuts = [ahead + (NFREQ - ahead) * n // summing for n in range(summing + 1)]
    for i in range(early, len(bounds)):
        after = (received[i - 2],)
        if i in SOURCES_DONE:
            source(SOURCES_DONE[i])
            after += (sums[-1],)
        n = i - early
        passes = [(bounds[i][0], counts[i], ALL_DIRS, places[i], n < summing)]
        if n < summing:
            passes.append((cuts[n], cuts[n + 1] - cuts[n], ALL_DIRS, None, True))
        result = advect(passes, later_sides, n == summing - 1, steep, raw, after)
        send(result)
        if n < summing:
            steep = result[2]
        if n == summing - 1:
            steep_other = lax.dynamic_index_in_dim(received[i][:, -1], 1 - half, 0, keepdims=False)
    source(len(bounds))
    out = state[0]
    return out.reshape(spectrum.shape)


def fits_pairs(mesh, spectrum):
    return (
        mesh.shape["comp"] == 2
        and spectrum.shape[0] == NDIR * NFREQ
        and spectrum.shape[1] == 8 * mesh.shape["tx"]
        and spectrum.shape[2] == 256 * mesh.shape["ty"]
    )


def solution(mesh):
    in_specs = (
        P("comp", "tx", "ty"),
        P("tx", "ty"),
        P("tx", "ty", None, None),
        P("tx", "ty", None),
        P(None, "tx", "ty"),
        P("tx", "ty"),
        P("tx", "ty"),
    )
    out_specs = P("comp", "tx", "ty")

    def step(spectrum, *others):
        body = paired_shards if fits_pairs(mesh, spectrum) else shards
        mapped = jax.shard_map(body, mesh=mesh, in_specs=in_specs, out_specs=out_specs, check_vma=False)
        return mapped(spectrum, *others)

    return step
```

```python
import functools
import math

import jax
import jax.numpy as jnp
from jax import lax
from jax.experimental import pallas as pl
from jax.experimental.pallas import tpu as pltpu
from jax.sharding import PartitionSpec as P

NDIR = 36
NFREQ = 50


TIME_STEP = 240.0
CELL_SIZE = 11100.0
GRAVITY = 9.81
LOW_FREQ = 0.0373
HIGH_FREQ = 1.0
WIND_GROWTH = 0.0001
WIND_FACTOR = 28.0
SATURATION_LOSS = 0.0005
CUMULATIVE_LOSS = 0.001
STEEPNESS_LOSS = 0.005
SATURATION_LEVEL = 0.6


def padded(value, sides, width, wrap):
    for axis, dim in sides:
        size, length = (lax.axis_size(axis), value.shape[dim])
        up = [(i, (i + 1) % size) for i in range(size if wrap else size - 1)]
        down = [(j, i) for i, j in up]
        last = lax.slice_in_dim(value, length - width, length, axis=dim)
        first = lax.slice_in_dim(value, 0, width, axis=dim)
        before = lax.ppermute(last, axis, up)
        after = lax.ppermute(first, axis, down)
        value = jnp.concatenate([before, value, after], axis=dim)
    return value


def freq_values(freq_ids):
    return (
        2.0
        * math.pi
        * LOW_FREQ
        * jnp.exp(freq_ids.astype(jnp.float32) * (math.log(HIGH_FREQ / LOW_FREQ) / (NFREQ - 1)))
    )


def wave_tables(first_comp, comp_count):
    comp_ids = first_comp + jnp.arange(comp_count, dtype=jnp.int32)
    headings = (comp_ids // NFREQ).astype(jnp.float32) * (2.0 * math.pi / NDIR)
    return (headings, freq_values(comp_ids % NFREQ))


def advect(
    energy,
    west_side,
    east_side,
    south_side,
    north_side,
    prev_dir,
    next_dir,
    headings,
    ang_freq,
    slopes,
):
    group_speed = GRAVITY / (2.0 * ang_freq)
    along_x = (TIME_STEP / CELL_SIZE * group_speed * jnp.cos(headings))[:, None, None]
    along_y = (TIME_STEP / CELL_SIZE * group_speed * jnp.sin(headings))[:, None, None]
    bending = TIME_STEP * NDIR / (2.0 * math.pi) * (2.0 * math.pi * LOW_FREQ) / ang_freq
    turning = bending[:, None, None] * (
        jnp.sin(headings)[:, None, None] * slopes[0][None]
        - jnp.cos(headings)[:, None, None] * slopes[1][None]
    )
    change = jnp.maximum(along_x, 0.0) * (energy - west_side) + jnp.minimum(along_x, 0.0) * (
        east_side - energy
    )
    change = (
        change
        + jnp.maximum(along_y, 0.0) * (energy - south_side)
        + jnp.minimum(along_y, 0.0) * (north_side - energy)
    )
    change = (
        change
        + jnp.maximum(turning, 0.0) * (energy - prev_dir)
        + jnp.minimum(turning, 0.0) * (next_dir - energy)
    )
    return energy - change


def source_terms(spectra, friction, wind_angle):
    dir_ids = jnp.arange(NDIR, dtype=jnp.int32)
    offset = (dir_ids[:, None] - dir_ids[None, :]) % NDIR
    nearest = jnp.minimum(offset, NDIR - offset)
    spread = jnp.where(
        4 * nearest < NDIR, jnp.cos(offset.astype(jnp.float32) * (2.0 * math.pi / NDIR)) ** 2, 0.0
    )
    spread = spread / jnp.sum(spread, axis=1, keepdims=True)
    sat_level = jnp.einsum("de,efp->dfp", spread, spectra, precision=lax.Precision.HIGHEST)
    excess = jnp.maximum(sat_level / SATURATION_LEVEL - 1.0, 0.0)
    excess_sq = excess * excess
    freq_ids = jnp.arange(NFREQ, dtype=jnp.int32)
    below_mask = (freq_ids[None, :] < freq_ids[:, None]).astype(jnp.float32)
    running = (
        jnp.einsum("fg,dgp->dfp", below_mask, excess_sq, precision=lax.Precision.HIGHEST) / NFREQ
    )
    ang_freq = freq_values(freq_ids)
    weights = (ang_freq / ang_freq[NFREQ - 1]) ** 2
    steepness = jnp.einsum("dfp,f->p", spectra, weights, precision=lax.Precision.HIGHEST) / (
        NDIR * NFREQ
    )
    headings = dir_ids.astype(jnp.float32) * (2.0 * math.pi / NDIR)
    alignment = (
        jnp.cos(headings)[:, None, None] * jnp.cos(wind_angle)[None, None, :]
        + jnp.sin(headings)[:, None, None] * jnp.sin(wind_angle)[None, None, :]
    )
    forcing = WIND_FACTOR / GRAVITY * friction[None, None, :] * ang_freq[None, :, None] * alignment
    growth = WIND_GROWTH * ang_freq[None, :, None] * jnp.maximum(forcing - 1.0, 0.0)
    losses = ang_freq[None, :, None] * (
        SATURATION_LOSS * excess_sq
        + CUMULATIVE_LOSS * running
        + STEEPNESS_LOSS * (steepness * steepness)[None, None, :]
    )
    return spectra * (1.0 + TIME_STEP * growth) / (1.0 + TIME_STEP * losses)


def shards(spectrum, sea_mask, owner_list, owner_count, slopes, friction, wind_angle):
    comp_size = lax.axis_size("comp")
    local_comps = spectrum.shape[0]
    cell_count = spectrum.shape[1] * spectrum.shape[2]
    sea_cells = sea_mask.astype(jnp.float32)
    masked = spectrum * sea_cells[None]
    headings, ang_freq = wave_tables(lax.axis_index("comp") * local_comps, local_comps)
    padded_lon = padded(masked, (("tx", 1),), 1, True)
    padded_lat = padded(masked, (("ty", 2),), 1, False)
    padded_dir = padded(masked, (("comp", 0),), NFREQ, True)
    advected = (
        advect(
            masked,
            padded_lon[:, :-2],
            padded_lon[:, 2:],
            padded_lat[:, :, :-2],
            padded_lat[:, :, 2:],
            padded_dir[:local_comps],
            padded_dir[2 * NFREQ :],
            headings,
            ang_freq,
            slopes,
        )
        * sea_cells[None]
    )
    moved_flat = advected.reshape(local_comps, cell_count)
    cell_names = owner_list[0, 0]
    slot_ids = jnp.arange(cell_names.shape[1], dtype=jnp.int32)
    in_use = slot_ids[None, :] < owner_count[0, 0][:, None]
    target = jnp.where(in_use, cell_names, cell_count).reshape(-1)
    owners = cell_names.shape[0]
    capacity = cell_names.shape[1]
    tiles_x = lax.axis_size("tx")
    cell_ids = jnp.arange(cell_count, dtype=jnp.int32)
    selector = (cell_ids[:, None] == target[None, :]).astype(jnp.float32)
    outgoing = jnp.dot(moved_flat, selector, precision=lax.Precision.HIGHEST).reshape(
        local_comps, owners, capacity
    )
    wind_rows = jnp.stack([friction.reshape(-1), wind_angle.reshape(-1)])
    point_data = jnp.dot(wind_rows, selector, precision=lax.Precision.HIGHEST).reshape(
        2, owners, capacity
    )
    spectra = lax.all_to_all(outgoing, ("comp", "tx"), split_axis=1, concat_axis=1, tiled=True)
    extras = lax.all_to_all(point_data, ("comp", "tx"), split_axis=1, concat_axis=1, tiled=True)
    batch_size = spectra.shape[2]
    full_spec = (
        spectra.reshape(local_comps, comp_size, tiles_x * batch_size)
        .transpose(1, 0, 2)
        .reshape(NDIR, NFREQ, tiles_x * batch_size)
    )
    extra_rows = extras.reshape(2, comp_size, tiles_x * batch_size)[:, 0]
    result = source_terms(full_spec, extra_rows[0], extra_rows[1])
    homeward = (
        result.reshape(comp_size, local_comps, tiles_x * batch_size)
        .transpose(1, 0, 2)
        .reshape(local_comps, comp_size * tiles_x, batch_size)
    )
    returned = lax.all_to_all(homeward, ("comp", "tx"), split_axis=1, concat_axis=1, tiled=True)
    gathered = lax.dot_general(
        returned.reshape(local_comps, owners * capacity),
        selector,
        (((1,), (1,)), ((), ())),
        precision=lax.Precision.HIGHEST,
    )
    listed = jnp.sum(selector, axis=1) > 0.5
    updated = jnp.where(listed[None], gathered, moved_flat)
    return updated.reshape(spectrum.shape)


def chunk_bounds():
    return [(5 * i, 5 * i + 5) for i in range(9)] + [(45, 47), (47, 49), (49, 50)]


HALO_GROUPS = ((0, 15), (15, 50))
SUM_CHUNKS = 3
SOURCES_DONE = {8: 2, 9: 5, 10: 7, 11: 9}
HALF_DIRS = NDIR // 2
SIDE_DIRS = 8
LEAD_DIRS = 9
VMEM_BYTES = 24 * 1024 * 1024
SMALL_COST = pl.CostEstimate(flops=1024, bytes_accessed=1024, transcendentals=0)


FREQ_STEP = (HIGH_FREQ / LOW_FREQ) ** (1.0 / (NFREQ - 1))


def frequency(index):
    return 2.0 * math.pi * LOW_FREQ * FREQ_STEP**index


def heading(index):
    return 2.0 * math.pi * index / NDIR


def raw_kernel(spec_ref, raw_ref, sems):
    copies = []
    for i, d in enumerate((0, HALF_DIRS - 1)):
        copy = pltpu.make_async_copy(spec_ref.at[d], raw_ref.at[i], sems.at[i])
        copy.start()
        copies.append(copy)
    for copy in copies:
        copy.wait()


def raw_edges(spec):
    return pl.pallas_call(
        raw_kernel,
        out_shape=jax.ShapeDtypeStruct((2, NFREQ, 8, 256), jnp.float32),
        in_specs=[pl.BlockSpec(memory_space=pl.ANY)],
        out_specs=pl.BlockSpec(memory_space=pltpu.VMEM),
        scratch_shapes=[pltpu.SemaphoreType.DMA((2,))],
        compiler_params=pltpu.CompilerParams(vmem_limit_bytes=VMEM_BYTES),
        cost_estimate=SMALL_COST,
    )(spec)


def pack_kernel(first, count, sea_ref, spec_ref, after_ref, lead_ref, trail_ref, lat_ref, held, sems):
    def body(flipped):
        lead_row, trail_row = (0, 7) if flipped else (7, 0)
        part = 0 if flipped else 1
        copies = []
        for d in range(HALF_DIRS):
            for h in range(2):
                copy = pltpu.make_async_copy(
                    spec_ref.at[d, pl.ds(first, count), :, pl.ds(128 * h, 128)], held.at[h * HALF_DIRS + d], sems.at[h * HALF_DIRS + d]
                )
                copy.start()
                copies.append(copy)
        rows = held.reshape((2 * HALF_DIRS + 1) * count * 8, 128)
        for d in range(HALF_DIRS):
            for h in range(2):
                copies[2 * d + h].wait()
                lanes_here = slice(128 * h, 128 * h + 128)
                start = (h * HALF_DIRS + d) * count * 8
                if d < LEAD_DIRS:
                    column = rows[pl.ds(start + lead_row, count, stride=8), :]
                    lead_ref[d * count : (d + 1) * count, lanes_here] = column * sea_ref[lead_row : lead_row + 1, lanes_here]
                elif d > LEAD_DIRS:
                    t = d - LEAD_DIRS - 1
                    column = rows[pl.ds(start + trail_row, count, stride=8), :]
                    trail_ref[t * count : (t + 1) * count, lanes_here] = column * sea_ref[trail_row : trail_row + 1, lanes_here]
        lane = 0 if flipped else 127
        lanes = lax.broadcasted_iota(jnp.int32, (8, 128), 1)
        sea_line = jnp.broadcast_to(sea_ref[:, 128 * part + lane : 128 * part + lane + 1], (8, 128))

        def one(f, kept):
            here = lanes == f
            return tuple(
                jnp.where(here, jnp.broadcast_to(held[part * HALF_DIRS + d, f][:, lane : lane + 1], (8, 128)), kept[d])
                for d in range(HALF_DIRS)
            )

        zeros = jnp.zeros((8, 128), jnp.float32)
        kept = lax.fori_loop(0, count, one, (zeros,) * HALF_DIRS, unroll=5)
        for d in range(HALF_DIRS):
            lat_ref[d] = kept[d] * sea_line

    half = lax.axis_index("comp")

    @pl.when(half == 0)
    def _():
        body(False)

    @pl.when(half != 0)
    def _():
        body(True)


def pack(first, count, sea, spec, after):
    vmem = pl.BlockSpec(memory_space=pltpu.VMEM)
    hold = pl.BlockSpec(memory_space=pl.ANY)
    return pl.pallas_call(
        functools.partial(pack_kernel, first, count),
        out_shape=[
            jax.ShapeDtypeStruct((LEAD_DIRS * count, 256), jnp.float32),
            jax.ShapeDtypeStruct(((HALF_DIRS - LEAD_DIRS - 1) * count, 256), jnp.float32),
            jax.ShapeDtypeStruct((HALF_DIRS, 8, 128), jnp.float32),
        ],
        in_specs=[vmem, hold, hold],
        out_specs=[vmem] * 3,
        scratch_shapes=[
            pltpu.VMEM((2 * HALF_DIRS + 1, count, 8, 128), jnp.float32),
            pltpu.SemaphoreType.DMA((2 * HALF_DIRS,)),
        ],
        compiler_params=pltpu.CompilerParams(vmem_limit_bytes=VMEM_BYTES),
        cost_estimate=SMALL_COST,
    )(sea, spec, after)


ALL_DIRS = tuple(range(HALF_DIRS))
INNER_DIRS = ALL_DIRS[1:-1]
OUTER_DIRS = (0, HALF_DIRS - 1)


def is_sent(d):
    return d < SIDE_DIRS or d >= HALF_DIRS - SIDE_DIRS


def slab_index(dirs, count, base=0):
    return {d: base + count * n for n, d in enumerate(d for d in dirs if is_sent(d))}


def advect_kernel(
    group, passes, carries, waits, has_raw,
    sea_ref, slope_ref, spec_ref, lead_ref, trail_ref, lat_ref, steep_ref, *rest,
):
    sums = any(summed for *_, summed in passes)
    raw_ref = rest[0] if has_raw else None
    rest = rest[has_raw + waits :]
    held, turn, sem = rest[-3:]
    send_ref, keep_ref = rest[:2]
    if sums:
        steep_out_ref = rest[-4]
    copies, base = [], 0
    for i, (first, count, *_) in enumerate(passes):
        copy = pltpu.make_async_copy(spec_ref.at[:, pl.ds(first, count)], held.at[:, pl.ds(base, count)], sem.at[i])
        copy.start()
        copies.append(copy)
        base += count
    for d in range(HALF_DIRS):
        turn[d] = math.sin(heading(d)) * slope_ref[0] - math.cos(heading(d)) * slope_ref[1]
    if sums:
        steep_out_ref[...] = steep_ref[...]
    for copy in copies:
        copy.wait()
    rows_at = lax.broadcasted_iota(jnp.int32, (8, 256), 0)
    lanes_at = lax.broadcasted_iota(jnp.int32, (8, 256), 1)
    per_cell = TIME_STEP / CELL_SIZE * GRAVITY / 2.0
    bending = TIME_STEP * NDIR / (2.0 * math.pi) * (2.0 * math.pi * LOW_FREQ)
    group_count = group[1] - group[0]

    def body(flipped):
        lead_row, lead_shift = (7, 7) if flipped else (0, 1)
        trail_row, trail_shift = (0, 1) if flipped else (7, 7)
        lat_lane, lat_shift = (255, 255) if flipped else (0, 1)

        def one(first, dirs, slabs, summed, base, f, factors):
            sea = sea_ref[...]
            inverse, weight = factors
            total = jnp.zeros((8, 256), jnp.float32)
            offset = first - group[0]

            def energy(d):
                if d < 0:
                    return raw_ref[1, first + f] * sea
                if d >= HALF_DIRS:
                    return raw_ref[0, first + f] * sea
                return held[d, base + f] * sea

            known = {}
            for d in dirs:
                known = {e: known[e] if e in known else energy(e) for e in (d - 1, d, d + 1)}
                prev, here, after = known[d - 1], known[d], known[d + 1]
                rate = turn[d]
                size = jnp.abs(rate) * bending
                moved = size * jnp.where(rate > 0.0, prev, after)
                along_x = per_cell * abs(math.cos(heading(d)))
                along_y = per_cell * abs(math.sin(heading(d)))
                fixed = 0.0
                if d != LEAD_DIRS:
                    if d < LEAD_DIRS:
                        row = lead_ref[pl.ds(d * group_count + offset + f, 1), :]
                        edge, shift = lead_row, lead_shift
                    else:
                        row = trail_ref[pl.ds((d - LEAD_DIRS - 1) * group_count + offset + f, 1), :]
                        edge, shift = trail_row, trail_shift
                    side = jnp.where(rows_at == edge, jnp.broadcast_to(row, (8, 256)), pltpu.roll(here, shift, 0))
                    moved = moved + along_x * side
                    fixed += along_x
                if d != 0:
                    halo = pltpu.roll(lat_ref[d], lax.rem((lat_lane % 128) + 128 - (offset + f), 128), 1)
                    halo = jnp.concatenate([halo, halo], axis=1)
                    side = jnp.where(lanes_at == lat_lane, halo, pltpu.roll(here, lat_shift, 1))
                    moved = moved + along_y * side
                    fixed += along_y
                result = (here - inverse * ((size + fixed) * here - moved)) * sea
                if slabs is not None and is_sent(d):
                    send_ref[slabs[d] + f] = result
                elif slabs is not None:
                    keep_ref[d - SIDE_DIRS, f] = result
                total = total + result
            if summed:
                steep_out_ref[...] += weight * total
            return inverse * (1.0 / FREQ_STEP), weight * FREQ_STEP**2

        base = 0
        for first, count, dirs, slabs, summed in passes:
            factors = jnp.float32(1.0 / frequency(first)), jnp.float32((frequency(first) / frequency(NFREQ - 1)) ** 2)
            lax.fori_loop(0, count, functools.partial(one, first, dirs, slabs, summed, base), factors)
            base += count

    half = lax.axis_index("comp")

    @pl.when(half == 0)
    def _():
        body(False)

    @pl.when(half != 0)
    def _():
        body(True)

    if carries:
        send_ref[send_ref.shape[0] - 1] = steep_out_ref[...]


def advect_chunk(passes, group, carries, sea, slopes, spec, sides, steep, raw, after):
    vmem = pl.BlockSpec(memory_space=pltpu.VMEM)
    hold = pl.BlockSpec(memory_space=pl.ANY)
    slabs = sum(count * len(place) for _, count, _, place, _ in passes if place is not None)
    raw = () if raw is None else (raw,)
    out_shape = [
        jax.ShapeDtypeStruct((slabs + carries, 8, 256), jnp.float32),
        jax.ShapeDtypeStruct((HALF_DIRS - 2 * SIDE_DIRS, passes[0][1], 8, 256), jnp.float32),
    ]
    if any(summed for *_, summed in passes):
        out_shape.append(jax.ShapeDtypeStruct((8, 256), jnp.float32))
    return pl.pallas_call(
        functools.partial(advect_kernel, group, passes, carries, len(after), len(raw)),
        out_shape=out_shape,
        in_specs=[vmem, vmem, hold, vmem, vmem, vmem, vmem] + [vmem] * len(raw) + [hold] * len(after),
        out_specs=[vmem] * len(out_shape),
        scratch_shapes=[
            pltpu.VMEM((HALF_DIRS, sum(p[1] for p in passes), 8, 256), jnp.float32),
            pltpu.VMEM((HALF_DIRS, 8, 256), jnp.float32),
            pltpu.SemaphoreType.DMA((len(passes),)),
        ],
        compiler_params=pltpu.CompilerParams(vmem_limit_bytes=VMEM_BYTES),
        cost_estimate=SMALL_COST,
    )(sea, slopes, spec, *sides, steep, *raw, *after)


def source_kernel(
    first, count, inner, outer, chained, last,
    wind_ref, steep_a_ref, steep_b_ref, cum_ref, own_ref, keep_ref, other_ref, *rest,
):
    edge_own_ref, edge_other_ref = rest[:2] if outer else (None, None)
    out_ref, cum_out_ref, result, align, sems = rest[(2 if outer else 0) + chained :]
    weights = [math.cos(heading(m)) ** 2 / (9.0 * SATURATION_LEVEL) for m in range(SIDE_DIRS + 1)]
    steep = (steep_a_ref[...] + steep_b_ref[...]) * (1.0 / (NDIR * NFREQ))
    steep_sq = steep * steep
    for d in range(HALF_DIRS):
        align[d] = math.cos(heading(d)) * wind_ref[0] + math.sin(heading(d)) * wind_ref[1]
    cum_out_ref[...] = cum_ref[...]

    def leave(f):
        return pltpu.make_async_copy(result.at[:, f], out_ref.at[:, first + f], sems.at[f])

    def one(f, omega):
        gain = TIME_STEP * WIND_GROWTH * omega
        loss_sat = TIME_STEP * SATURATION_LOSS * omega
        loss_cum = TIME_STEP * CUMULATIVE_LOSS / NFREQ * omega
        loss_steep = TIME_STEP * STEEPNESS_LOSS * omega
        for half in range(2):
            lanes = slice(128 * half, 128 * half + 128)

            def slab(d, main, edge):
                return main[inner[d] + f, :, lanes] if d in inner else edge[outer[d] + f, :, lanes]

            first_dirs, last_dirs = ALL_DIRS[:SIDE_DIRS], ALL_DIRS[-SIDE_DIRS:]
            line = [slab(d, other_ref, edge_other_ref) for d in last_dirs]
            line += [slab(d, own_ref, edge_own_ref) for d in first_dirs]
            line += [keep_ref[i, f, :, lanes] for i in range(HALF_DIRS - 2 * SIDE_DIRS)]
            line += [slab(d, own_ref, edge_own_ref) for d in last_dirs]
            line += [slab(d, other_ref, edge_other_ref) for d in first_dirs]
            base = 1.0 + loss_steep * steep_sq[:, lanes]
            for d in range(HALF_DIRS):
                at = d + SIDE_DIRS
                level = weights[0] * line[at] - 1.0
                for m in range(1, SIDE_DIRS + 1):
                    level = level + weights[m] * (line[at - m] + line[at + m])
                excess = jnp.maximum(level, 0.0)
                square = excess * excess
                cum = cum_out_ref[d, :, lanes]
                cum_out_ref[d, :, lanes] = cum + square
                grown = 1.0 + gain * jnp.maximum(align[d, :, lanes] * omega - 1.0, 0.0)
                lost = base + loss_sat * square + loss_cum * cum
                result[d, f, :, lanes] = line[at] * grown / lost
        leave(f).start()
        return omega * FREQ_STEP

    lax.fori_loop(0, count, one, jnp.float32(frequency(first)))
    for f in range(count):
        leave(f).wait()


def source_chunk(first, count, inner, outer, last, wind, steep_own, steep_other, cum, own, keep, other, edges, out):
    vmem = pl.BlockSpec(memory_space=pltpu.VMEM)
    hold = pl.BlockSpec(memory_space=pl.ANY)
    chained = out is not None
    operands = (wind, steep_own, steep_other, cum, own, keep, other, *edges) + ((out,) if chained else ())
    out_shape = [jax.ShapeDtypeStruct((HALF_DIRS, NFREQ, 8, 256), jnp.float32)]
    running = [] if last else [jax.ShapeDtypeStruct((HALF_DIRS, 8, 256), jnp.float32)]
    result = pl.pallas_call(
        functools.partial(source_kernel, first, count, inner, outer, chained, last),
        out_shape=out_shape + running,
        in_specs=[vmem] * (7 + len(edges)) + [hold] * chained,
        out_specs=[hold] + [vmem] * len(running),
        scratch_shapes=[pltpu.VMEM((HALF_DIRS, 8, 256), jnp.float32)] * last
        + [
            pltpu.VMEM((HALF_DIRS, count, 8, 256), jnp.float32),
            pltpu.VMEM((HALF_DIRS, 8, 256), jnp.float32),
            pltpu.SemaphoreType.DMA((count,)),
        ],
        input_output_aliases={len(operands) - 1: 0} if chained else {},
        compiler_params=pltpu.CompilerParams(vmem_limit_bytes=VMEM_BYTES),
        cost_estimate=SMALL_COST,
    )(*operands)
    return result[0], None if last else result[1]


def ring_pairs(size, step, wrap):
    return [(i, (i + step) % size) for i in range(size) if wrap or 0 <= i + step < size]


def paired_shards(spectrum, sea_mask, owner_list, owner_count, slopes, friction, wind_angle):
    tiles_x, tiles_y = lax.axis_size("tx"), lax.axis_size("ty")
    half = lax.axis_index("comp")
    sign = 1.0 - 2.0 * half.astype(jnp.float32)
    spec = spectrum.reshape(HALF_DIRS, NFREQ, 8, 256)
    sea = sea_mask.astype(jnp.float32)
    turn = slopes * sign
    wind = (sign * WIND_FACTOR / GRAVITY) * friction * jnp.stack([jnp.cos(wind_angle), jnp.sin(wind_angle)])

    def joined(axis_size, step, wrap):
        ahead = ring_pairs(axis_size, step, wrap)
        back = ring_pairs(axis_size, -step, wrap)
        return ahead + [(axis_size + i, axis_size + j) for i, j in back]

    swap = [(0, 1), (1, 0)]
    lead_pairs = joined(tiles_x, 1, True)
    trail_pairs = joined(tiles_x, -1, True)
    lat_pairs = joined(tiles_y, 1, False)

    spec = pltpu.with_memory_space_constraint(spec, pltpu.HBM)
    bounds = chunk_bounds()
    raw = raw_edges(spec)

    def halo(g, after):
        begin, end = HALO_GROUPS[g]
        lead, trail, lat = pack(begin, end - begin, sea, spec, after)
        sides = (
            lax.ppermute(lead, ("comp", "tx"), lead_pairs),
            lax.ppermute(trail, ("comp", "tx"), trail_pairs),
            lax.ppermute(lat, ("comp", "ty"), lat_pairs),
        )
        return sides, lead

    first_sides, _ = halo(0, raw)
    raw = lax.ppermute(raw, "comp", swap)
    early = sum(end <= HALO_GROUPS[0][1] for _, end in bounds)
    counts = [end - begin for begin, end in bounds]
    places = [slab_index(INNER_DIRS if i == 0 else ALL_DIRS, counts[i]) for i in range(len(bounds))]
    edge_place = slab_index(OUTER_DIRS, counts[0], base=2 * SIDE_DIRS * counts[1])

    def advect(passes, sides, carries, steep, raw, after):
        group = HALO_GROUPS[0] if sides is first_sides else HALO_GROUPS[1]
        return advect_chunk(passes, group, carries, sea, turn, spec, sides, steep, raw, after)

    sent, kept, received, sums = [], [], [], []

    def send(result):
        sent.append(result[0])
        kept.append(result[1])
        received.append(lax.ppermute(result[0], "comp", swap))

    def source(upto):
        for j in range(len(sums), upto):
            outer, edges = (edge_place, (sent[1], received[1])) if j == 0 else (None, ())
            state[:] = source_chunk(
                bounds[j][0], counts[j], places[j], outer, j == len(bounds) - 1, wind, steep, steep_other,
                state[1], sent[j], kept[j], received[j], edges, state[0],
            )
            sums.append(state[1])

    steep = jnp.zeros((8, 256), jnp.float32)
    for i in range(early):
        passes = [(bounds[i][0], counts[i], INNER_DIRS if i == 0 else ALL_DIRS, places[i], True)]
        after = ()
        if i == 1:
            passes.append((bounds[0][0], counts[0], OUTER_DIRS, edge_place, True))
        if i >= 2:
            after = (received[i - 2], packed)
        result = advect(passes, first_sides, False, steep, raw if i else None, after)
        send(result)
        steep = result[2]
        if i == 1:
            later_sides, packed = halo(1, steep)
    state = [None, jnp.zeros((HALF_DIRS, 8, 256), jnp.float32)]
    summing = SUM_CHUNKS
    ahead = bounds[early + summing][0]
    cuts = [ahead + (NFREQ - ahead) * n // summing for n in range(summing + 1)]
    for i in range(early, len(bounds)):
        after = (received[i - 2],)
        if i in SOURCES_DONE:
            source(SOURCES_DONE[i])
            after += (sums[-1],)
        n = i - early
        passes = [(bounds[i][0], counts[i], ALL_DIRS, places[i], n < summing)]
        if n < summing:
            passes.append((cuts[n], cuts[n + 1] - cuts[n], ALL_DIRS, None, True))
        result = advect(passes, later_sides, n == summing - 1, steep, raw, after)
        send(result)
        if n < summing:
            steep = result[2]
        if n == summing - 1:
            steep_other = received[i][-1]
    source(len(bounds))
    out = state[0]
    return out.reshape(spectrum.shape)


def fits_pairs(mesh, spectrum):
    return (
        mesh.shape["comp"] == 2
        and spectrum.shape[0] == NDIR * NFREQ
        and spectrum.shape[1] == 8 * mesh.shape["tx"]
        and spectrum.shape[2] == 256 * mesh.shape["ty"]
    )


def solution(mesh):
    in_specs = (
        P("comp", "tx", "ty"),
        P("tx", "ty"),
        P("tx", "ty", None, None),
        P("tx", "ty", None),
        P(None, "tx", "ty"),
        P("tx", "ty"),
        P("tx", "ty"),
    )
    out_specs = P("comp", "tx", "ty")

    def step(spectrum, *others):
        body = paired_shards if fits_pairs(mesh, spectrum) else shards
        mapped = jax.shard_map(body, mesh=mesh, in_specs=in_specs, out_specs=out_specs, check_vma=False)
        return mapped(spectrum, *others)

    return step
```

```python
import functools
import math

import jax
import jax.numpy as jnp
from jax import lax
from jax.experimental import pallas as pl
from jax.experimental.pallas import tpu as pltpu
from jax.sharding import PartitionSpec as P

NDIR = 36
NFREQ = 50


TIME_STEP = 240.0
CELL_SIZE = 11100.0
GRAVITY = 9.81
LOW_FREQ = 0.0373
HIGH_FREQ = 1.0
WIND_GROWTH = 0.0001
WIND_FACTOR = 28.0
SATURATION_LOSS = 0.0005
CUMULATIVE_LOSS = 0.001
STEEPNESS_LOSS = 0.005
SATURATION_LEVEL = 0.6


def padded(value, sides, width, wrap):
    for axis, dim in sides:
        size, length = (lax.axis_size(axis), value.shape[dim])
        up = [(i, (i + 1) % size) for i in range(size if wrap else size - 1)]
        down = [(j, i) for i, j in up]
        last = lax.slice_in_dim(value, length - width, length, axis=dim)
        first = lax.slice_in_dim(value, 0, width, axis=dim)
        before = lax.ppermute(last, axis, up)
        after = lax.ppermute(first, axis, down)
        value = jnp.concatenate([before, value, after], axis=dim)
    return value


def freq_values(freq_ids):
    return (
        2.0
        * math.pi
        * LOW_FREQ
        * jnp.exp(freq_ids.astype(jnp.float32) * (math.log(HIGH_FREQ / LOW_FREQ) / (NFREQ - 1)))
    )


def wave_tables(first_comp, comp_count):
    comp_ids = first_comp + jnp.arange(comp_count, dtype=jnp.int32)
    headings = (comp_ids // NFREQ).astype(jnp.float32) * (2.0 * math.pi / NDIR)
    return (headings, freq_values(comp_ids % NFREQ))


def advect(
    energy,
    west_side,
    east_side,
    south_side,
    north_side,
    prev_dir,
    next_dir,
    headings,
    ang_freq,
    slopes,
):
    group_speed = GRAVITY / (2.0 * ang_freq)
    along_x = (TIME_STEP / CELL_SIZE * group_speed * jnp.cos(headings))[:, None, None]
    along_y = (TIME_STEP / CELL_SIZE * group_speed * jnp.sin(headings))[:, None, None]
    bending = TIME_STEP * NDIR / (2.0 * math.pi) * (2.0 * math.pi * LOW_FREQ) / ang_freq
    turning = bending[:, None, None] * (
        jnp.sin(headings)[:, None, None] * slopes[0][None]
        - jnp.cos(headings)[:, None, None] * slopes[1][None]
    )
    change = jnp.maximum(along_x, 0.0) * (energy - west_side) + jnp.minimum(along_x, 0.0) * (
        east_side - energy
    )
    change = (
        change
        + jnp.maximum(along_y, 0.0) * (energy - south_side)
        + jnp.minimum(along_y, 0.0) * (north_side - energy)
    )
    change = (
        change
        + jnp.maximum(turning, 0.0) * (energy - prev_dir)
        + jnp.minimum(turning, 0.0) * (next_dir - energy)
    )
    return energy - change


def source_terms(spectra, friction, wind_angle):
    dir_ids = jnp.arange(NDIR, dtype=jnp.int32)
    offset = (dir_ids[:, None] - dir_ids[None, :]) % NDIR
    nearest = jnp.minimum(offset, NDIR - offset)
    spread = jnp.where(
        4 * nearest < NDIR, jnp.cos(offset.astype(jnp.float32) * (2.0 * math.pi / NDIR)) ** 2, 0.0
    )
    spread = spread / jnp.sum(spread, axis=1, keepdims=True)
    sat_level = jnp.einsum("de,efp->dfp", spread, spectra, precision=lax.Precision.HIGHEST)
    excess = jnp.maximum(sat_level / SATURATION_LEVEL - 1.0, 0.0)
    excess_sq = excess * excess
    freq_ids = jnp.arange(NFREQ, dtype=jnp.int32)
    below_mask = (freq_ids[None, :] < freq_ids[:, None]).astype(jnp.float32)
    running = (
        jnp.einsum("fg,dgp->dfp", below_mask, excess_sq, precision=lax.Precision.HIGHEST) / NFREQ
    )
    ang_freq = freq_values(freq_ids)
    weights = (ang_freq / ang_freq[NFREQ - 1]) ** 2
    steepness = jnp.einsum("dfp,f->p", spectra, weights, precision=lax.Precision.HIGHEST) / (
        NDIR * NFREQ
    )
    headings = dir_ids.astype(jnp.float32) * (2.0 * math.pi / NDIR)
    alignment = (
        jnp.cos(headings)[:, None, None] * jnp.cos(wind_angle)[None, None, :]
        + jnp.sin(headings)[:, None, None] * jnp.sin(wind_angle)[None, None, :]
    )
    forcing = WIND_FACTOR / GRAVITY * friction[None, None, :] * ang_freq[None, :, None] * alignment
    growth = WIND_GROWTH * ang_freq[None, :, None] * jnp.maximum(forcing - 1.0, 0.0)
    losses = ang_freq[None, :, None] * (
        SATURATION_LOSS * excess_sq
        + CUMULATIVE_LOSS * running
        + STEEPNESS_LOSS * (steepness * steepness)[None, None, :]
    )
    return spectra * (1.0 + TIME_STEP * growth) / (1.0 + TIME_STEP * losses)


def shards(spectrum, sea_mask, owner_list, owner_count, slopes, friction, wind_angle):
    comp_size = lax.axis_size("comp")
    local_comps = spectrum.shape[0]
    cell_count = spectrum.shape[1] * spectrum.shape[2]
    sea_cells = sea_mask.astype(jnp.float32)
    masked = spectrum * sea_cells[None]
    headings, ang_freq = wave_tables(lax.axis_index("comp") * local_comps, local_comps)
    padded_lon = padded(masked, (("tx", 1),), 1, True)
    padded_lat = padded(masked, (("ty", 2),), 1, False)
    padded_dir = padded(masked, (("comp", 0),), NFREQ, True)
    advected = (
        advect(
            masked,
            padded_lon[:, :-2],
            padded_lon[:, 2:],
            padded_lat[:, :, :-2],
            padded_lat[:, :, 2:],
            padded_dir[:local_comps],
            padded_dir[2 * NFREQ :],
            headings,
            ang_freq,
            slopes,
        )
        * sea_cells[None]
    )
    moved_flat = advected.reshape(local_comps, cell_count)
    cell_names = owner_list[0, 0]
    slot_ids = jnp.arange(cell_names.shape[1], dtype=jnp.int32)
    in_use = slot_ids[None, :] < owner_count[0, 0][:, None]
    target = jnp.where(in_use, cell_names, cell_count).reshape(-1)
    owners = cell_names.shape[0]
    capacity = cell_names.shape[1]
    tiles_x = lax.axis_size("tx")
    cell_ids = jnp.arange(cell_count, dtype=jnp.int32)
    selector = (cell_ids[:, None] == target[None, :]).astype(jnp.float32)
    outgoing = jnp.dot(moved_flat, selector, precision=lax.Precision.HIGHEST).reshape(
        local_comps, owners, capacity
    )
    wind_rows = jnp.stack([friction.reshape(-1), wind_angle.reshape(-1)])
    point_data = jnp.dot(wind_rows, selector, precision=lax.Precision.HIGHEST).reshape(
        2, owners, capacity
    )
    spectra = lax.all_to_all(outgoing, ("comp", "tx"), split_axis=1, concat_axis=1, tiled=True)
    extras = lax.all_to_all(point_data, ("comp", "tx"), split_axis=1, concat_axis=1, tiled=True)
    batch_size = spectra.shape[2]
    full_spec = (
        spectra.reshape(local_comps, comp_size, tiles_x * batch_size)
        .transpose(1, 0, 2)
        .reshape(NDIR, NFREQ, tiles_x * batch_size)
    )
    extra_rows = extras.reshape(2, comp_size, tiles_x * batch_size)[:, 0]
    result = source_terms(full_spec, extra_rows[0], extra_rows[1])
    homeward = (
        result.reshape(comp_size, local_comps, tiles_x * batch_size)
        .transpose(1, 0, 2)
        .reshape(local_comps, comp_size * tiles_x, batch_size)
    )
    returned = lax.all_to_all(homeward, ("comp", "tx"), split_axis=1, concat_axis=1, tiled=True)
    gathered = lax.dot_general(
        returned.reshape(local_comps, owners * capacity),
        selector,
        (((1,), (1,)), ((), ())),
        precision=lax.Precision.HIGHEST,
    )
    listed = jnp.sum(selector, axis=1) > 0.5
    updated = jnp.where(listed[None], gathered, moved_flat)
    return updated.reshape(spectrum.shape)


def chunk_bounds():
    return [(5 * i, 5 * i + 5) for i in range(9)] + [(45, 47), (47, 49), (49, 50)]


HALO_GROUPS = ((0, 15), (15, 50))
SUM_CHUNKS = 3
SOURCES_DONE = {8: 2, 9: 5, 10: 7, 11: 9}
HALF_DIRS = NDIR // 2
SIDE_DIRS = 8
LEAD_DIRS = 9
VMEM_BYTES = 24 * 1024 * 1024
SMALL_COST = pl.CostEstimate(flops=1024, bytes_accessed=1024, transcendentals=0)


FREQ_STEP = (HIGH_FREQ / LOW_FREQ) ** (1.0 / (NFREQ - 1))


def frequency(index):
    return 2.0 * math.pi * LOW_FREQ * FREQ_STEP**index


def heading(index):
    return 2.0 * math.pi * index / NDIR


def pack_kernel(first, count, sea_ref, spec_ref, after_ref, lead_ref, trail_ref, lat_ref, held, sems):
    def body(flipped):
        lead_row, trail_row = (0, 7) if flipped else (7, 0)
        part = 0 if flipped else 1
        copies = []
        for d in range(HALF_DIRS):
            for h in range(2):
                place = h * HALF_DIRS + d
                copy = pltpu.make_async_copy(
                    spec_ref.at[pl.ds((d * NFREQ + first) * 8, count * 8), pl.ds(128 * h, 128)],
                    held.at[pl.ds(place * count * 8, count * 8)],
                    sems.at[place],
                )
                copy.start()
                copies.append(copy)
        for d in range(HALF_DIRS):
            for h in range(2):
                copies[2 * d + h].wait()
                lanes_here = slice(128 * h, 128 * h + 128)
                start = (h * HALF_DIRS + d) * count * 8
                if d < LEAD_DIRS:
                    column = held[pl.ds(start + lead_row, count, stride=8), :]
                    lead_ref[d * count : (d + 1) * count, lanes_here] = column * sea_ref[lead_row : lead_row + 1, lanes_here]
                elif d > LEAD_DIRS:
                    t = d - LEAD_DIRS - 1
                    column = held[pl.ds(start + trail_row, count, stride=8), :]
                    trail_ref[t * count : (t + 1) * count, lanes_here] = column * sea_ref[trail_row : trail_row + 1, lanes_here]
        lane = 0 if flipped else 127
        lanes = lax.broadcasted_iota(jnp.int32, (8, 128), 1)
        sea_line = jnp.broadcast_to(sea_ref[:, 128 * part + lane : 128 * part + lane + 1], (8, 128))

        def slab(d, f):
            return held[pl.ds(pl.multiple_of((part * HALF_DIRS + d) * count * 8 + f * 8, 8), 8), :]

        def one(f, kept):
            here = lanes == f
            return tuple(
                jnp.where(here, jnp.broadcast_to(slab(d, f)[:, lane : lane + 1], (8, 128)), kept[d])
                for d in range(HALF_DIRS)
            )

        zeros = jnp.zeros((8, 128), jnp.float32)
        kept = lax.fori_loop(0, count, one, (zeros,) * HALF_DIRS, unroll=5)
        for d in range(HALF_DIRS):
            lat_ref[d] = kept[d] * sea_line

    half = lax.axis_index("comp")

    @pl.when(half == 0)
    def _():
        body(False)

    @pl.when(half != 0)
    def _():
        body(True)


def pack(first, count, sea, spec, after):
    vmem = pl.BlockSpec(memory_space=pltpu.VMEM)
    hold = pl.BlockSpec(memory_space=pl.ANY)
    return pl.pallas_call(
        functools.partial(pack_kernel, first, count),
        out_shape=[
            jax.ShapeDtypeStruct((LEAD_DIRS * count, 256), jnp.float32),
            jax.ShapeDtypeStruct(((HALF_DIRS - LEAD_DIRS - 1) * count, 256), jnp.float32),
            jax.ShapeDtypeStruct((HALF_DIRS, 8, 128), jnp.float32),
        ],
        in_specs=[vmem, hold, hold],
        out_specs=[vmem] * 3,
        scratch_shapes=[
            pltpu.VMEM(((2 * HALF_DIRS + 1) * count * 8, 128), jnp.float32),
            pltpu.SemaphoreType.DMA((2 * HALF_DIRS,)),
        ],
        compiler_params=pltpu.CompilerParams(vmem_limit_bytes=VMEM_BYTES),
        cost_estimate=SMALL_COST,
    )(sea, spec, after)


ALL_DIRS = tuple(range(HALF_DIRS))
INNER_DIRS = ALL_DIRS[1:-1]
OUTER_DIRS = (0, HALF_DIRS - 1)


def is_sent(d):
    return d < SIDE_DIRS or d >= HALF_DIRS - SIDE_DIRS


def slab_index(dirs, count, base=0):
    return {d: base + count * n for n, d in enumerate(d for d in dirs if is_sent(d))}


def advect_kernel(
    group, passes, carries, waits, has_raw,
    sea_ref, slope_ref, spec_ref, lead_ref, trail_ref, lat_ref, steep_ref, *rest,
):
    sums = any(summed for *_, summed in passes)
    raw_refs = rest[:has_raw]
    rest = rest[has_raw + waits :]
    held, turn, sem = rest[-3:]
    send_ref, keep_ref = rest[:2]
    if sums:
        steep_out_ref = rest[-4]
    copies, base = [], 0
    for i, (first, count, *_) in enumerate(passes):
        copy = pltpu.make_async_copy(spec_ref.at[:, pl.ds(first, count)], held.at[:, pl.ds(base, count)], sem.at[i])
        copy.start()
        copies.append(copy)
        base += count
    for d in range(HALF_DIRS):
        turn[d] = math.sin(heading(d)) * slope_ref[0] - math.cos(heading(d)) * slope_ref[1]
    if sums:
        steep_out_ref[...] = steep_ref[...]
    for copy in copies:
        copy.wait()
    rows_at = lax.broadcasted_iota(jnp.int32, (8, 256), 0)
    lanes_at = lax.broadcasted_iota(jnp.int32, (8, 256), 1)
    per_cell = TIME_STEP / CELL_SIZE * GRAVITY / 2.0
    bending = TIME_STEP * NDIR / (2.0 * math.pi) * (2.0 * math.pi * LOW_FREQ)
    group_count = group[1] - group[0]

    def body(flipped):
        lead_row, lead_shift = (7, 7) if flipped else (0, 1)
        trail_row, trail_shift = (0, 1) if flipped else (7, 7)
        lat_lane, lat_shift = (255, 255) if flipped else (0, 1)

        def one(first, dirs, slabs, summed, base, f, factors):
            sea = sea_ref[...]
            inverse, weight = factors
            total = jnp.zeros((8, 256), jnp.float32)
            offset = first - group[0]

            def energy(d):
                if d < 0:
                    return raw_refs[1][first + f] * sea
                if d >= HALF_DIRS:
                    return raw_refs[0][first + f] * sea
                return held[d, base + f] * sea

            known = {}
            for d in dirs:
                known = {e: known[e] if e in known else energy(e) for e in (d - 1, d, d + 1)}
                prev, here, after = known[d - 1], known[d], known[d + 1]
                rate = turn[d]
                size = jnp.abs(rate) * bending
                moved = size * jnp.where(rate > 0.0, prev, after)
                along_x = per_cell * abs(math.cos(heading(d)))
                along_y = per_cell * abs(math.sin(heading(d)))
                fixed = 0.0
                if d != LEAD_DIRS:
                    if d < LEAD_DIRS:
                        row = lead_ref[pl.ds(d * group_count + offset + f, 1), :]
                        edge, shift = lead_row, lead_shift
                    else:
                        row = trail_ref[pl.ds((d - LEAD_DIRS - 1) * group_count + offset + f, 1), :]
                        edge, shift = trail_row, trail_shift
                    side = jnp.where(rows_at == edge, jnp.broadcast_to(row, (8, 256)), pltpu.roll(here, shift, 0))
                    moved = moved + along_x * side
                    fixed += along_x
                if d != 0:
                    halo = pltpu.roll(lat_ref[d], lax.rem((lat_lane % 128) + 128 - (offset + f), 128), 1)
                    halo = jnp.concatenate([halo, halo], axis=1)
                    side = jnp.where(lanes_at == lat_lane, halo, pltpu.roll(here, lat_shift, 1))
                    moved = moved + along_y * side
                    fixed += along_y
                result = (here - inverse * ((size + fixed) * here - moved)) * sea
                if slabs is not None and is_sent(d):
                    send_ref[slabs[d] + f] = result
                elif slabs is not None:
                    keep_ref[d - SIDE_DIRS, f] = result
                total = total + result
            if summed:
                steep_out_ref[...] += weight * total
            return inverse * (1.0 / FREQ_STEP), weight * FREQ_STEP**2

        base = 0
        for first, count, dirs, slabs, summed in passes:
            factors = jnp.float32(1.0 / frequency(first)), jnp.float32((frequency(first) / frequency(NFREQ - 1)) ** 2)
            lax.fori_loop(0, count, functools.partial(one, first, dirs, slabs, summed, base), factors)
            base += count

    half = lax.axis_index("comp")

    @pl.when(half == 0)
    def _():
        body(False)

    @pl.when(half != 0)
    def _():
        body(True)

    if carries:
        send_ref[send_ref.shape[0] - 1] = steep_out_ref[...]


def advect_chunk(passes, group, carries, sea, slopes, spec, sides, steep, raw, after):
    vmem = pl.BlockSpec(memory_space=pltpu.VMEM)
    hold = pl.BlockSpec(memory_space=pl.ANY)
    slabs = sum(count * len(place) for _, count, _, place, _ in passes if place is not None)
    out_shape = [
        jax.ShapeDtypeStruct((slabs + carries, 8, 256), jnp.float32),
        jax.ShapeDtypeStruct((HALF_DIRS - 2 * SIDE_DIRS, passes[0][1], 8, 256), jnp.float32),
    ]
    if any(summed for *_, summed in passes):
        out_shape.append(jax.ShapeDtypeStruct((8, 256), jnp.float32))
    return pl.pallas_call(
        functools.partial(advect_kernel, group, passes, carries, len(after), len(raw)),
        out_shape=out_shape,
        in_specs=[vmem, vmem, hold, vmem, vmem, vmem, vmem] + [vmem] * len(raw) + [hold] * len(after),
        out_specs=[vmem] * len(out_shape),
        scratch_shapes=[
            pltpu.VMEM((HALF_DIRS, sum(p[1] for p in passes), 8, 256), jnp.float32),
            pltpu.VMEM((HALF_DIRS, 8, 256), jnp.float32),
            pltpu.SemaphoreType.DMA((len(passes),)),
        ],
        compiler_params=pltpu.CompilerParams(vmem_limit_bytes=VMEM_BYTES),
        cost_estimate=SMALL_COST,
    )(sea, slopes, spec, *sides, steep, *raw, *after)


def source_kernel(
    first, count, inner, outer, chained, last,
    wind_ref, steep_a_ref, steep_b_ref, cum_ref, own_ref, keep_ref, other_ref, *rest,
):
    edge_own_ref, edge_other_ref = rest[:2] if outer else (None, None)
    out_ref, cum_out_ref, result, align, sems = rest[(2 if outer else 0) + chained :]
    weights = [math.cos(heading(m)) ** 2 / (9.0 * SATURATION_LEVEL) for m in range(SIDE_DIRS + 1)]
    steep = (steep_a_ref[...] + steep_b_ref[...]) * (1.0 / (NDIR * NFREQ))
    steep_sq = steep * steep
    for d in range(HALF_DIRS):
        align[d] = math.cos(heading(d)) * wind_ref[0] + math.sin(heading(d)) * wind_ref[1]
    cum_out_ref[...] = cum_ref[...]

    def leave(f):
        return pltpu.make_async_copy(result.at[:, f], out_ref.at[:, first + f], sems.at[f])

    def one(f, omega):
        gain = TIME_STEP * WIND_GROWTH * omega
        loss_sat = TIME_STEP * SATURATION_LOSS * omega
        loss_cum = TIME_STEP * CUMULATIVE_LOSS / NFREQ * omega
        loss_steep = TIME_STEP * STEEPNESS_LOSS * omega
        for half in range(2):
            lanes = slice(128 * half, 128 * half + 128)

            def slab(d, main, edge):
                return main[inner[d] + f, :, lanes] if d in inner else edge[outer[d] + f, :, lanes]

            first_dirs, last_dirs = ALL_DIRS[:SIDE_DIRS], ALL_DIRS[-SIDE_DIRS:]
            line = [slab(d, other_ref, edge_other_ref) for d in last_dirs]
            line += [slab(d, own_ref, edge_own_ref) for d in first_dirs]
            line += [keep_ref[i, f, :, lanes] for i in range(HALF_DIRS - 2 * SIDE_DIRS)]
            line += [slab(d, own_ref, edge_own_ref) for d in last_dirs]
            line += [slab(d, other_ref, edge_other_ref) for d in first_dirs]
            base = 1.0 + loss_steep * steep_sq[:, lanes]
            for d in range(HALF_DIRS):
                at = d + SIDE_DIRS
                level = weights[0] * line[at] - 1.0
                for m in range(1, SIDE_DIRS + 1):
                    level = level + weights[m] * (line[at - m] + line[at + m])
                excess = jnp.maximum(level, 0.0)
                square = excess * excess
                cum = cum_out_ref[d, :, lanes]
                cum_out_ref[d, :, lanes] = cum + square
                grown = 1.0 + gain * jnp.maximum(align[d, :, lanes] * omega - 1.0, 0.0)
                lost = base + loss_sat * square + loss_cum * cum
                result[d, f, :, lanes] = line[at] * grown / lost
        leave(f).start()
        return omega * FREQ_STEP

    lax.fori_loop(0, count, one, jnp.float32(frequency(first)))
    for f in range(count):
        leave(f).wait()


def source_chunk(first, count, inner, outer, last, wind, steep_own, steep_other, cum, own, keep, other, edges, out):
    vmem = pl.BlockSpec(memory_space=pltpu.VMEM)
    hold = pl.BlockSpec(memory_space=pl.ANY)
    chained = out is not None
    operands = (wind, steep_own, steep_other, cum, own, keep, other, *edges) + ((out,) if chained else ())
    out_shape = [jax.ShapeDtypeStruct((HALF_DIRS, NFREQ, 8, 256), jnp.float32)]
    running = [] if last else [jax.ShapeDtypeStruct((HALF_DIRS, 8, 256), jnp.float32)]
    result = pl.pallas_call(
        functools.partial(source_kernel, first, count, inner, outer, chained, last),
        out_shape=out_shape + running,
        in_specs=[vmem] * (7 + len(edges)) + [hold] * chained,
        out_specs=[hold] + [vmem] * len(running),
        scratch_shapes=[pltpu.VMEM((HALF_DIRS, 8, 256), jnp.float32)] * last
        + [
            pltpu.VMEM((HALF_DIRS, count, 8, 256), jnp.float32),
            pltpu.VMEM((HALF_DIRS, 8, 256), jnp.float32),
            pltpu.SemaphoreType.DMA((count,)),
        ],
        input_output_aliases={len(operands) - 1: 0} if chained else {},
        compiler_params=pltpu.CompilerParams(vmem_limit_bytes=VMEM_BYTES),
        cost_estimate=SMALL_COST,
    )(*operands)
    return result[0], None if last else result[1]


def ring_pairs(size, step, wrap):
    return [(i, (i + step) % size) for i in range(size) if wrap or 0 <= i + step < size]


def paired_shards(spectrum, sea_mask, owner_list, owner_count, slopes, friction, wind_angle):
    tiles_x, tiles_y = lax.axis_size("tx"), lax.axis_size("ty")
    half = lax.axis_index("comp")
    sign = 1.0 - 2.0 * half.astype(jnp.float32)
    spec = spectrum.reshape(HALF_DIRS, NFREQ, 8, 256)
    sea = sea_mask.astype(jnp.float32)
    turn = slopes * sign
    wind = (sign * WIND_FACTOR / GRAVITY) * friction * jnp.stack([jnp.cos(wind_angle), jnp.sin(wind_angle)])

    def joined(axis_size, step, wrap):
        ahead = ring_pairs(axis_size, step, wrap)
        back = ring_pairs(axis_size, -step, wrap)
        return ahead + [(axis_size + i, axis_size + j) for i, j in back]

    swap = [(0, 1), (1, 0)]
    lead_pairs = joined(tiles_x, 1, True)
    trail_pairs = joined(tiles_x, -1, True)
    lat_pairs = joined(tiles_y, 1, False)

    rows = pltpu.with_memory_space_constraint(spectrum.reshape(HALF_DIRS * NFREQ * 8, 256), pltpu.HBM)
    spec = pltpu.with_memory_space_constraint(spec, pltpu.HBM)
    bounds = chunk_bounds()
    edges = [lax.slice_in_dim(spectrum, d * NFREQ, (d + 1) * NFREQ) for d in OUTER_DIRS]

    def halo(g, after):
        begin, end = HALO_GROUPS[g]
        lead, trail, lat = pack(begin, end - begin, sea, rows, after)
        sides = (
            lax.ppermute(lead, ("comp", "tx"), lead_pairs),
            lax.ppermute(trail, ("comp", "tx"), trail_pairs),
            lax.ppermute(lat, ("comp", "ty"), lat_pairs),
        )
        return sides, lead

    first_sides, _ = halo(0, edges[1])
    raw = tuple(lax.ppermute(edge, "comp", swap) for edge in edges)
    early = sum(end <= HALO_GROUPS[0][1] for _, end in bounds)
    counts = [end - begin for begin, end in bounds]
    places = [slab_index(INNER_DIRS if i == 0 else ALL_DIRS, counts[i]) for i in range(len(bounds))]
    edge_place = slab_index(OUTER_DIRS, counts[0], base=2 * SIDE_DIRS * counts[1])

    def advect(passes, sides, carries, steep, raw, after):
        group = HALO_GROUPS[0] if sides is first_sides else HALO_GROUPS[1]
        return advect_chunk(passes, group, carries, sea, turn, spec, sides, steep, raw, after)

    sent, kept, received, sums = [], [], [], []

    def send(result):
        sent.append(result[0])
        kept.append(result[1])
        received.append(lax.ppermute(result[0], "comp", swap))

    def source(upto):
        for j in range(len(sums), upto):
            outer, edges = (edge_place, (sent[1], received[1])) if j == 0 else (None, ())
            state[:] = source_chunk(
                bounds[j][0], counts[j], places[j], outer, j == len(bounds) - 1, wind, steep, steep_other,
                state[1], sent[j], kept[j], received[j], edges, state[0],
            )
            sums.append(state[1])

    steep = jnp.zeros((8, 256), jnp.float32)
    for i in range(early):
        passes = [(bounds[i][0], counts[i], INNER_DIRS if i == 0 else ALL_DIRS, places[i], True)]
        after = ()
        if i == 1:
            passes.append((bounds[0][0], counts[0], OUTER_DIRS, edge_place, True))
        if i >= 2:
            after = (received[i - 2], packed)
        result = advect(passes, first_sides, False, steep, raw if i else (), after)
        send(result)
        steep = result[2]
        if i == 1:
            later_sides, packed = halo(1, steep)
    state = [None, jnp.zeros((HALF_DIRS, 8, 256), jnp.float32)]
    summing = SUM_CHUNKS
    ahead = bounds[early + summing][0]
    cuts = [ahead + (NFREQ - ahead) * n // summing for n in range(summing + 1)]
    for i in range(early, len(bounds)):
        after = (received[i - 2],)
        if i in SOURCES_DONE:
            source(SOURCES_DONE[i])
            after += (sums[-1],)
        n = i - early
        passes = [(bounds[i][0], counts[i], ALL_DIRS, places[i], n < summing)]
        if n < summing:
            passes.append((cuts[n], cuts[n + 1] - cuts[n], ALL_DIRS, None, True))
        result = advect(passes, later_sides, n == summing - 1, steep, raw, after)
        send(result)
        if n < summing:
            steep = result[2]
        if n == summing - 1:
            steep_other = received[i][-1]
    source(len(bounds))
    out = state[0]
    return out.reshape(spectrum.shape)


def fits_pairs(mesh, spectrum):
    return (
        mesh.shape["comp"] == 2
        and spectrum.shape[0] == NDIR * NFREQ
        and spectrum.shape[1] == 8 * mesh.shape["tx"]
        and spectrum.shape[2] == 256 * mesh.shape["ty"]
    )


def solution(mesh):
    in_specs = (
        P("comp", "tx", "ty"),
        P("tx", "ty"),
        P("tx", "ty", None, None),
        P("tx", "ty", None),
        P(None, "tx", "ty"),
        P("tx", "ty"),
        P("tx", "ty"),
    )
    out_specs = P("comp", "tx", "ty")

    def step(spectrum, *others):
        body = paired_shards if fits_pairs(mesh, spectrum) else shards
        mapped = jax.shard_map(body, mesh=mesh, in_specs=in_specs, out_specs=out_specs, check_vma=False)
        return mapped(spectrum, *others)

    return step
```

```python
import functools
import math

import jax
import jax.numpy as jnp
from jax import lax
from jax.experimental import pallas as pl
from jax.experimental.pallas import tpu as pltpu
from jax.sharding import PartitionSpec as P

NDIR = 36
NFREQ = 50


TIME_STEP = 240.0
CELL_SIZE = 11100.0
GRAVITY = 9.81
LOW_FREQ = 0.0373
HIGH_FREQ = 1.0
WIND_GROWTH = 0.0001
WIND_FACTOR = 28.0
SATURATION_LOSS = 0.0005
CUMULATIVE_LOSS = 0.001
STEEPNESS_LOSS = 0.005
SATURATION_LEVEL = 0.6


def padded(value, sides, width, wrap):
    for axis, dim in sides:
        size, length = (lax.axis_size(axis), value.shape[dim])
        up = [(i, (i + 1) % size) for i in range(size if wrap else size - 1)]
        down = [(j, i) for i, j in up]
        last = lax.slice_in_dim(value, length - width, length, axis=dim)
        first = lax.slice_in_dim(value, 0, width, axis=dim)
        before = lax.ppermute(last, axis, up)
        after = lax.ppermute(first, axis, down)
        value = jnp.concatenate([before, value, after], axis=dim)
    return value


def freq_values(freq_ids):
    return (
        2.0
        * math.pi
        * LOW_FREQ
        * jnp.exp(freq_ids.astype(jnp.float32) * (math.log(HIGH_FREQ / LOW_FREQ) / (NFREQ - 1)))
    )


def wave_tables(first_comp, comp_count):
    comp_ids = first_comp + jnp.arange(comp_count, dtype=jnp.int32)
    headings = (comp_ids // NFREQ).astype(jnp.float32) * (2.0 * math.pi / NDIR)
    return (headings, freq_values(comp_ids % NFREQ))


def advect(
    energy,
    west_side,
    east_side,
    south_side,
    north_side,
    prev_dir,
    next_dir,
    headings,
    ang_freq,
    slopes,
):
    group_speed = GRAVITY / (2.0 * ang_freq)
    along_x = (TIME_STEP / CELL_SIZE * group_speed * jnp.cos(headings))[:, None, None]
    along_y = (TIME_STEP / CELL_SIZE * group_speed * jnp.sin(headings))[:, None, None]
    bending = TIME_STEP * NDIR / (2.0 * math.pi) * (2.0 * math.pi * LOW_FREQ) / ang_freq
    turning = bending[:, None, None] * (
        jnp.sin(headings)[:, None, None] * slopes[0][None]
        - jnp.cos(headings)[:, None, None] * slopes[1][None]
    )
    change = jnp.maximum(along_x, 0.0) * (energy - west_side) + jnp.minimum(along_x, 0.0) * (
        east_side - energy
    )
    change = (
        change
        + jnp.maximum(along_y, 0.0) * (energy - south_side)
        + jnp.minimum(along_y, 0.0) * (north_side - energy)
    )
    change = (
        change
        + jnp.maximum(turning, 0.0) * (energy - prev_dir)
        + jnp.minimum(turning, 0.0) * (next_dir - energy)
    )
    return energy - change


def source_terms(spectra, friction, wind_angle):
    dir_ids = jnp.arange(NDIR, dtype=jnp.int32)
    offset = (dir_ids[:, None] - dir_ids[None, :]) % NDIR
    nearest = jnp.minimum(offset, NDIR - offset)
    spread = jnp.where(
        4 * nearest < NDIR, jnp.cos(offset.astype(jnp.float32) * (2.0 * math.pi / NDIR)) ** 2, 0.0
    )
    spread = spread / jnp.sum(spread, axis=1, keepdims=True)
    sat_level = jnp.einsum("de,efp->dfp", spread, spectra, precision=lax.Precision.HIGHEST)
    excess = jnp.maximum(sat_level / SATURATION_LEVEL - 1.0, 0.0)
    excess_sq = excess * excess
    freq_ids = jnp.arange(NFREQ, dtype=jnp.int32)
    below_mask = (freq_ids[None, :] < freq_ids[:, None]).astype(jnp.float32)
    running = (
        jnp.einsum("fg,dgp->dfp", below_mask, excess_sq, precision=lax.Precision.HIGHEST) / NFREQ
    )
    ang_freq = freq_values(freq_ids)
    weights = (ang_freq / ang_freq[NFREQ - 1]) ** 2
    steepness = jnp.einsum("dfp,f->p", spectra, weights, precision=lax.Precision.HIGHEST) / (
        NDIR * NFREQ
    )
    headings = dir_ids.astype(jnp.float32) * (2.0 * math.pi / NDIR)
    alignment = (
        jnp.cos(headings)[:, None, None] * jnp.cos(wind_angle)[None, None, :]
        + jnp.sin(headings)[:, None, None] * jnp.sin(wind_angle)[None, None, :]
    )
    forcing = WIND_FACTOR / GRAVITY * friction[None, None, :] * ang_freq[None, :, None] * alignment
    growth = WIND_GROWTH * ang_freq[None, :, None] * jnp.maximum(forcing - 1.0, 0.0)
    losses = ang_freq[None, :, None] * (
        SATURATION_LOSS * excess_sq
        + CUMULATIVE_LOSS * running
        + STEEPNESS_LOSS * (steepness * steepness)[None, None, :]
    )
    return spectra * (1.0 + TIME_STEP * growth) / (1.0 + TIME_STEP * losses)


def shards(spectrum, sea_mask, owner_list, owner_count, slopes, friction, wind_angle):
    comp_size = lax.axis_size("comp")
    local_comps = spectrum.shape[0]
    cell_count = spectrum.shape[1] * spectrum.shape[2]
    sea_cells = sea_mask.astype(jnp.float32)
    masked = spectrum * sea_cells[None]
    headings, ang_freq = wave_tables(lax.axis_index("comp") * local_comps, local_comps)
    padded_lon = padded(masked, (("tx", 1),), 1, True)
    padded_lat = padded(masked, (("ty", 2),), 1, False)
    padded_dir = padded(masked, (("comp", 0),), NFREQ, True)
    advected = (
        advect(
            masked,
            padded_lon[:, :-2],
            padded_lon[:, 2:],
            padded_lat[:, :, :-2],
            padded_lat[:, :, 2:],
            padded_dir[:local_comps],
            padded_dir[2 * NFREQ :],
            headings,
            ang_freq,
            slopes,
        )
        * sea_cells[None]
    )
    moved_flat = advected.reshape(local_comps, cell_count)
    cell_names = owner_list[0, 0]
    slot_ids = jnp.arange(cell_names.shape[1], dtype=jnp.int32)
    in_use = slot_ids[None, :] < owner_count[0, 0][:, None]
    target = jnp.where(in_use, cell_names, cell_count).reshape(-1)
    owners = cell_names.shape[0]
    capacity = cell_names.shape[1]
    tiles_x = lax.axis_size("tx")
    cell_ids = jnp.arange(cell_count, dtype=jnp.int32)
    selector = (cell_ids[:, None] == target[None, :]).astype(jnp.float32)
    outgoing = jnp.dot(moved_flat, selector, precision=lax.Precision.HIGHEST).reshape(
        local_comps, owners, capacity
    )
    wind_rows = jnp.stack([friction.reshape(-1), wind_angle.reshape(-1)])
    point_data = jnp.dot(wind_rows, selector, precision=lax.Precision.HIGHEST).reshape(
        2, owners, capacity
    )
    spectra = lax.all_to_all(outgoing, ("comp", "tx"), split_axis=1, concat_axis=1, tiled=True)
    extras = lax.all_to_all(point_data, ("comp", "tx"), split_axis=1, concat_axis=1, tiled=True)
    batch_size = spectra.shape[2]
    full_spec = (
        spectra.reshape(local_comps, comp_size, tiles_x * batch_size)
        .transpose(1, 0, 2)
        .reshape(NDIR, NFREQ, tiles_x * batch_size)
    )
    extra_rows = extras.reshape(2, comp_size, tiles_x * batch_size)[:, 0]
    result = source_terms(full_spec, extra_rows[0], extra_rows[1])
    homeward = (
        result.reshape(comp_size, local_comps, tiles_x * batch_size)
        .transpose(1, 0, 2)
        .reshape(local_comps, comp_size * tiles_x, batch_size)
    )
    returned = lax.all_to_all(homeward, ("comp", "tx"), split_axis=1, concat_axis=1, tiled=True)
    gathered = lax.dot_general(
        returned.reshape(local_comps, owners * capacity),
        selector,
        (((1,), (1,)), ((), ())),
        precision=lax.Precision.HIGHEST,
    )
    listed = jnp.sum(selector, axis=1) > 0.5
    updated = jnp.where(listed[None], gathered, moved_flat)
    return updated.reshape(spectrum.shape)


def chunk_bounds():
    return [(5 * i, 5 * i + 5) for i in range(9)] + [(45, 47), (47, 49), (49, 50)]


HALO_GROUPS = ((0, 15), (15, 50))
SUM_CHUNKS = 3
SOURCES_DONE = {8: 2, 9: 5, 10: 7, 11: 9}
HALF_DIRS = NDIR // 2
SIDE_DIRS = 8
LEAD_DIRS = 9
VMEM_BYTES = 24 * 1024 * 1024
SMALL_COST = pl.CostEstimate(flops=1024, bytes_accessed=1024, transcendentals=0)


FREQ_STEP = (HIGH_FREQ / LOW_FREQ) ** (1.0 / (NFREQ - 1))


def frequency(index):
    return 2.0 * math.pi * LOW_FREQ * FREQ_STEP**index


def heading(index):
    return 2.0 * math.pi * index / NDIR


def raw_kernel(spec_ref, raw_ref, sems):
    copies = []
    for i, d in enumerate((0, HALF_DIRS - 1)):
        copy = pltpu.make_async_copy(spec_ref.at[d], raw_ref.at[i], sems.at[i])
        copy.start()
        copies.append(copy)
    for copy in copies:
        copy.wait()


def raw_edges(spec):
    return pl.pallas_call(
        raw_kernel,
        out_shape=jax.ShapeDtypeStruct((2, NFREQ, 8, 256), jnp.float32),
        in_specs=[pl.BlockSpec(memory_space=pl.ANY)],
        out_specs=pl.BlockSpec(memory_space=pltpu.VMEM),
        scratch_shapes=[pltpu.SemaphoreType.DMA((2,))],
        compiler_params=pltpu.CompilerParams(vmem_limit_bytes=VMEM_BYTES),
        cost_estimate=SMALL_COST,
    )(spec)


def pack_kernel(first, count, sea_ref, spec_ref, after_ref, lead_ref, trail_ref, lat_ref, held, sems):
    def body(flipped):
        lead_row, trail_row = (0, 7) if flipped else (7, 0)
        part = 0 if flipped else 1
        copies = []
        for d in range(HALF_DIRS):
            for h in range(2):
                place = h * HALF_DIRS + d
                copy = pltpu.make_async_copy(
                    spec_ref.at[pl.ds((d * NFREQ + first) * 8, count * 8), pl.ds(128 * h, 128)],
                    held.at[pl.ds(place * count * 8, count * 8)],
                    sems.at[place],
                )
                copy.start()
                copies.append(copy)
        for d in range(HALF_DIRS):
            for h in range(2):
                copies[2 * d + h].wait()
                lanes_here = slice(128 * h, 128 * h + 128)
                start = (h * HALF_DIRS + d) * count * 8
                if d < LEAD_DIRS:
                    column = held[pl.ds(start + lead_row, count, stride=8), :]
                    lead_ref[d * count : (d + 1) * count, lanes_here] = column * sea_ref[lead_row : lead_row + 1, lanes_here]
                elif d > LEAD_DIRS:
                    t = d - LEAD_DIRS - 1
                    column = held[pl.ds(start + trail_row, count, stride=8), :]
                    trail_ref[t * count : (t + 1) * count, lanes_here] = column * sea_ref[trail_row : trail_row + 1, lanes_here]
        lane = 0 if flipped else 127
        lanes = lax.broadcasted_iota(jnp.int32, (8, 128), 1)
        sea_line = jnp.broadcast_to(sea_ref[:, 128 * part + lane : 128 * part + lane + 1], (8, 128))

        def slab(d, f):
            return held[pl.ds(pl.multiple_of((part * HALF_DIRS + d) * count * 8 + f * 8, 8), 8), :]

        def one(f, kept):
            here = lanes == f
            return tuple(
                jnp.where(here, jnp.broadcast_to(slab(d, f)[:, lane : lane + 1], (8, 128)), kept[d])
                for d in range(HALF_DIRS)
            )

        zeros = jnp.zeros((8, 128), jnp.float32)
        kept = lax.fori_loop(0, count, one, (zeros,) * HALF_DIRS, unroll=5)
        for d in range(HALF_DIRS):
            lat_ref[d] = kept[d] * sea_line

    half = lax.axis_index("comp")

    @pl.when(half == 0)
    def _():
        body(False)

    @pl.when(half != 0)
    def _():
        body(True)


def pack(first, count, sea, spec, after):
    vmem = pl.BlockSpec(memory_space=pltpu.VMEM)
    hold = pl.BlockSpec(memory_space=pl.ANY)
    return pl.pallas_call(
        functools.partial(pack_kernel, first, count),
        out_shape=[
            jax.ShapeDtypeStruct((LEAD_DIRS * count, 256), jnp.float32),
            jax.ShapeDtypeStruct(((HALF_DIRS - LEAD_DIRS - 1) * count, 256), jnp.float32),
            jax.ShapeDtypeStruct((HALF_DIRS, 8, 128), jnp.float32),
        ],
        in_specs=[vmem, hold, hold],
        out_specs=[vmem] * 3,
        scratch_shapes=[
            pltpu.VMEM(((2 * HALF_DIRS + 1) * count * 8, 128), jnp.float32),
            pltpu.SemaphoreType.DMA((2 * HALF_DIRS,)),
        ],
        compiler_params=pltpu.CompilerParams(vmem_limit_bytes=VMEM_BYTES),
        cost_estimate=SMALL_COST,
    )(sea, spec, after)


ALL_DIRS = tuple(range(HALF_DIRS))
INNER_DIRS = ALL_DIRS[1:-1]
OUTER_DIRS = (0, HALF_DIRS - 1)


def is_sent(d):
    return d < SIDE_DIRS or d >= HALF_DIRS - SIDE_DIRS


def slab_index(dirs, count, base=0):
    return {d: base + count * n for n, d in enumerate(d for d in dirs if is_sent(d))}


def advect_kernel(
    group, passes, carries, waits, has_raw,
    sea_ref, slope_ref, spec_ref, lead_ref, trail_ref, lat_ref, steep_ref, *rest,
):
    sums = any(summed for *_, summed in passes)
    raw_ref = rest[0] if has_raw else None
    rest = rest[has_raw + waits :]
    held, turn, sem = rest[-3:]
    send_ref, keep_ref = rest[:2]
    if sums:
        steep_out_ref = rest[-4]
    copies, base = [], 0
    for i, (first, count, *_) in enumerate(passes):
        copy = pltpu.make_async_copy(spec_ref.at[:, pl.ds(first, count)], held.at[:, pl.ds(base, count)], sem.at[i])
        copy.start()
        copies.append(copy)
        base += count
    for d in range(HALF_DIRS):
        turn[d] = math.sin(heading(d)) * slope_ref[0] - math.cos(heading(d)) * slope_ref[1]
    if sums:
        steep_out_ref[...] = steep_ref[...]
    for copy in copies:
        copy.wait()
    rows_at = lax.broadcasted_iota(jnp.int32, (8, 256), 0)
    lanes_at = lax.broadcasted_iota(jnp.int32, (8, 256), 1)
    per_cell = TIME_STEP / CELL_SIZE * GRAVITY / 2.0
    bending = TIME_STEP * NDIR / (2.0 * math.pi) * (2.0 * math.pi * LOW_FREQ)
    group_count = group[1] - group[0]

    def body(flipped):
        lead_row, lead_shift = (7, 7) if flipped else (0, 1)
        trail_row, trail_shift = (0, 1) if flipped else (7, 7)
        lat_lane, lat_shift = (255, 255) if flipped else (0, 1)

        def one(first, dirs, slabs, summed, base, f, factors):
            sea = sea_ref[...]
            inverse, weight = factors
            total = jnp.zeros((8, 256), jnp.float32)
            offset = first - group[0]

            def energy(d):
                if d < 0:
                    return raw_ref[1, first + f] * sea
                if d >= HALF_DIRS:
                    return raw_ref[0, first + f] * sea
                return held[d, base + f] * sea

            known = {}
            for d in dirs:
                known = {e: known[e] if e in known else energy(e) for e in (d - 1, d, d + 1)}
                prev, here, after = known[d - 1], known[d], known[d + 1]
                rate = turn[d]
                size = jnp.abs(rate) * bending
                moved = size * jnp.where(rate > 0.0, prev, after)
                along_x = per_cell * abs(math.cos(heading(d)))
                along_y = per_cell * abs(math.sin(heading(d)))
                fixed = 0.0
                if d != LEAD_DIRS:
                    if d < LEAD_DIRS:
                        row = lead_ref[pl.ds(d * group_count + offset + f, 1), :]
                        edge, shift = lead_row, lead_shift
                    else:
                        row = trail_ref[pl.ds((d - LEAD_DIRS - 1) * group_count + offset + f, 1), :]
                        edge, shift = trail_row, trail_shift
                    side = jnp.where(rows_at == edge, jnp.broadcast_to(row, (8, 256)), pltpu.roll(here, shift, 0))
                    moved = moved + along_x * side
                    fixed += along_x
                if d != 0:
                    halo = pltpu.roll(lat_ref[d], lax.rem((lat_lane % 128) + 128 - (offset + f), 128), 1)
                    halo = jnp.concatenate([halo, halo], axis=1)
                    side = jnp.where(lanes_at == lat_lane, halo, pltpu.roll(here, lat_shift, 1))
                    moved = moved + along_y * side
                    fixed += along_y
                result = (here - inverse * ((size + fixed) * here - moved)) * sea
                if slabs is not None and is_sent(d):
                    send_ref[slabs[d] + f] = result
                elif slabs is not None:
                    keep_ref[d - SIDE_DIRS, f] = result
                total = total + result
            if summed:
                steep_out_ref[...] += weight * total
            return inverse * (1.0 / FREQ_STEP), weight * FREQ_STEP**2

        base = 0
        for first, count, dirs, slabs, summed in passes:
            factors = jnp.float32(1.0 / frequency(first)), jnp.float32((frequency(first) / frequency(NFREQ - 1)) ** 2)
            lax.fori_loop(0, count, functools.partial(one, first, dirs, slabs, summed, base), factors)
            base += count

    half = lax.axis_index("comp")

    @pl.when(half == 0)
    def _():
        body(False)

    @pl.when(half != 0)
    def _():
        body(True)

    if carries:
        send_ref[send_ref.shape[0] - 1] = steep_out_ref[...]


def advect_chunk(passes, group, carries, sea, slopes, spec, sides, steep, raw, after):
    vmem = pl.BlockSpec(memory_space=pltpu.VMEM)
    hold = pl.BlockSpec(memory_space=pl.ANY)
    slabs = sum(count * len(place) for _, count, _, place, _ in passes if place is not None)
    raw = () if raw is None else (raw,)
    out_shape = [
        jax.ShapeDtypeStruct((slabs + carries, 8, 256), jnp.float32),
        jax.ShapeDtypeStruct((HALF_DIRS - 2 * SIDE_DIRS, passes[0][1], 8, 256), jnp.float32),
    ]
    if any(summed for *_, summed in passes):
        out_shape.append(jax.ShapeDtypeStruct((8, 256), jnp.float32))
    return pl.pallas_call(
        functools.partial(advect_kernel, group, passes, carries, len(after), len(raw)),
        out_shape=out_shape,
        in_specs=[vmem, vmem, hold, vmem, vmem, vmem, vmem] + [vmem] * len(raw) + [hold] * len(after),
        out_specs=[vmem] * len(out_shape),
        scratch_shapes=[
            pltpu.VMEM((HALF_DIRS, sum(p[1] for p in passes), 8, 256), jnp.float32),
            pltpu.VMEM((HALF_DIRS, 8, 256), jnp.float32),
            pltpu.SemaphoreType.DMA((len(passes),)),
        ],
        compiler_params=pltpu.CompilerParams(vmem_limit_bytes=VMEM_BYTES),
        cost_estimate=SMALL_COST,
    )(sea, slopes, spec, *sides, steep, *raw, *after)


def source_kernel(
    first, count, inner, outer, chained, last,
    wind_ref, steep_a_ref, steep_b_ref, cum_ref, own_ref, keep_ref, other_ref, *rest,
):
    edge_own_ref, edge_other_ref = rest[:2] if outer else (None, None)
    out_ref, cum_out_ref, result, align, sems = rest[(2 if outer else 0) + chained :]
    weights = [math.cos(heading(m)) ** 2 / (9.0 * SATURATION_LEVEL) for m in range(SIDE_DIRS + 1)]
    steep = (steep_a_ref[...] + steep_b_ref[...]) * (1.0 / (NDIR * NFREQ))
    steep_sq = steep * steep
    for d in range(HALF_DIRS):
        align[d] = math.cos(heading(d)) * wind_ref[0] + math.sin(heading(d)) * wind_ref[1]
    cum_out_ref[...] = cum_ref[...]

    def leave(f):
        return pltpu.make_async_copy(result.at[:, f], out_ref.at[:, first + f], sems.at[f])

    def one(f, omega):
        gain = TIME_STEP * WIND_GROWTH * omega
        loss_sat = TIME_STEP * SATURATION_LOSS * omega
        loss_cum = TIME_STEP * CUMULATIVE_LOSS / NFREQ * omega
        loss_steep = TIME_STEP * STEEPNESS_LOSS * omega
        for half in range(2):
            lanes = slice(128 * half, 128 * half + 128)

            def slab(d, main, edge):
                return main[inner[d] + f, :, lanes] if d in inner else edge[outer[d] + f, :, lanes]

            first_dirs, last_dirs = ALL_DIRS[:SIDE_DIRS], ALL_DIRS[-SIDE_DIRS:]
            line = [slab(d, other_ref, edge_other_ref) for d in last_dirs]
            line += [slab(d, own_ref, edge_own_ref) for d in first_dirs]
            line += [keep_ref[i, f, :, lanes] for i in range(HALF_DIRS - 2 * SIDE_DIRS)]
            line += [slab(d, own_ref, edge_own_ref) for d in last_dirs]
            line += [slab(d, other_ref, edge_other_ref) for d in first_dirs]
            base = 1.0 + loss_steep * steep_sq[:, lanes]
            for d in range(HALF_DIRS):
                at = d + SIDE_DIRS
                level = weights[0] * line[at] - 1.0
                for m in range(1, SIDE_DIRS + 1):
                    level = level + weights[m] * (line[at - m] + line[at + m])
                excess = jnp.maximum(level, 0.0)
                square = excess * excess
                cum = cum_out_ref[d, :, lanes]
                cum_out_ref[d, :, lanes] = cum + square
                grown = 1.0 + gain * jnp.maximum(align[d, :, lanes] * omega - 1.0, 0.0)
                lost = base + loss_sat * square + loss_cum * cum
                result[d, f, :, lanes] = line[at] * grown / lost
        leave(f).start()
        return omega * FREQ_STEP

    lax.fori_loop(0, count, one, jnp.float32(frequency(first)))
    for f in range(count):
        leave(f).wait()


def source_chunk(first, count, inner, outer, last, wind, steep_own, steep_other, cum, own, keep, other, edges, out):
    vmem = pl.BlockSpec(memory_space=pltpu.VMEM)
    hold = pl.BlockSpec(memory_space=pl.ANY)
    chained = out is not None
    operands = (wind, steep_own, steep_other, cum, own, keep, other, *edges) + ((out,) if chained else ())
    out_shape = [jax.ShapeDtypeStruct((HALF_DIRS, NFREQ, 8, 256), jnp.float32)]
    running = [] if last else [jax.ShapeDtypeStruct((HALF_DIRS, 8, 256), jnp.float32)]
    result = pl.pallas_call(
        functools.partial(source_kernel, first, count, inner, outer, chained, last),
        out_shape=out_shape + running,
        in_specs=[vmem] * (7 + len(edges)) + [hold] * chained,
        out_specs=[hold] + [vmem] * len(running),
        scratch_shapes=[pltpu.VMEM((HALF_DIRS, 8, 256), jnp.float32)] * last
        + [
            pltpu.VMEM((HALF_DIRS, count, 8, 256), jnp.float32),
            pltpu.VMEM((HALF_DIRS, 8, 256), jnp.float32),
            pltpu.SemaphoreType.DMA((count,)),
        ],
        input_output_aliases={len(operands) - 1: 0} if chained else {},
        compiler_params=pltpu.CompilerParams(vmem_limit_bytes=VMEM_BYTES),
        cost_estimate=SMALL_COST,
    )(*operands)
    return result[0], None if last else result[1]


def ring_pairs(size, step, wrap):
    return [(i, (i + step) % size) for i in range(size) if wrap or 0 <= i + step < size]


def paired_shards(spectrum, sea_mask, owner_list, owner_count, slopes, friction, wind_angle):
    tiles_x, tiles_y = lax.axis_size("tx"), lax.axis_size("ty")
    half = lax.axis_index("comp")
    sign = 1.0 - 2.0 * half.astype(jnp.float32)
    spec = spectrum.reshape(HALF_DIRS, NFREQ, 8, 256)
    sea = sea_mask.astype(jnp.float32)
    turn = slopes * sign
    wind = (sign * WIND_FACTOR / GRAVITY) * friction * jnp.stack([jnp.cos(wind_angle), jnp.sin(wind_angle)])

    def joined(axis_size, step, wrap):
        ahead = ring_pairs(axis_size, step, wrap)
        back = ring_pairs(axis_size, -step, wrap)
        return ahead + [(axis_size + i, axis_size + j) for i, j in back]

    swap = [(0, 1), (1, 0)]
    lead_pairs = joined(tiles_x, 1, True)
    trail_pairs = joined(tiles_x, -1, True)
    lat_pairs = joined(tiles_y, 1, False)

    rows = pltpu.with_memory_space_constraint(spectrum.reshape(HALF_DIRS * NFREQ * 8, 256), pltpu.HBM)
    spec = pltpu.with_memory_space_constraint(spec, pltpu.HBM)
    bounds = chunk_bounds()
    raw = raw_edges(spec)

    def halo(g, after):
        begin, end = HALO_GROUPS[g]
        lead, trail, lat = pack(begin, end - begin, sea, rows, after)
        sides = (
            lax.ppermute(lead, ("comp", "tx"), lead_pairs),
            lax.ppermute(trail, ("comp", "tx"), trail_pairs),
            lax.ppermute(lat, ("comp", "ty"), lat_pairs),
        )
        return sides, lead

    first_sides, _ = halo(0, raw)
    raw = lax.ppermute(raw, "comp", swap)
    early = sum(end <= HALO_GROUPS[0][1] for _, end in bounds)
    counts = [end - begin for begin, end in bounds]
    places = [slab_index(INNER_DIRS if i == 0 else ALL_DIRS, counts[i]) for i in range(len(bounds))]
    edge_place = slab_index(OUTER_DIRS, counts[0], base=2 * SIDE_DIRS * counts[1])

    def advect(passes, sides, carries, steep, raw, after):
        group = HALO_GROUPS[0] if sides is first_sides else HALO_GROUPS[1]
        return advect_chunk(passes, group, carries, sea, turn, spec, sides, steep, raw, after)

    sent, kept, received, sums = [], [], [], []

    def send(result):
        sent.append(result[0])
        kept.append(result[1])
        received.append(lax.ppermute(result[0], "comp", swap))

    def source(upto):
        for j in range(len(sums), upto):
            outer, edges = (edge_place, (sent[1], received[1])) if j == 0 else (None, ())
            state[:] = source_chunk(
                bounds[j][0], counts[j], places[j], outer, j == len(bounds) - 1, wind, steep, steep_other,
                state[1], sent[j], kept[j], received[j], edges, state[0],
            )
            sums.append(state[1])

    steep = jnp.zeros((8, 256), jnp.float32)
    for i in range(early):
        passes = [(bounds[i][0], counts[i], INNER_DIRS if i == 0 else ALL_DIRS, places[i], True)]
        after = ()
        if i == 1:
            passes.append((bounds[0][0], counts[0], OUTER_DIRS, edge_place, True))
        if i >= 2:
            after = (received[i - 2], packed)
        result = advect(passes, first_sides, False, steep, raw if i else None, after)
        send(result)
        steep = result[2]
        if i == 1:
            later_sides, packed = halo(1, steep)
    state = [None, jnp.zeros((HALF_DIRS, 8, 256), jnp.float32)]
    summing = SUM_CHUNKS
    ahead = bounds[early + summing][0]
    cuts = [ahead + (NFREQ - ahead) * n // summing for n in range(summing + 1)]
    for i in range(early, len(bounds)):
        after = (received[i - 2],)
        if i in SOURCES_DONE:
            source(SOURCES_DONE[i])
            after += (sums[-1],)
        n = i - early
        passes = [(bounds[i][0], counts[i], ALL_DIRS, places[i], n < summing)]
        if n < summing:
            passes.append((cuts[n], cuts[n + 1] - cuts[n], ALL_DIRS, None, True))
        result = advect(passes, later_sides, n == summing - 1, steep, raw, after)
        send(result)
        if n < summing:
            steep = result[2]
        if n == summing - 1:
            steep_other = received[i][-1]
    source(len(bounds))
    out = state[0]
    return out.reshape(spectrum.shape)


def fits_pairs(mesh, spectrum):
    return (
        mesh.shape["comp"] == 2
        and spectrum.shape[0] == NDIR * NFREQ
        and spectrum.shape[1] == 8 * mesh.shape["tx"]
        and spectrum.shape[2] == 256 * mesh.shape["ty"]
    )


def solution(mesh):
    in_specs = (
        P("comp", "tx", "ty"),
        P("tx", "ty"),
        P("tx", "ty", None, None),
        P("tx", "ty", None),
        P(None, "tx", "ty"),
        P("tx", "ty"),
        P("tx", "ty"),
    )
    out_specs = P("comp", "tx", "ty")

    def step(spectrum, *others):
        body = paired_shards if fits_pairs(mesh, spectrum) else shards
        mapped = jax.shard_map(body, mesh=mesh, in_specs=in_specs, out_specs=out_specs, check_vma=False)
        return mapped(spectrum, *others)

    return step
```

```python
import functools
import math

import jax
import jax.numpy as jnp
from jax import lax
from jax.experimental import pallas as pl
from jax.experimental.pallas import tpu as pltpu
from jax.sharding import PartitionSpec as P

NDIR = 36
NFREQ = 50


TIME_STEP = 240.0
CELL_SIZE = 11100.0
GRAVITY = 9.81
LOW_FREQ = 0.0373
HIGH_FREQ = 1.0
WIND_GROWTH = 0.0001
WIND_FACTOR = 28.0
SATURATION_LOSS = 0.0005
CUMULATIVE_LOSS = 0.001
STEEPNESS_LOSS = 0.005
SATURATION_LEVEL = 0.6


def padded(value, sides, width, wrap):
    for axis, dim in sides:
        size, length = (lax.axis_size(axis), value.shape[dim])
        up = [(i, (i + 1) % size) for i in range(size if wrap else size - 1)]
        down = [(j, i) for i, j in up]
        last = lax.slice_in_dim(value, length - width, length, axis=dim)
        first = lax.slice_in_dim(value, 0, width, axis=dim)
        before = lax.ppermute(last, axis, up)
        after = lax.ppermute(first, axis, down)
        value = jnp.concatenate([before, value, after], axis=dim)
    return value


def freq_values(freq_ids):
    return (
        2.0
        * math.pi
        * LOW_FREQ
        * jnp.exp(freq_ids.astype(jnp.float32) * (math.log(HIGH_FREQ / LOW_FREQ) / (NFREQ - 1)))
    )


def wave_tables(first_comp, comp_count):
    comp_ids = first_comp + jnp.arange(comp_count, dtype=jnp.int32)
    headings = (comp_ids // NFREQ).astype(jnp.float32) * (2.0 * math.pi / NDIR)
    return (headings, freq_values(comp_ids % NFREQ))


def advect(
    energy,
    west_side,
    east_side,
    south_side,
    north_side,
    prev_dir,
    next_dir,
    headings,
    ang_freq,
    slopes,
):
    group_speed = GRAVITY / (2.0 * ang_freq)
    along_x = (TIME_STEP / CELL_SIZE * group_speed * jnp.cos(headings))[:, None, None]
    along_y = (TIME_STEP / CELL_SIZE * group_speed * jnp.sin(headings))[:, None, None]
    bending = TIME_STEP * NDIR / (2.0 * math.pi) * (2.0 * math.pi * LOW_FREQ) / ang_freq
    turning = bending[:, None, None] * (
        jnp.sin(headings)[:, None, None] * slopes[0][None]
        - jnp.cos(headings)[:, None, None] * slopes[1][None]
    )
    change = jnp.maximum(along_x, 0.0) * (energy - west_side) + jnp.minimum(along_x, 0.0) * (
        east_side - energy
    )
    change = (
        change
        + jnp.maximum(along_y, 0.0) * (energy - south_side)
        + jnp.minimum(along_y, 0.0) * (north_side - energy)
    )
    change = (
        change
        + jnp.maximum(turning, 0.0) * (energy - prev_dir)
        + jnp.minimum(turning, 0.0) * (next_dir - energy)
    )
    return energy - change


def source_terms(spectra, friction, wind_angle):
    dir_ids = jnp.arange(NDIR, dtype=jnp.int32)
    offset = (dir_ids[:, None] - dir_ids[None, :]) % NDIR
    nearest = jnp.minimum(offset, NDIR - offset)
    spread = jnp.where(
        4 * nearest < NDIR, jnp.cos(offset.astype(jnp.float32) * (2.0 * math.pi / NDIR)) ** 2, 0.0
    )
    spread = spread / jnp.sum(spread, axis=1, keepdims=True)
    sat_level = jnp.einsum("de,efp->dfp", spread, spectra, precision=lax.Precision.HIGHEST)
    excess = jnp.maximum(sat_level / SATURATION_LEVEL - 1.0, 0.0)
    excess_sq = excess * excess
    freq_ids = jnp.arange(NFREQ, dtype=jnp.int32)
    below_mask = (freq_ids[None, :] < freq_ids[:, None]).astype(jnp.float32)
    running = (
        jnp.einsum("fg,dgp->dfp", below_mask, excess_sq, precision=lax.Precision.HIGHEST) / NFREQ
    )
    ang_freq = freq_values(freq_ids)
    weights = (ang_freq / ang_freq[NFREQ - 1]) ** 2
    steepness = jnp.einsum("dfp,f->p", spectra, weights, precision=lax.Precision.HIGHEST) / (
        NDIR * NFREQ
    )
    headings = dir_ids.astype(jnp.float32) * (2.0 * math.pi / NDIR)
    alignment = (
        jnp.cos(headings)[:, None, None] * jnp.cos(wind_angle)[None, None, :]
        + jnp.sin(headings)[:, None, None] * jnp.sin(wind_angle)[None, None, :]
    )
    forcing = WIND_FACTOR / GRAVITY * friction[None, None, :] * ang_freq[None, :, None] * alignment
    growth = WIND_GROWTH * ang_freq[None, :, None] * jnp.maximum(forcing - 1.0, 0.0)
    losses = ang_freq[None, :, None] * (
        SATURATION_LOSS * excess_sq
        + CUMULATIVE_LOSS * running
        + STEEPNESS_LOSS * (steepness * steepness)[None, None, :]
    )
    return spectra * (1.0 + TIME_STEP * growth) / (1.0 + TIME_STEP * losses)


def shards(spectrum, sea_mask, owner_list, owner_count, slopes, friction, wind_angle):
    comp_size = lax.axis_size("comp")
    local_comps = spectrum.shape[0]
    cell_count = spectrum.shape[1] * spectrum.shape[2]
    sea_cells = sea_mask.astype(jnp.float32)
    masked = spectrum * sea_cells[None]
    headings, ang_freq = wave_tables(lax.axis_index("comp") * local_comps, local_comps)
    padded_lon = padded(masked, (("tx", 1),), 1, True)
    padded_lat = padded(masked, (("ty", 2),), 1, False)
    padded_dir = padded(masked, (("comp", 0),), NFREQ, True)
    advected = (
        advect(
            masked,
            padded_lon[:, :-2],
            padded_lon[:, 2:],
            padded_lat[:, :, :-2],
            padded_lat[:, :, 2:],
            padded_dir[:local_comps],
            padded_dir[2 * NFREQ :],
            headings,
            ang_freq,
            slopes,
        )
        * sea_cells[None]
    )
    moved_flat = advected.reshape(local_comps, cell_count)
    cell_names = owner_list[0, 0]
    slot_ids = jnp.arange(cell_names.shape[1], dtype=jnp.int32)
    in_use = slot_ids[None, :] < owner_count[0, 0][:, None]
    target = jnp.where(in_use, cell_names, cell_count).reshape(-1)
    owners = cell_names.shape[0]
    capacity = cell_names.shape[1]
    tiles_x = lax.axis_size("tx")
    cell_ids = jnp.arange(cell_count, dtype=jnp.int32)
    selector = (cell_ids[:, None] == target[None, :]).astype(jnp.float32)
    outgoing = jnp.dot(moved_flat, selector, precision=lax.Precision.HIGHEST).reshape(
        local_comps, owners, capacity
    )
    wind_rows = jnp.stack([friction.reshape(-1), wind_angle.reshape(-1)])
    point_data = jnp.dot(wind_rows, selector, precision=lax.Precision.HIGHEST).reshape(
        2, owners, capacity
    )
    spectra = lax.all_to_all(outgoing, ("comp", "tx"), split_axis=1, concat_axis=1, tiled=True)
    extras = lax.all_to_all(point_data, ("comp", "tx"), split_axis=1, concat_axis=1, tiled=True)
    batch_size = spectra.shape[2]
    full_spec = (
        spectra.reshape(local_comps, comp_size, tiles_x * batch_size)
        .transpose(1, 0, 2)
        .reshape(NDIR, NFREQ, tiles_x * batch_size)
    )
    extra_rows = extras.reshape(2, comp_size, tiles_x * batch_size)[:, 0]
    result = source_terms(full_spec, extra_rows[0], extra_rows[1])
    homeward = (
        result.reshape(comp_size, local_comps, tiles_x * batch_size)
        .transpose(1, 0, 2)
        .reshape(local_comps, comp_size * tiles_x, batch_size)
    )
    returned = lax.all_to_all(homeward, ("comp", "tx"), split_axis=1, concat_axis=1, tiled=True)
    gathered = lax.dot_general(
        returned.reshape(local_comps, owners * capacity),
        selector,
        (((1,), (1,)), ((), ())),
        precision=lax.Precision.HIGHEST,
    )
    listed = jnp.sum(selector, axis=1) > 0.5
    updated = jnp.where(listed[None], gathered, moved_flat)
    return updated.reshape(spectrum.shape)


def chunk_bounds():
    return [(5 * i, 5 * i + 5) for i in range(9)] + [(45, 47), (47, 49), (49, 50)]


HALO_GROUPS = ((0, 15), (15, 50))
SUM_CHUNKS = 3
RAW_PIECES = 10
SOURCES_DONE = {8: 2, 9: 5, 10: 7, 11: 9}
HALF_DIRS = NDIR // 2
SIDE_DIRS = 8
LEAD_DIRS = 9
VMEM_BYTES = 24 * 1024 * 1024
SMALL_COST = pl.CostEstimate(flops=1024, bytes_accessed=1024, transcendentals=0)


FREQ_STEP = (HIGH_FREQ / LOW_FREQ) ** (1.0 / (NFREQ - 1))


def frequency(index):
    return 2.0 * math.pi * LOW_FREQ * FREQ_STEP**index


def heading(index):
    return 2.0 * math.pi * index / NDIR


def raw_kernel(spec_ref, raw_ref, sems):
    copies = []
    for i, d in enumerate((0, HALF_DIRS - 1)):
        for n in range(RAW_PIECES):
            part = pl.ds(n * (NFREQ // RAW_PIECES), NFREQ // RAW_PIECES)
            copy = pltpu.make_async_copy(spec_ref.at[d, part], raw_ref.at[i, part], sems.at[i, n])
            copy.start()
            copies.append(copy)
    for copy in copies:
        copy.wait()


def raw_edges(spec):
    return pl.pallas_call(
        raw_kernel,
        out_shape=jax.ShapeDtypeStruct((2, NFREQ, 8, 256), jnp.float32),
        in_specs=[pl.BlockSpec(memory_space=pl.ANY)],
        out_specs=pl.BlockSpec(memory_space=pltpu.VMEM),
        scratch_shapes=[pltpu.SemaphoreType.DMA((2, RAW_PIECES))],
        compiler_params=pltpu.CompilerParams(vmem_limit_bytes=VMEM_BYTES),
        cost_estimate=SMALL_COST,
    )(spec)


def pack_kernel(first, count, sea_ref, spec_ref, after_ref, lead_ref, trail_ref, lat_ref, held, sems):
    def body(flipped):
        lead_row, trail_row = (0, 7) if flipped else (7, 0)
        part = 0 if flipped else 1
        copies = []
        for d in range(HALF_DIRS):
            for h in range(2):
                place = h * HALF_DIRS + d
                copy = pltpu.make_async_copy(
                    spec_ref.at[pl.ds((d * NFREQ + first) * 8, count * 8), pl.ds(128 * h, 128)],
                    held.at[pl.ds(place * count * 8, count * 8)],
                    sems.at[place],
                )
                copy.start()
                copies.append(copy)
        for d in range(HALF_DIRS):
            for h in range(2):
                copies[2 * d + h].wait()
                lanes_here = slice(128 * h, 128 * h + 128)
                start = (h * HALF_DIRS + d) * count * 8
                if d < LEAD_DIRS:
                    column = held[pl.ds(start + lead_row, count, stride=8), :]
                    lead_ref[d * count : (d + 1) * count, lanes_here] = column * sea_ref[lead_row : lead_row + 1, lanes_here]
                elif d > LEAD_DIRS:
                    t = d - LEAD_DIRS - 1
                    column = held[pl.ds(start + trail_row, count, stride=8), :]
                    trail_ref[t * count : (t + 1) * count, lanes_here] = column * sea_ref[trail_row : trail_row + 1, lanes_here]
        lane = 0 if flipped else 127
        lanes = lax.broadcasted_iota(jnp.int32, (8, 128), 1)
        sea_line = jnp.broadcast_to(sea_ref[:, 128 * part + lane : 128 * part + lane + 1], (8, 128))

        def slab(d, f):
            return held[pl.ds(pl.multiple_of((part * HALF_DIRS + d) * count * 8 + f * 8, 8), 8), :]

        def one(f, kept):
            here = lanes == f
            return tuple(
                jnp.where(here, jnp.broadcast_to(slab(d, f)[:, lane : lane + 1], (8, 128)), kept[d])
                for d in range(HALF_DIRS)
            )

        zeros = jnp.zeros((8, 128), jnp.float32)
        kept = lax.fori_loop(0, count, one, (zeros,) * HALF_DIRS, unroll=5)
        for d in range(HALF_DIRS):
            lat_ref[d] = kept[d] * sea_line

    half = lax.axis_index("comp")

    @pl.when(half == 0)
    def _():
        body(False)

    @pl.when(half != 0)
    def _():
        body(True)


def pack(first, count, sea, spec, after):
    vmem = pl.BlockSpec(memory_space=pltpu.VMEM)
    hold = pl.BlockSpec(memory_space=pl.ANY)
    return pl.pallas_call(
        functools.partial(pack_kernel, first, count),
        out_shape=[
            jax.ShapeDtypeStruct((LEAD_DIRS * count, 256), jnp.float32),
            jax.ShapeDtypeStruct(((HALF_DIRS - LEAD_DIRS - 1) * count, 256), jnp.float32),
            jax.ShapeDtypeStruct((HALF_DIRS, 8, 128), jnp.float32),
        ],
        in_specs=[vmem, hold, hold],
        out_specs=[vmem] * 3,
        scratch_shapes=[
            pltpu.VMEM(((2 * HALF_DIRS + 1) * count * 8, 128), jnp.float32),
            pltpu.SemaphoreType.DMA((2 * HALF_DIRS,)),
        ],
        compiler_params=pltpu.CompilerParams(vmem_limit_bytes=VMEM_BYTES),
        cost_estimate=SMALL_COST,
    )(sea, spec, after)


ALL_DIRS = tuple(range(HALF_DIRS))
INNER_DIRS = ALL_DIRS[1:-1]
OUTER_DIRS = (0, HALF_DIRS - 1)


def is_sent(d):
    return d < SIDE_DIRS or d >= HALF_DIRS - SIDE_DIRS


def slab_index(dirs, count, base=0):
    return {d: base + count * n for n, d in enumerate(d for d in dirs if is_sent(d))}


def advect_kernel(
    group, passes, carries, waits, has_raw,
    sea_ref, slope_ref, spec_ref, lead_ref, trail_ref, lat_ref, steep_ref, *rest,
):
    sums = any(summed for *_, summed in passes)
    raw_ref = rest[0] if has_raw else None
    rest = rest[has_raw + waits :]
    held, turn, sem = rest[-3:]
    send_ref, keep_ref = rest[:2]
    if sums:
        steep_out_ref = rest[-4]
    copies, base = [], 0
    for i, (first, count, *_) in enumerate(passes):
        copy = pltpu.make_async_copy(spec_ref.at[:, pl.ds(first, count)], held.at[:, pl.ds(base, count)], sem.at[i])
        copy.start()
        copies.append(copy)
        base += count
    for d in range(HALF_DIRS):
        turn[d] = math.sin(heading(d)) * slope_ref[0] - math.cos(heading(d)) * slope_ref[1]
    if sums:
        steep_out_ref[...] = steep_ref[...]
    for copy in copies:
        copy.wait()
    rows_at = lax.broadcasted_iota(jnp.int32, (8, 256), 0)
    lanes_at = lax.broadcasted_iota(jnp.int32, (8, 256), 1)
    per_cell = TIME_STEP / CELL_SIZE * GRAVITY / 2.0
    bending = TIME_STEP * NDIR / (2.0 * math.pi) * (2.0 * math.pi * LOW_FREQ)
    group_count = group[1] - group[0]

    def body(flipped):
        lead_row, lead_shift = (7, 7) if flipped else (0, 1)
        trail_row, trail_shift = (0, 1) if flipped else (7, 7)
        lat_lane, lat_shift = (255, 255) if flipped else (0, 1)

        def one(first, dirs, slabs, summed, base, f, factors):
            sea = sea_ref[...]
            inverse, weight = factors
            total = jnp.zeros((8, 256), jnp.float32)
            offset = first - group[0]

            def energy(d):
                if d < 0:
                    return raw_ref[1, first + f] * sea
                if d >= HALF_DIRS:
                    return raw_ref[0, first + f] * sea
                return held[d, base + f] * sea

            known = {}
            for d in dirs:
                known = {e: known[e] if e in known else energy(e) for e in (d - 1, d, d + 1)}
                prev, here, after = known[d - 1], known[d], known[d + 1]
                rate = turn[d]
                size = jnp.abs(rate) * bending
                moved = size * jnp.where(rate > 0.0, prev, after)
                along_x = per_cell * abs(math.cos(heading(d)))
                along_y = per_cell * abs(math.sin(heading(d)))
                fixed = 0.0
                if d != LEAD_DIRS:
                    if d < LEAD_DIRS:
                        row = lead_ref[pl.ds(d * group_count + offset + f, 1), :]
                        edge, shift = lead_row, lead_shift
                    else:
                        row = trail_ref[pl.ds((d - LEAD_DIRS - 1) * group_count + offset + f, 1), :]
                        edge, shift = trail_row, trail_shift
                    side = jnp.where(rows_at == edge, jnp.broadcast_to(row, (8, 256)), pltpu.roll(here, shift, 0))
                    moved = moved + along_x * side
                    fixed += along_x
                if d != 0:
                    halo = pltpu.roll(lat_ref[d], lax.rem((lat_lane % 128) + 128 - (offset + f), 128), 1)
                    halo = jnp.concatenate([halo, halo], axis=1)
                    side = jnp.where(lanes_at == lat_lane, halo, pltpu.roll(here, lat_shift, 1))
                    moved = moved + along_y * side
                    fixed += along_y
                result = (here - inverse * ((size + fixed) * here - moved)) * sea
                if slabs is not None and is_sent(d):
                    send_ref[slabs[d] + f] = result
                elif slabs is not None:
                    keep_ref[d - SIDE_DIRS, f] = result
                total = total + result
            if summed:
                steep_out_ref[...] += weight * total
            return inverse * (1.0 / FREQ_STEP), weight * FREQ_STEP**2

        base = 0
        for first, count, dirs, slabs, summed in passes:
            factors = jnp.float32(1.0 / frequency(first)), jnp.float32((frequency(first) / frequency(NFREQ - 1)) ** 2)
            lax.fori_loop(0, count, functools.partial(one, first, dirs, slabs, summed, base), factors)
            base += count

    half = lax.axis_index("comp")

    @pl.when(half == 0)
    def _():
        body(False)

    @pl.when(half != 0)
    def _():
        body(True)

    if carries:
        send_ref[send_ref.shape[0] - 1] = steep_out_ref[...]


def advect_chunk(passes, group, carries, sea, slopes, spec, sides, steep, raw, after):
    vmem = pl.BlockSpec(memory_space=pltpu.VMEM)
    hold = pl.BlockSpec(memory_space=pl.ANY)
    slabs = sum(count * len(place) for _, count, _, place, _ in passes if place is not None)
    raw = () if raw is None else (raw,)
    out_shape = [
        jax.ShapeDtypeStruct((slabs + carries, 8, 256), jnp.float32),
        jax.ShapeDtypeStruct((HALF_DIRS - 2 * SIDE_DIRS, passes[0][1], 8, 256), jnp.float32),
    ]
    if any(summed for *_, summed in passes):
        out_shape.append(jax.ShapeDtypeStruct((8, 256), jnp.float32))
    return pl.pallas_call(
        functools.partial(advect_kernel, group, passes, carries, len(after), len(raw)),
        out_shape=out_shape,
        in_specs=[vmem, vmem, hold, vmem, vmem, vmem, vmem] + [vmem] * len(raw) + [hold] * len(after),
        out_specs=[vmem] * len(out_shape),
        scratch_shapes=[
            pltpu.VMEM((HALF_DIRS, sum(p[1] for p in passes), 8, 256), jnp.float32),
            pltpu.VMEM((HALF_DIRS, 8, 256), jnp.float32),
            pltpu.SemaphoreType.DMA((len(passes),)),
        ],
        compiler_params=pltpu.CompilerParams(vmem_limit_bytes=VMEM_BYTES),
        cost_estimate=SMALL_COST,
    )(sea, slopes, spec, *sides, steep, *raw, *after)


def source_kernel(
    first, count, inner, outer, chained, last,
    wind_ref, steep_a_ref, steep_b_ref, cum_ref, own_ref, keep_ref, other_ref, *rest,
):
    edge_own_ref, edge_other_ref = rest[:2] if outer else (None, None)
    out_ref, cum_out_ref, result, align, sems = rest[(2 if outer else 0) + chained :]
    weights = [math.cos(heading(m)) ** 2 / (9.0 * SATURATION_LEVEL) for m in range(SIDE_DIRS + 1)]
    steep = (steep_a_ref[...] + steep_b_ref[...]) * (1.0 / (NDIR * NFREQ))
    steep_sq = steep * steep
    for d in range(HALF_DIRS):
        align[d] = math.cos(heading(d)) * wind_ref[0] + math.sin(heading(d)) * wind_ref[1]
    cum_out_ref[...] = cum_ref[...]

    def leave(f, half):
        lanes = pl.ds(128 * half, 128)
        return pltpu.make_async_copy(result.at[:, f, :, lanes], out_ref.at[:, first + f, :, lanes], sems.at[f, half])

    def one(f, omega):
        gain = TIME_STEP * WIND_GROWTH * omega
        loss_sat = TIME_STEP * SATURATION_LOSS * omega
        loss_cum = TIME_STEP * CUMULATIVE_LOSS / NFREQ * omega
        loss_steep = TIME_STEP * STEEPNESS_LOSS * omega
        for half in range(2):
            lanes = slice(128 * half, 128 * half + 128)

            def slab(d, main, edge):
                return main[inner[d] + f, :, lanes] if d in inner else edge[outer[d] + f, :, lanes]

            first_dirs, last_dirs = ALL_DIRS[:SIDE_DIRS], ALL_DIRS[-SIDE_DIRS:]
            line = [slab(d, other_ref, edge_other_ref) for d in last_dirs]
            line += [slab(d, own_ref, edge_own_ref) for d in first_dirs]
            line += [keep_ref[i, f, :, lanes] for i in range(HALF_DIRS - 2 * SIDE_DIRS)]
            line += [slab(d, own_ref, edge_own_ref) for d in last_dirs]
            line += [slab(d, other_ref, edge_other_ref) for d in first_dirs]
            base = 1.0 + loss_steep * steep_sq[:, lanes]
            for d in range(HALF_DIRS):
                at = d + SIDE_DIRS
                level = weights[0] * line[at] - 1.0
                for m in range(1, SIDE_DIRS + 1):
                    level = level + weights[m] * (line[at - m] + line[at + m])
                excess = jnp.maximum(level, 0.0)
                square = excess * excess
                cum = cum_out_ref[d, :, lanes]
                cum_out_ref[d, :, lanes] = cum + square
                grown = 1.0 + gain * jnp.maximum(align[d, :, lanes] * omega - 1.0, 0.0)
                lost = base + loss_sat * square + loss_cum * cum
                result[d, f, :, lanes] = line[at] * grown / lost
            leave(f, half).start()
        return omega * FREQ_STEP

    lax.fori_loop(0, count, one, jnp.float32(frequency(first)))
    for f in range(count):
        for half in range(2):
            leave(f, half).wait()


def source_chunk(first, count, inner, outer, last, wind, steep_own, steep_other, cum, own, keep, other, edges, out):
    vmem = pl.BlockSpec(memory_space=pltpu.VMEM)
    hold = pl.BlockSpec(memory_space=pl.ANY)
    chained = out is not None
    operands = (wind, steep_own, steep_other, cum, own, keep, other, *edges) + ((out,) if chained else ())
    out_shape = [jax.ShapeDtypeStruct((HALF_DIRS, NFREQ, 8, 256), jnp.float32)]
    running = [] if last else [jax.ShapeDtypeStruct((HALF_DIRS, 8, 256), jnp.float32)]
    result = pl.pallas_call(
        functools.partial(source_kernel, first, count, inner, outer, chained, last),
        out_shape=out_shape + running,
        in_specs=[vmem] * (7 + len(edges)) + [hold] * chained,
        out_specs=[hold] + [vmem] * len(running),
        scratch_shapes=[pltpu.VMEM((HALF_DIRS, 8, 256), jnp.float32)] * last
        + [
            pltpu.VMEM((HALF_DIRS, count, 8, 256), jnp.float32),
            pltpu.VMEM((HALF_DIRS, 8, 256), jnp.float32),
            pltpu.SemaphoreType.DMA((count, 2)),
        ],
        input_output_aliases={len(operands) - 1: 0} if chained else {},
        compiler_params=pltpu.CompilerParams(vmem_limit_bytes=VMEM_BYTES),
        cost_estimate=SMALL_COST,
    )(*operands)
    return result[0], None if last else result[1]


def ring_pairs(size, step, wrap):
    return [(i, (i + step) % size) for i in range(size) if wrap or 0 <= i + step < size]


def paired_shards(spectrum, sea_mask, owner_list, owner_count, slopes, friction, wind_angle):
    tiles_x, tiles_y = lax.axis_size("tx"), lax.axis_size("ty")
    half = lax.axis_index("comp")
    sign = 1.0 - 2.0 * half.astype(jnp.float32)
    spec = spectrum.reshape(HALF_DIRS, NFREQ, 8, 256)
    sea = sea_mask.astype(jnp.float32)
    turn = slopes * sign
    wind = (sign * WIND_FACTOR / GRAVITY) * friction * jnp.stack([jnp.cos(wind_angle), jnp.sin(wind_angle)])

    def joined(axis_size, step, wrap):
        ahead = ring_pairs(axis_size, step, wrap)
        back = ring_pairs(axis_size, -step, wrap)
        return ahead + [(axis_size + i, axis_size + j) for i, j in back]

    swap = [(0, 1), (1, 0)]
    lead_pairs = joined(tiles_x, 1, True)
    trail_pairs = joined(tiles_x, -1, True)
    lat_pairs = joined(tiles_y, 1, False)

    rows = pltpu.with_memory_space_constraint(spectrum.reshape(HALF_DIRS * NFREQ * 8, 256), pltpu.HBM)
    spec = pltpu.with_memory_space_constraint(spec, pltpu.HBM)
    bounds = chunk_bounds()
    raw = raw_edges(spec)

    def halo(g, after):
        begin, end = HALO_GROUPS[g]
        lead, trail, lat = pack(begin, end - begin, sea, rows, after)
        sides = (
            lax.ppermute(lead, ("comp", "tx"), lead_pairs),
            lax.ppermute(trail, ("comp", "tx"), trail_pairs),
            lax.ppermute(lat, ("comp", "ty"), lat_pairs),
        )
        return sides, lead

    first_sides, _ = halo(0, raw)
    raw = lax.ppermute(raw, "comp", swap)
    early = sum(end <= HALO_GROUPS[0][1] for _, end in bounds)
    counts = [end - begin for begin, end in bounds]
    places = [slab_index(INNER_DIRS if i == 0 else ALL_DIRS, counts[i]) for i in range(len(bounds))]
    edge_place = slab_index(OUTER_DIRS, counts[0], base=2 * SIDE_DIRS * counts[1])

    def advect(passes, sides, carries, steep, raw, after):
        group = HALO_GROUPS[0] if sides is first_sides else HALO_GROUPS[1]
        return advect_chunk(passes, group, carries, sea, turn, spec, sides, steep, raw, after)

    sent, kept, received, sums = [], [], [], []

    def send(result):
        sent.append(result[0])
        kept.append(result[1])
        received.append(lax.ppermute(result[0], "comp", swap))

    def source(upto):
        for j in range(len(sums), upto):
            outer, edges = (edge_place, (sent[1], received[1])) if j == 0 else (None, ())
            state[:] = source_chunk(
                bounds[j][0], counts[j], places[j], outer, j == len(bounds) - 1, wind, steep, steep_other,
                state[1], sent[j], kept[j], received[j], edges, state[0],
            )
            sums.append(state[1])

    steep = jnp.zeros((8, 256), jnp.float32)
    for i in range(early):
        passes = [(bounds[i][0], counts[i], INNER_DIRS if i == 0 else ALL_DIRS, places[i], True)]
        after = ()
        if i == 1:
            passes.append((bounds[0][0], counts[0], OUTER_DIRS, edge_place, True))
        if i >= 2:
            after = (received[i - 2], packed)
        result = advect(passes, first_sides, False, steep, raw if i else None, after)
        send(result)
        steep = result[2]
        if i == 1:
            later_sides, packed = halo(1, steep)
    state = [None, jnp.zeros((HALF_DIRS, 8, 256), jnp.float32)]
    summing = SUM_CHUNKS
    ahead = bounds[early + summing][0]
    cuts = [ahead + (NFREQ - ahead) * n // summing for n in range(summing + 1)]
    for i in range(early, len(bounds)):
        after = (received[i - 2],)
        if i in SOURCES_DONE:
            source(SOURCES_DONE[i])
            after += (sums[-1],)
        n = i - early
        passes = [(bounds[i][0], counts[i], ALL_DIRS, places[i], n < summing)]
        if n < summing:
            passes.append((cuts[n], cuts[n + 1] - cuts[n], ALL_DIRS, None, True))
        result = advect(passes, later_sides, n == summing - 1, steep, raw, after)
        send(result)
        if n < summing:
            steep = result[2]
        if n == summing - 1:
            steep_other = received[i][-1]
    source(len(bounds))
    out = state[0]
    return out.reshape(spectrum.shape)


def fits_pairs(mesh, spectrum):
    return (
        mesh.shape["comp"] == 2
        and spectrum.shape[0] == NDIR * NFREQ
        and spectrum.shape[1] == 8 * mesh.shape["tx"]
        and spectrum.shape[2] == 256 * mesh.shape["ty"]
    )


def solution(mesh):
    in_specs = (
        P("comp", "tx", "ty"),
        P("tx", "ty"),
        P("tx", "ty", None, None),
        P("tx", "ty", None),
        P(None, "tx", "ty"),
        P("tx", "ty"),
        P("tx", "ty"),
    )
    out_specs = P("comp", "tx", "ty")

    def step(spectrum, *others):
        body = paired_shards if fits_pairs(mesh, spectrum) else shards
        mapped = jax.shard_map(body, mesh=mesh, in_specs=in_specs, out_specs=out_specs, check_vma=False)
        return mapped(spectrum, *others)

    return step
```

```python
import functools
import math

import jax
import jax.numpy as jnp
from jax import lax
from jax.experimental import pallas as pl
from jax.experimental.pallas import tpu as pltpu
from jax.sharding import PartitionSpec as P

NDIR = 36
NFREQ = 50


TIME_STEP = 240.0
CELL_SIZE = 11100.0
GRAVITY = 9.81
LOW_FREQ = 0.0373
HIGH_FREQ = 1.0
WIND_GROWTH = 0.0001
WIND_FACTOR = 28.0
SATURATION_LOSS = 0.0005
CUMULATIVE_LOSS = 0.001
STEEPNESS_LOSS = 0.005
SATURATION_LEVEL = 0.6


def padded(value, sides, width, wrap):
    for axis, dim in sides:
        size, length = (lax.axis_size(axis), value.shape[dim])
        up = [(i, (i + 1) % size) for i in range(size if wrap else size - 1)]
        down = [(j, i) for i, j in up]
        last = lax.slice_in_dim(value, length - width, length, axis=dim)
        first = lax.slice_in_dim(value, 0, width, axis=dim)
        before = lax.ppermute(last, axis, up)
        after = lax.ppermute(first, axis, down)
        value = jnp.concatenate([before, value, after], axis=dim)
    return value


def freq_values(freq_ids):
    return (
        2.0
        * math.pi
        * LOW_FREQ
        * jnp.exp(freq_ids.astype(jnp.float32) * (math.log(HIGH_FREQ / LOW_FREQ) / (NFREQ - 1)))
    )


def wave_tables(first_comp, comp_count):
    comp_ids = first_comp + jnp.arange(comp_count, dtype=jnp.int32)
    headings = (comp_ids // NFREQ).astype(jnp.float32) * (2.0 * math.pi / NDIR)
    return (headings, freq_values(comp_ids % NFREQ))


def advect(
    energy,
    west_side,
    east_side,
    south_side,
    north_side,
    prev_dir,
    next_dir,
    headings,
    ang_freq,
    slopes,
):
    group_speed = GRAVITY / (2.0 * ang_freq)
    along_x = (TIME_STEP / CELL_SIZE * group_speed * jnp.cos(headings))[:, None, None]
    along_y = (TIME_STEP / CELL_SIZE * group_speed * jnp.sin(headings))[:, None, None]
    bending = TIME_STEP * NDIR / (2.0 * math.pi) * (2.0 * math.pi * LOW_FREQ) / ang_freq
    turning = bending[:, None, None] * (
        jnp.sin(headings)[:, None, None] * slopes[0][None]
        - jnp.cos(headings)[:, None, None] * slopes[1][None]
    )
    change = jnp.maximum(along_x, 0.0) * (energy - west_side) + jnp.minimum(along_x, 0.0) * (
        east_side - energy
    )
    change = (
        change
        + jnp.maximum(along_y, 0.0) * (energy - south_side)
        + jnp.minimum(along_y, 0.0) * (north_side - energy)
    )
    change = (
        change
        + jnp.maximum(turning, 0.0) * (energy - prev_dir)
        + jnp.minimum(turning, 0.0) * (next_dir - energy)
    )
    return energy - change


def source_terms(spectra, friction, wind_angle):
    dir_ids = jnp.arange(NDIR, dtype=jnp.int32)
    offset = (dir_ids[:, None] - dir_ids[None, :]) % NDIR
    nearest = jnp.minimum(offset, NDIR - offset)
    spread = jnp.where(
        4 * nearest < NDIR, jnp.cos(offset.astype(jnp.float32) * (2.0 * math.pi / NDIR)) ** 2, 0.0
    )
    spread = spread / jnp.sum(spread, axis=1, keepdims=True)
    sat_level = jnp.einsum("de,efp->dfp", spread, spectra, precision=lax.Precision.HIGHEST)
    excess = jnp.maximum(sat_level / SATURATION_LEVEL - 1.0, 0.0)
    excess_sq = excess * excess
    freq_ids = jnp.arange(NFREQ, dtype=jnp.int32)
    below_mask = (freq_ids[None, :] < freq_ids[:, None]).astype(jnp.float32)
    running = (
        jnp.einsum("fg,dgp->dfp", below_mask, excess_sq, precision=lax.Precision.HIGHEST) / NFREQ
    )
    ang_freq = freq_values(freq_ids)
    weights = (ang_freq / ang_freq[NFREQ - 1]) ** 2
    steepness = jnp.einsum("dfp,f->p", spectra, weights, precision=lax.Precision.HIGHEST) / (
        NDIR * NFREQ
    )
    headings = dir_ids.astype(jnp.float32) * (2.0 * math.pi / NDIR)
    alignment = (
        jnp.cos(headings)[:, None, None] * jnp.cos(wind_angle)[None, None, :]
        + jnp.sin(headings)[:, None, None] * jnp.sin(wind_angle)[None, None, :]
    )
    forcing = WIND_FACTOR / GRAVITY * friction[None, None, :] * ang_freq[None, :, None] * alignment
    growth = WIND_GROWTH * ang_freq[None, :, None] * jnp.maximum(forcing - 1.0, 0.0)
    losses = ang_freq[None, :, None] * (
        SATURATION_LOSS * excess_sq
        + CUMULATIVE_LOSS * running
        + STEEPNESS_LOSS * (steepness * steepness)[None, None, :]
    )
    return spectra * (1.0 + TIME_STEP * growth) / (1.0 + TIME_STEP * losses)


def shards(spectrum, sea_mask, owner_list, owner_count, slopes, friction, wind_angle):
    comp_size = lax.axis_size("comp")
    local_comps = spectrum.shape[0]
    cell_count = spectrum.shape[1] * spectrum.shape[2]
    sea_cells = sea_mask.astype(jnp.float32)
    masked = spectrum * sea_cells[None]
    headings, ang_freq = wave_tables(lax.axis_index("comp") * local_comps, local_comps)
    padded_lon = padded(masked, (("tx", 1),), 1, True)
    padded_lat = padded(masked, (("ty", 2),), 1, False)
    padded_dir = padded(masked, (("comp", 0),), NFREQ, True)
    advected = (
        advect(
            masked,
            padded_lon[:, :-2],
            padded_lon[:, 2:],
            padded_lat[:, :, :-2],
            padded_lat[:, :, 2:],
            padded_dir[:local_comps],
            padded_dir[2 * NFREQ :],
            headings,
            ang_freq,
            slopes,
        )
        * sea_cells[None]
    )
    moved_flat = advected.reshape(local_comps, cell_count)
    cell_names = owner_list[0, 0]
    slot_ids = jnp.arange(cell_names.shape[1], dtype=jnp.int32)
    in_use = slot_ids[None, :] < owner_count[0, 0][:, None]
    target = jnp.where(in_use, cell_names, cell_count).reshape(-1)
    owners = cell_names.shape[0]
    capacity = cell_names.shape[1]
    tiles_x = lax.axis_size("tx")
    cell_ids = jnp.arange(cell_count, dtype=jnp.int32)
    selector = (cell_ids[:, None] == target[None, :]).astype(jnp.float32)
    outgoing = jnp.dot(moved_flat, selector, precision=lax.Precision.HIGHEST).reshape(
        local_comps, owners, capacity
    )
    wind_rows = jnp.stack([friction.reshape(-1), wind_angle.reshape(-1)])
    point_data = jnp.dot(wind_rows, selector, precision=lax.Precision.HIGHEST).reshape(
        2, owners, capacity
    )
    spectra = lax.all_to_all(outgoing, ("comp", "tx"), split_axis=1, concat_axis=1, tiled=True)
    extras = lax.all_to_all(point_data, ("comp", "tx"), split_axis=1, concat_axis=1, tiled=True)
    batch_size = spectra.shape[2]
    full_spec = (
        spectra.reshape(local_comps, comp_size, tiles_x * batch_size)
        .transpose(1, 0, 2)
        .reshape(NDIR, NFREQ, tiles_x * batch_size)
    )
    extra_rows = extras.reshape(2, comp_size, tiles_x * batch_size)[:, 0]
    result = source_terms(full_spec, extra_rows[0], extra_rows[1])
    homeward = (
        result.reshape(comp_size, local_comps, tiles_x * batch_size)
        .transpose(1, 0, 2)
        .reshape(local_comps, comp_size * tiles_x, batch_size)
    )
    returned = lax.all_to_all(homeward, ("comp", "tx"), split_axis=1, concat_axis=1, tiled=True)
    gathered = lax.dot_general(
        returned.reshape(local_comps, owners * capacity),
        selector,
        (((1,), (1,)), ((), ())),
        precision=lax.Precision.HIGHEST,
    )
    listed = jnp.sum(selector, axis=1) > 0.5
    updated = jnp.where(listed[None], gathered, moved_flat)
    return updated.reshape(spectrum.shape)


def chunk_bounds():
    return [(5 * i, 5 * i + 5) for i in range(9)] + [(45, 47), (47, 49), (49, 50)]


HALO_GROUPS = ((0, 15), (15, 50))
SUM_CHUNKS = 3
SOURCES_DONE = {8: 2, 9: 5, 10: 7, 11: 9}
HALF_DIRS = NDIR // 2
SIDE_DIRS = 8
LEAD_DIRS = 9
VMEM_BYTES = 24 * 1024 * 1024
SMALL_COST = pl.CostEstimate(flops=1024, bytes_accessed=1024, transcendentals=0)


FREQ_STEP = (HIGH_FREQ / LOW_FREQ) ** (1.0 / (NFREQ - 1))


def frequency(index):
    return 2.0 * math.pi * LOW_FREQ * FREQ_STEP**index


def heading(index):
    return 2.0 * math.pi * index / NDIR


def raw_kernel(spec_ref, raw_ref, sems):
    copies = []
    for i, d in enumerate((0, HALF_DIRS - 1)):
        copy = pltpu.make_async_copy(spec_ref.at[d], raw_ref.at[i], sems.at[i])
        copy.start()
        copies.append(copy)
    for copy in copies:
        copy.wait()


def raw_edges(spec):
    return pl.pallas_call(
        raw_kernel,
        out_shape=jax.ShapeDtypeStruct((2, NFREQ, 8, 256), jnp.float32),
        in_specs=[pl.BlockSpec(memory_space=pl.ANY)],
        out_specs=pl.BlockSpec(memory_space=pltpu.VMEM),
        scratch_shapes=[pltpu.SemaphoreType.DMA((2,))],
        compiler_params=pltpu.CompilerParams(vmem_limit_bytes=VMEM_BYTES),
        cost_estimate=SMALL_COST,
    )(spec)


def pack_kernel(first, count, sea_ref, spec_ref, after_ref, lead_ref, trail_ref, lat_ref, held, sems):
    def body(flipped):
        lead_row, trail_row = (0, 7) if flipped else (7, 0)
        part = 0 if flipped else 1
        copies = []
        for d in range(HALF_DIRS):
            for h in range(2):
                place = h * HALF_DIRS + d
                copy = pltpu.make_async_copy(
                    spec_ref.at[pl.ds((d * NFREQ + first) * 8, count * 8), pl.ds(128 * h, 128)],
                    held.at[pl.ds(place * count * 8, count * 8)],
                    sems.at[place],
                )
                copy.start()
                copies.append(copy)
        for d in range(HALF_DIRS):
            for h in range(2):
                copies[2 * d + h].wait()
                lanes_here = slice(128 * h, 128 * h + 128)
                start = (h * HALF_DIRS + d) * count * 8
                if d < LEAD_DIRS:
                    column = held[pl.ds(start + lead_row, count, stride=8), :]
                    lead_ref[d * count : (d + 1) * count, lanes_here] = column * sea_ref[lead_row : lead_row + 1, lanes_here]
                elif d > LEAD_DIRS:
                    t = d - LEAD_DIRS - 1
                    column = held[pl.ds(start + trail_row, count, stride=8), :]
                    trail_ref[t * count : (t + 1) * count, lanes_here] = column * sea_ref[trail_row : trail_row + 1, lanes_here]
        lane = 0 if flipped else 127
        lanes = lax.broadcasted_iota(jnp.int32, (8, 128), 1)
        sea_line = jnp.broadcast_to(sea_ref[:, 128 * part + lane : 128 * part + lane + 1], (8, 128))

        def slab(d, f):
            return held[pl.ds(pl.multiple_of((part * HALF_DIRS + d) * count * 8 + f * 8, 8), 8), :]

        def one(f, kept):
            here = lanes == f
            return tuple(
                jnp.where(here, jnp.broadcast_to(slab(d, f)[:, lane : lane + 1], (8, 128)), kept[d])
                for d in range(HALF_DIRS)
            )

        zeros = jnp.zeros((8, 128), jnp.float32)
        kept = lax.fori_loop(0, count, one, (zeros,) * HALF_DIRS, unroll=5)
        for d in range(HALF_DIRS):
            lat_ref[d] = kept[d] * sea_line

    half = lax.axis_index("comp")

    @pl.when(half == 0)
    def _():
        body(False)

    @pl.when(half != 0)
    def _():
        body(True)


def pack(first, count, sea, spec, after):
    vmem = pl.BlockSpec(memory_space=pltpu.VMEM)
    hold = pl.BlockSpec(memory_space=pl.ANY)
    return pl.pallas_call(
        functools.partial(pack_kernel, first, count),
        out_shape=[
            jax.ShapeDtypeStruct((LEAD_DIRS * count, 256), jnp.float32),
            jax.ShapeDtypeStruct(((HALF_DIRS - LEAD_DIRS - 1) * count, 256), jnp.float32),
            jax.ShapeDtypeStruct((HALF_DIRS, 8, 128), jnp.float32),
        ],
        in_specs=[vmem, hold, hold],
        out_specs=[vmem] * 3,
        scratch_shapes=[
            pltpu.VMEM(((2 * HALF_DIRS + 1) * count * 8, 128), jnp.float32),
            pltpu.SemaphoreType.DMA((2 * HALF_DIRS,)),
        ],
        compiler_params=pltpu.CompilerParams(vmem_limit_bytes=VMEM_BYTES),
        cost_estimate=SMALL_COST,
    )(sea, spec, after)


ALL_DIRS = tuple(range(HALF_DIRS))
INNER_DIRS = ALL_DIRS[1:-1]
OUTER_DIRS = (0, HALF_DIRS - 1)


def is_sent(d):
    return d < SIDE_DIRS or d >= HALF_DIRS - SIDE_DIRS


def slab_index(dirs, count, base=0):
    return {d: base + count * n for n, d in enumerate(d for d in dirs if is_sent(d))}


def advect_kernel(
    group, passes, carries, waits, has_raw,
    sea_ref, slope_ref, spec_ref, lead_ref, trail_ref, lat_ref, steep_ref, *rest,
):
    sums = any(summed for *_, summed in passes)
    raw_ref = rest[0] if has_raw else None
    rest = rest[has_raw + waits :]
    held, turn, sem = rest[-3:]
    send_ref, keep_ref = rest[:2]
    if sums:
        steep_out_ref = rest[-4]
    copies, base = [], 0
    for i, (first, count, *_) in enumerate(passes):
        copy = pltpu.make_async_copy(spec_ref.at[:, pl.ds(first, count)], held.at[:, pl.ds(base, count)], sem.at[i])
        copy.start()
        copies.append(copy)
        base += count
    for d in range(HALF_DIRS):
        turn[d] = math.sin(heading(d)) * slope_ref[0] - math.cos(heading(d)) * slope_ref[1]
    if sums:
        steep_out_ref[...] = steep_ref[...]
    for copy in copies:
        copy.wait()
    rows_at = lax.broadcasted_iota(jnp.int32, (8, 256), 0)
    lanes_at = lax.broadcasted_iota(jnp.int32, (8, 256), 1)
    per_cell = TIME_STEP / CELL_SIZE * GRAVITY / 2.0
    bending = TIME_STEP * NDIR / (2.0 * math.pi) * (2.0 * math.pi * LOW_FREQ)
    group_count = group[1] - group[0]

    def body(flipped):
        lead_row, lead_shift = (7, 7) if flipped else (0, 1)
        trail_row, trail_shift = (0, 1) if flipped else (7, 7)
        lat_lane, lat_shift = (255, 255) if flipped else (0, 1)

        def one(first, dirs, slabs, summed, base, f, factors):
            sea = sea_ref[...]
            inverse, weight = factors
            total = jnp.zeros((8, 256), jnp.float32)
            offset = first - group[0]

            def energy(d):
                if d < 0:
                    return raw_ref[1, first + f] * sea
                if d >= HALF_DIRS:
                    return raw_ref[0, first + f] * sea
                return held[d, base + f] * sea

            known = {}
            for d in dirs:
                known = {e: known[e] if e in known else energy(e) for e in (d - 1, d, d + 1)}
                prev, here, after = known[d - 1], known[d], known[d + 1]
                rate = turn[d]
                size = jnp.abs(rate) * bending
                moved = size * jnp.where(rate > 0.0, prev, after)
                along_x = per_cell * abs(math.cos(heading(d)))
                along_y = per_cell * abs(math.sin(heading(d)))
                fixed = 0.0
                if d != LEAD_DIRS:
                    if d < LEAD_DIRS:
                        row = lead_ref[pl.ds(d * group_count + offset + f, 1), :]
                        edge, shift = lead_row, lead_shift
                    else:
                        row = trail_ref[pl.ds((d - LEAD_DIRS - 1) * group_count + offset + f, 1), :]
                        edge, shift = trail_row, trail_shift
                    side = jnp.where(rows_at == edge, jnp.broadcast_to(row, (8, 256)), pltpu.roll(here, shift, 0))
                    moved = moved + along_x * side
                    fixed += along_x
                if d != 0:
                    halo = pltpu.roll(lat_ref[d], lax.rem((lat_lane % 128) + 128 - (offset + f), 128), 1)
                    halo = jnp.concatenate([halo, halo], axis=1)
                    side = jnp.where(lanes_at == lat_lane, halo, pltpu.roll(here, lat_shift, 1))
                    moved = moved + along_y * side
                    fixed += along_y
                result = (here - inverse * ((size + fixed) * here - moved)) * sea
                if slabs is not None and is_sent(d):
                    send_ref[slabs[d] + f] = result
                elif slabs is not None:
                    keep_ref[d - SIDE_DIRS, f] = result
                total = total + result
            if summed:
                steep_out_ref[...] += weight * total
            return inverse * (1.0 / FREQ_STEP), weight * FREQ_STEP**2

        base = 0
        for first, count, dirs, slabs, summed in passes:
            factors = jnp.float32(1.0 / frequency(first)), jnp.float32((frequency(first) / frequency(NFREQ - 1)) ** 2)
            lax.fori_loop(0, count, functools.partial(one, first, dirs, slabs, summed, base), factors)
            base += count

    half = lax.axis_index("comp")

    @pl.when(half == 0)
    def _():
        body(False)

    @pl.when(half != 0)
    def _():
        body(True)

    if carries:
        send_ref[send_ref.shape[0] - 1] = steep_out_ref[...]


def advect_chunk(passes, group, carries, sea, slopes, spec, sides, steep, raw, after):
    vmem = pl.BlockSpec(memory_space=pltpu.VMEM)
    hold = pl.BlockSpec(memory_space=pl.ANY)
    slabs = sum(count * len(place) for _, count, _, place, _ in passes if place is not None)
    raw = () if raw is None else (raw,)
    out_shape = [
        jax.ShapeDtypeStruct((slabs + carries, 8, 256), jnp.float32),
        jax.ShapeDtypeStruct((HALF_DIRS - 2 * SIDE_DIRS, passes[0][1], 8, 256), jnp.float32),
    ]
    if any(summed for *_, summed in passes):
        out_shape.append(jax.ShapeDtypeStruct((8, 256), jnp.float32))
    return pl.pallas_call(
        functools.partial(advect_kernel, group, passes, carries, len(after), len(raw)),
        out_shape=out_shape,
        in_specs=[vmem, vmem, hold, vmem, vmem, vmem, vmem] + [vmem] * len(raw) + [hold] * len(after),
        out_specs=[vmem] * len(out_shape),
        scratch_shapes=[
            pltpu.VMEM((HALF_DIRS, sum(p[1] for p in passes), 8, 256), jnp.float32),
            pltpu.VMEM((HALF_DIRS, 8, 256), jnp.float32),
            pltpu.SemaphoreType.DMA((len(passes),)),
        ],
        compiler_params=pltpu.CompilerParams(vmem_limit_bytes=VMEM_BYTES),
        cost_estimate=SMALL_COST,
    )(sea, slopes, spec, *sides, steep, *raw, *after)


def source_kernel(
    first, count, inner, outer, chained, last,
    wind_ref, steep_a_ref, steep_b_ref, cum_ref, own_ref, keep_ref, other_ref, *rest,
):
    edge_own_ref, edge_other_ref = rest[:2] if outer else (None, None)
    rest = rest[(2 if outer else 0) + chained :]
    single = last and count == 1
    if single:
        out_ref, result, sems = rest
    else:
        out_ref, cum_out_ref, result, align, sems = rest
    weights = [math.cos(heading(m)) ** 2 / (9.0 * SATURATION_LEVEL) for m in range(SIDE_DIRS + 1)]
    steep = (steep_a_ref[...] + steep_b_ref[...]) * (1.0 / (NDIR * NFREQ))
    steep_sq = steep * steep
    if not single:
        for d in range(HALF_DIRS):
            align[d] = math.cos(heading(d)) * wind_ref[0] + math.sin(heading(d)) * wind_ref[1]
        cum_out_ref[...] = cum_ref[...]

    def leave(f, half):
        lanes = pl.ds(128 * half, 128)
        return pltpu.make_async_copy(result.at[:, f, :, lanes], out_ref.at[:, first + f, :, lanes], sems.at[f, half])

    def one(f, omega):
        gain = TIME_STEP * WIND_GROWTH * omega
        loss_sat = TIME_STEP * SATURATION_LOSS * omega
        loss_cum = TIME_STEP * CUMULATIVE_LOSS / NFREQ * omega
        loss_steep = TIME_STEP * STEEPNESS_LOSS * omega
        for half in range(2):
            lanes = slice(128 * half, 128 * half + 128)

            def slab(d, main, edge):
                return main[inner[d] + f, :, lanes] if d in inner else edge[outer[d] + f, :, lanes]

            first_dirs, last_dirs = ALL_DIRS[:SIDE_DIRS], ALL_DIRS[-SIDE_DIRS:]
            line = [slab(d, other_ref, edge_other_ref) for d in last_dirs]
            line += [slab(d, own_ref, edge_own_ref) for d in first_dirs]
            line += [keep_ref[i, f, :, lanes] for i in range(HALF_DIRS - 2 * SIDE_DIRS)]
            line += [slab(d, own_ref, edge_own_ref) for d in last_dirs]
            line += [slab(d, other_ref, edge_other_ref) for d in first_dirs]
            base = 1.0 + loss_steep * steep_sq[:, lanes]
            for d in range(HALF_DIRS):
                at = d + SIDE_DIRS
                level = weights[0] * line[at] - 1.0
                for m in range(1, SIDE_DIRS + 1):
                    level = level + weights[m] * (line[at - m] + line[at + m])
                excess = jnp.maximum(level, 0.0)
                square = excess * excess
                if single:
                    cum = cum_ref[d, :, lanes]
                    along = math.cos(heading(d)) * wind_ref[0, :, lanes] + math.sin(heading(d)) * wind_ref[1, :, lanes]
                else:
                    cum = cum_out_ref[d, :, lanes]
                    cum_out_ref[d, :, lanes] = cum + square
                    along = align[d, :, lanes]
                grown = 1.0 + gain * jnp.maximum(along * omega - 1.0, 0.0)
                lost = base + loss_sat * square + loss_cum * cum
                result[d, f, :, lanes] = line[at] * grown / lost
            leave(f, half).start()
        return omega * FREQ_STEP

    if single:
        one(0, jnp.float32(frequency(first)))
    else:
        lax.fori_loop(0, count, one, jnp.float32(frequency(first)))
    for f in range(count):
        for half in range(2):
            leave(f, half).wait()


def source_chunk(first, count, inner, outer, last, wind, steep_own, steep_other, cum, own, keep, other, edges, out):
    vmem = pl.BlockSpec(memory_space=pltpu.VMEM)
    hold = pl.BlockSpec(memory_space=pl.ANY)
    chained = out is not None
    operands = (wind, steep_own, steep_other, cum, own, keep, other, *edges) + ((out,) if chained else ())
    out_shape = [jax.ShapeDtypeStruct((HALF_DIRS, NFREQ, 8, 256), jnp.float32)]
    single = last and count == 1
    running = [] if last else [jax.ShapeDtypeStruct((HALF_DIRS, 8, 256), jnp.float32)]
    result = pl.pallas_call(
        functools.partial(source_kernel, first, count, inner, outer, chained, last),
        out_shape=out_shape + running,
        in_specs=[vmem] * (7 + len(edges)) + [hold] * chained,
        out_specs=[hold] + [vmem] * len(running),
        scratch_shapes=[pltpu.VMEM((HALF_DIRS, 8, 256), jnp.float32)] * (last and not single)
        + [pltpu.VMEM((HALF_DIRS, count, 8, 256), jnp.float32)]
        + [pltpu.VMEM((HALF_DIRS, 8, 256), jnp.float32)] * (not single)
        + [pltpu.SemaphoreType.DMA((count, 2))],
        input_output_aliases={len(operands) - 1: 0} if chained else {},
        compiler_params=pltpu.CompilerParams(vmem_limit_bytes=VMEM_BYTES),
        cost_estimate=SMALL_COST,
    )(*operands)
    return result[0], None if last else result[1]


def ring_pairs(size, step, wrap):
    return [(i, (i + step) % size) for i in range(size) if wrap or 0 <= i + step < size]


def paired_shards(spectrum, sea_mask, owner_list, owner_count, slopes, friction, wind_angle):
    tiles_x, tiles_y = lax.axis_size("tx"), lax.axis_size("ty")
    half = lax.axis_index("comp")
    sign = 1.0 - 2.0 * half.astype(jnp.float32)
    spec = spectrum.reshape(HALF_DIRS, NFREQ, 8, 256)
    sea = sea_mask.astype(jnp.float32)
    turn = slopes * sign
    wind = (sign * WIND_FACTOR / GRAVITY) * friction * jnp.stack([jnp.cos(wind_angle), jnp.sin(wind_angle)])

    def joined(axis_size, step, wrap):
        ahead = ring_pairs(axis_size, step, wrap)
        back = ring_pairs(axis_size, -step, wrap)
        return ahead + [(axis_size + i, axis_size + j) for i, j in back]

    swap = [(0, 1), (1, 0)]
    lead_pairs = joined(tiles_x, 1, True)
    trail_pairs = joined(tiles_x, -1, True)
    lat_pairs = joined(tiles_y, 1, False)

    rows = pltpu.with_memory_space_constraint(spectrum.reshape(HALF_DIRS * NFREQ * 8, 256), pltpu.HBM)
    spec = pltpu.with_memory_space_constraint(spec, pltpu.HBM)
    bounds = chunk_bounds()
    raw = raw_edges(spec)

    def halo(g, after):
        begin, end = HALO_GROUPS[g]
        lead, trail, lat = pack(begin, end - begin, sea, rows, after)
        sides = (
            lax.ppermute(lead, ("comp", "tx"), lead_pairs),
            lax.ppermute(trail, ("comp", "tx"), trail_pairs),
            lax.ppermute(lat, ("comp", "ty"), lat_pairs),
        )
        return sides, lead

    first_sides, _ = halo(0, raw)
    raw = lax.ppermute(raw, "comp", swap)
    early = sum(end <= HALO_GROUPS[0][1] for _, end in bounds)
    counts = [end - begin for begin, end in bounds]
    places = [slab_index(INNER_DIRS if i == 0 else ALL_DIRS, counts[i]) for i in range(len(bounds))]
    edge_place = slab_index(OUTER_DIRS, counts[0], base=2 * SIDE_DIRS * counts[1])

    def advect(passes, sides, carries, steep, raw, after):
        group = HALO_GROUPS[0] if sides is first_sides else HALO_GROUPS[1]
        return advect_chunk(passes, group, carries, sea, turn, spec, sides, steep, raw, after)

    sent, kept, received, sums = [], [], [], []

    def send(result):
        sent.append(result[0])
        kept.append(result[1])
        received.append(lax.ppermute(result[0], "comp", swap))

    def source(upto):
        for j in range(len(sums), upto):
            outer, edges = (edge_place, (sent[1], received[1])) if j == 0 else (None, ())
            state[:] = source_chunk(
                bounds[j][0], counts[j], places[j], outer, j == len(bounds) - 1, wind, steep, steep_other,
                state[1], sent[j], kept[j], received[j], edges, state[0],
            )
            sums.append(state[1])

    steep = jnp.zeros((8, 256), jnp.float32)
    for i in range(early):
        passes = [(bounds[i][0], counts[i], INNER_DIRS if i == 0 else ALL_DIRS, places[i], True)]
        after = ()
        if i == 1:
            passes.append((bounds[0][0], counts[0], OUTER_DIRS, edge_place, True))
        if i >= 2:
            after = (received[i - 2], packed)
        result = advect(passes, first_sides, False, steep, raw if i else None, after)
        send(result)
        steep = result[2]
        if i == 1:
            later_sides, packed = halo(1, steep)
    state = [None, jnp.zeros((HALF_DIRS, 8, 256), jnp.float32)]
    summing = SUM_CHUNKS
    ahead = bounds[early + summing][0]
    cuts = [ahead + (NFREQ - ahead) * n // summing for n in range(summing + 1)]
    for i in range(early, len(bounds)):
        after = (received[i - 2],)
        if i in SOURCES_DONE:
            source(SOURCES_DONE[i])
            after += (sums[-1],)
        n = i - early
        passes = [(bounds[i][0], counts[i], ALL_DIRS, places[i], n < summing)]
        if n < summing:
            passes.append((cuts[n], cuts[n + 1] - cuts[n], ALL_DIRS, None, True))
        result = advect(passes, later_sides, n == summing - 1, steep, raw, after)
        send(result)
        if n < summing:
            steep = result[2]
        if n == summing - 1:
            steep_other = received[i][-1]
    source(len(bounds))
    out = state[0]
    return out.reshape(spectrum.shape)


def fits_pairs(mesh, spectrum):
    return (
        mesh.shape["comp"] == 2
        and spectrum.shape[0] == NDIR * NFREQ
        and spectrum.shape[1] == 8 * mesh.shape["tx"]
        and spectrum.shape[2] == 256 * mesh.shape["ty"]
    )


def solution(mesh):
    in_specs = (
        P("comp", "tx", "ty"),
        P("tx", "ty"),
        P("tx", "ty", None, None),
        P("tx", "ty", None),
        P(None, "tx", "ty"),
        P("tx", "ty"),
        P("tx", "ty"),
    )
    out_specs = P("comp", "tx", "ty")

    def step(spectrum, *others):
        body = paired_shards if fits_pairs(mesh, spectrum) else shards
        mapped = jax.shard_map(body, mesh=mesh, in_specs=in_specs, out_specs=out_specs, check_vma=False)
        return mapped(spectrum, *others)

    return step
```

```python
import functools
import math

import jax
import jax.numpy as jnp
from jax import lax
from jax.experimental import pallas as pl
from jax.experimental.pallas import tpu as pltpu
from jax.sharding import PartitionSpec as P

NDIR = 36
NFREQ = 50


TIME_STEP = 240.0
CELL_SIZE = 11100.0
GRAVITY = 9.81
LOW_FREQ = 0.0373
HIGH_FREQ = 1.0
WIND_GROWTH = 0.0001
WIND_FACTOR = 28.0
SATURATION_LOSS = 0.0005
CUMULATIVE_LOSS = 0.001
STEEPNESS_LOSS = 0.005
SATURATION_LEVEL = 0.6


def padded(value, sides, width, wrap):
    for axis, dim in sides:
        size, length = (lax.axis_size(axis), value.shape[dim])
        up = [(i, (i + 1) % size) for i in range(size if wrap else size - 1)]
        down = [(j, i) for i, j in up]
        last = lax.slice_in_dim(value, length - width, length, axis=dim)
        first = lax.slice_in_dim(value, 0, width, axis=dim)
        before = lax.ppermute(last, axis, up)
        after = lax.ppermute(first, axis, down)
        value = jnp.concatenate([before, value, after], axis=dim)
    return value


def freq_values(freq_ids):
    return (
        2.0
        * math.pi
        * LOW_FREQ
        * jnp.exp(freq_ids.astype(jnp.float32) * (math.log(HIGH_FREQ / LOW_FREQ) / (NFREQ - 1)))
    )


def wave_tables(first_comp, comp_count):
    comp_ids = first_comp + jnp.arange(comp_count, dtype=jnp.int32)
    headings = (comp_ids // NFREQ).astype(jnp.float32) * (2.0 * math.pi / NDIR)
    return (headings, freq_values(comp_ids % NFREQ))


def advect(
    energy,
    west_side,
    east_side,
    south_side,
    north_side,
    prev_dir,
    next_dir,
    headings,
    ang_freq,
    slopes,
):
    group_speed = GRAVITY / (2.0 * ang_freq)
    along_x = (TIME_STEP / CELL_SIZE * group_speed * jnp.cos(headings))[:, None, None]
    along_y = (TIME_STEP / CELL_SIZE * group_speed * jnp.sin(headings))[:, None, None]
    bending = TIME_STEP * NDIR / (2.0 * math.pi) * (2.0 * math.pi * LOW_FREQ) / ang_freq
    turning = bending[:, None, None] * (
        jnp.sin(headings)[:, None, None] * slopes[0][None]
        - jnp.cos(headings)[:, None, None] * slopes[1][None]
    )
    change = jnp.maximum(along_x, 0.0) * (energy - west_side) + jnp.minimum(along_x, 0.0) * (
        east_side - energy
    )
    change = (
        change
        + jnp.maximum(along_y, 0.0) * (energy - south_side)
        + jnp.minimum(along_y, 0.0) * (north_side - energy)
    )
    change = (
        change
        + jnp.maximum(turning, 0.0) * (energy - prev_dir)
        + jnp.minimum(turning, 0.0) * (next_dir - energy)
    )
    return energy - change


def source_terms(spectra, friction, wind_angle):
    dir_ids = jnp.arange(NDIR, dtype=jnp.int32)
    offset = (dir_ids[:, None] - dir_ids[None, :]) % NDIR
    nearest = jnp.minimum(offset, NDIR - offset)
    spread = jnp.where(
        4 * nearest < NDIR, jnp.cos(offset.astype(jnp.float32) * (2.0 * math.pi / NDIR)) ** 2, 0.0
    )
    spread = spread / jnp.sum(spread, axis=1, keepdims=True)
    sat_level = jnp.einsum("de,efp->dfp", spread, spectra, precision=lax.Precision.HIGHEST)
    excess = jnp.maximum(sat_level / SATURATION_LEVEL - 1.0, 0.0)
    excess_sq = excess * excess
    freq_ids = jnp.arange(NFREQ, dtype=jnp.int32)
    below_mask = (freq_ids[None, :] < freq_ids[:, None]).astype(jnp.float32)
    running = (
        jnp.einsum("fg,dgp->dfp", below_mask, excess_sq, precision=lax.Precision.HIGHEST) / NFREQ
    )
    ang_freq = freq_values(freq_ids)
    weights = (ang_freq / ang_freq[NFREQ - 1]) ** 2
    steepness = jnp.einsum("dfp,f->p", spectra, weights, precision=lax.Precision.HIGHEST) / (
        NDIR * NFREQ
    )
    headings = dir_ids.astype(jnp.float32) * (2.0 * math.pi / NDIR)
    alignment = (
        jnp.cos(headings)[:, None, None] * jnp.cos(wind_angle)[None, None, :]
        + jnp.sin(headings)[:, None, None] * jnp.sin(wind_angle)[None, None, :]
    )
    forcing = WIND_FACTOR / GRAVITY * friction[None, None, :] * ang_freq[None, :, None] * alignment
    growth = WIND_GROWTH * ang_freq[None, :, None] * jnp.maximum(forcing - 1.0, 0.0)
    losses = ang_freq[None, :, None] * (
        SATURATION_LOSS * excess_sq
        + CUMULATIVE_LOSS * running
        + STEEPNESS_LOSS * (steepness * steepness)[None, None, :]
    )
    return spectra * (1.0 + TIME_STEP * growth) / (1.0 + TIME_STEP * losses)


def shards(spectrum, sea_mask, owner_list, owner_count, slopes, friction, wind_angle):
    comp_size = lax.axis_size("comp")
    local_comps = spectrum.shape[0]
    cell_count = spectrum.shape[1] * spectrum.shape[2]
    sea_cells = sea_mask.astype(jnp.float32)
    masked = spectrum * sea_cells[None]
    headings, ang_freq = wave_tables(lax.axis_index("comp") * local_comps, local_comps)
    padded_lon = padded(masked, (("tx", 1),), 1, True)
    padded_lat = padded(masked, (("ty", 2),), 1, False)
    padded_dir = padded(masked, (("comp", 0),), NFREQ, True)
    advected = (
        advect(
            masked,
            padded_lon[:, :-2],
            padded_lon[:, 2:],
            padded_lat[:, :, :-2],
            padded_lat[:, :, 2:],
            padded_dir[:local_comps],
            padded_dir[2 * NFREQ :],
            headings,
            ang_freq,
            slopes,
        )
        * sea_cells[None]
    )
    moved_flat = advected.reshape(local_comps, cell_count)
    cell_names = owner_list[0, 0]
    slot_ids = jnp.arange(cell_names.shape[1], dtype=jnp.int32)
    in_use = slot_ids[None, :] < owner_count[0, 0][:, None]
    target = jnp.where(in_use, cell_names, cell_count).reshape(-1)
    owners = cell_names.shape[0]
    capacity = cell_names.shape[1]
    tiles_x = lax.axis_size("tx")
    cell_ids = jnp.arange(cell_count, dtype=jnp.int32)
    selector = (cell_ids[:, None] == target[None, :]).astype(jnp.float32)
    outgoing = jnp.dot(moved_flat, selector, precision=lax.Precision.HIGHEST).reshape(
        local_comps, owners, capacity
    )
    wind_rows = jnp.stack([friction.reshape(-1), wind_angle.reshape(-1)])
    point_data = jnp.dot(wind_rows, selector, precision=lax.Precision.HIGHEST).reshape(
        2, owners, capacity
    )
    spectra = lax.all_to_all(outgoing, ("comp", "tx"), split_axis=1, concat_axis=1, tiled=True)
    extras = lax.all_to_all(point_data, ("comp", "tx"), split_axis=1, concat_axis=1, tiled=True)
    batch_size = spectra.shape[2]
    full_spec = (
        spectra.reshape(local_comps, comp_size, tiles_x * batch_size)
        .transpose(1, 0, 2)
        .reshape(NDIR, NFREQ, tiles_x * batch_size)
    )
    extra_rows = extras.reshape(2, comp_size, tiles_x * batch_size)[:, 0]
    result = source_terms(full_spec, extra_rows[0], extra_rows[1])
    homeward = (
        result.reshape(comp_size, local_comps, tiles_x * batch_size)
        .transpose(1, 0, 2)
        .reshape(local_comps, comp_size * tiles_x, batch_size)
    )
    returned = lax.all_to_all(homeward, ("comp", "tx"), split_axis=1, concat_axis=1, tiled=True)
    gathered = lax.dot_general(
        returned.reshape(local_comps, owners * capacity),
        selector,
        (((1,), (1,)), ((), ())),
        precision=lax.Precision.HIGHEST,
    )
    listed = jnp.sum(selector, axis=1) > 0.5
    updated = jnp.where(listed[None], gathered, moved_flat)
    return updated.reshape(spectrum.shape)


def chunk_bounds():
    return [(5 * i, 5 * i + 5) for i in range(6)] + [(30, 40), (40, 45), (45, 47), (47, 49), (49, 50)]


HALO_GROUPS = ((0, 15), (15, 50))
SUM_CHUNKS = 3
SOURCES_DONE = {8: 5, 9: 7, 10: 8}
HALF_DIRS = NDIR // 2
SIDE_DIRS = 8
LEAD_DIRS = 9
VMEM_BYTES = 24 * 1024 * 1024
SMALL_COST = pl.CostEstimate(flops=1024, bytes_accessed=1024, transcendentals=0)


FREQ_STEP = (HIGH_FREQ / LOW_FREQ) ** (1.0 / (NFREQ - 1))


def frequency(index):
    return 2.0 * math.pi * LOW_FREQ * FREQ_STEP**index


def heading(index):
    return 2.0 * math.pi * index / NDIR


def raw_kernel(spec_ref, raw_ref, sems):
    copies = []
    for i, d in enumerate((0, HALF_DIRS - 1)):
        copy = pltpu.make_async_copy(spec_ref.at[d], raw_ref.at[i], sems.at[i])
        copy.start()
        copies.append(copy)
    for copy in copies:
        copy.wait()


def raw_edges(spec):
    return pl.pallas_call(
        raw_kernel,
        out_shape=jax.ShapeDtypeStruct((2, NFREQ, 8, 256), jnp.float32),
        in_specs=[pl.BlockSpec(memory_space=pl.ANY)],
        out_specs=pl.BlockSpec(memory_space=pltpu.VMEM),
        scratch_shapes=[pltpu.SemaphoreType.DMA((2,))],
        compiler_params=pltpu.CompilerParams(vmem_limit_bytes=VMEM_BYTES),
        cost_estimate=SMALL_COST,
    )(spec)


def pack_kernel(first, count, sea_ref, spec_ref, after_ref, lead_ref, trail_ref, lat_ref, held, sems):
    def body(flipped):
        lead_row, trail_row = (0, 7) if flipped else (7, 0)
        part = 0 if flipped else 1
        copies = []
        for d in range(HALF_DIRS):
            for h in range(2):
                place = h * HALF_DIRS + d
                copy = pltpu.make_async_copy(
                    spec_ref.at[pl.ds((d * NFREQ + first) * 8, count * 8), pl.ds(128 * h, 128)],
                    held.at[pl.ds(place * count * 8, count * 8)],
                    sems.at[place],
                )
                copy.start()
                copies.append(copy)
        for d in range(HALF_DIRS):
            for h in range(2):
                copies[2 * d + h].wait()
                lanes_here = slice(128 * h, 128 * h + 128)
                start = (h * HALF_DIRS + d) * count * 8
                if d < LEAD_DIRS:
                    column = held[pl.ds(start + lead_row, count, stride=8), :]
                    lead_ref[d * count : (d + 1) * count, lanes_here] = column * sea_ref[lead_row : lead_row + 1, lanes_here]
                elif d > LEAD_DIRS:
                    t = d - LEAD_DIRS - 1
                    column = held[pl.ds(start + trail_row, count, stride=8), :]
                    trail_ref[t * count : (t + 1) * count, lanes_here] = column * sea_ref[trail_row : trail_row + 1, lanes_here]
        lane = 0 if flipped else 127
        lanes = lax.broadcasted_iota(jnp.int32, (8, 128), 1)
        sea_line = jnp.broadcast_to(sea_ref[:, 128 * part + lane : 128 * part + lane + 1], (8, 128))

        def slab(d, f):
            return held[pl.ds(pl.multiple_of((part * HALF_DIRS + d) * count * 8 + f * 8, 8), 8), :]

        def one(f, kept):
            here = lanes == f
            return tuple(
                jnp.where(here, jnp.broadcast_to(slab(d, f)[:, lane : lane + 1], (8, 128)), kept[d])
                for d in range(HALF_DIRS)
            )

        zeros = jnp.zeros((8, 128), jnp.float32)
        kept = lax.fori_loop(0, count, one, (zeros,) * HALF_DIRS, unroll=5)
        for d in range(HALF_DIRS):
            lat_ref[d] = kept[d] * sea_line

    half = lax.axis_index("comp")

    @pl.when(half == 0)
    def _():
        body(False)

    @pl.when(half != 0)
    def _():
        body(True)


def pack(first, count, sea, spec, after):
    vmem = pl.BlockSpec(memory_space=pltpu.VMEM)
    hold = pl.BlockSpec(memory_space=pl.ANY)
    return pl.pallas_call(
        functools.partial(pack_kernel, first, count),
        out_shape=[
            jax.ShapeDtypeStruct((LEAD_DIRS * count, 256), jnp.float32),
            jax.ShapeDtypeStruct(((HALF_DIRS - LEAD_DIRS - 1) * count, 256), jnp.float32),
            jax.ShapeDtypeStruct((HALF_DIRS, 8, 128), jnp.float32),
        ],
        in_specs=[vmem, hold, hold],
        out_specs=[vmem] * 3,
        scratch_shapes=[
            pltpu.VMEM(((2 * HALF_DIRS + 1) * count * 8, 128), jnp.float32),
            pltpu.SemaphoreType.DMA((2 * HALF_DIRS,)),
        ],
        compiler_params=pltpu.CompilerParams(vmem_limit_bytes=VMEM_BYTES),
        cost_estimate=SMALL_COST,
    )(sea, spec, after)


ALL_DIRS = tuple(range(HALF_DIRS))
INNER_DIRS = ALL_DIRS[1:-1]
OUTER_DIRS = (0, HALF_DIRS - 1)


def is_sent(d):
    return d < SIDE_DIRS or d >= HALF_DIRS - SIDE_DIRS


def slab_index(dirs, count, base=0):
    return {d: base + count * n for n, d in enumerate(d for d in dirs if is_sent(d))}


def advect_kernel(
    group, passes, carries, waits, has_raw,
    sea_ref, slope_ref, spec_ref, lead_ref, trail_ref, lat_ref, steep_ref, *rest,
):
    sums = any(summed for *_, summed in passes)
    raw_ref = rest[0] if has_raw else None
    rest = rest[has_raw + waits :]
    held, turn, sem = rest[-3:]
    send_ref, keep_ref = rest[:2]
    if sums:
        steep_out_ref = rest[-4]
    copies, base = [], 0
    for i, (first, count, *_) in enumerate(passes):
        copy = pltpu.make_async_copy(spec_ref.at[:, pl.ds(first, count)], held.at[:, pl.ds(base, count)], sem.at[i])
        copy.start()
        copies.append(copy)
        base += count
    for d in range(HALF_DIRS):
        turn[d] = math.sin(heading(d)) * slope_ref[0] - math.cos(heading(d)) * slope_ref[1]
    if sums:
        steep_out_ref[...] = steep_ref[...]
    for copy in copies:
        copy.wait()
    rows_at = lax.broadcasted_iota(jnp.int32, (8, 256), 0)
    lanes_at = lax.broadcasted_iota(jnp.int32, (8, 256), 1)
    per_cell = TIME_STEP / CELL_SIZE * GRAVITY / 2.0
    bending = TIME_STEP * NDIR / (2.0 * math.pi) * (2.0 * math.pi * LOW_FREQ)
    group_count = group[1] - group[0]

    def body(flipped):
        lead_row, lead_shift = (7, 7) if flipped else (0, 1)
        trail_row, trail_shift = (0, 1) if flipped else (7, 7)
        lat_lane, lat_shift = (255, 255) if flipped else (0, 1)

        def one(first, dirs, slabs, summed, base, f, factors):
            sea = sea_ref[...]
            inverse, weight = factors
            total = jnp.zeros((8, 256), jnp.float32)
            offset = first - group[0]

            def energy(d):
                if d < 0:
                    return raw_ref[1, first + f] * sea
                if d >= HALF_DIRS:
                    return raw_ref[0, first + f] * sea
                return held[d, base + f] * sea

            known = {}
            for d in dirs:
                known = {e: known[e] if e in known else energy(e) for e in (d - 1, d, d + 1)}
                prev, here, after = known[d - 1], known[d], known[d + 1]
                rate = turn[d]
                size = jnp.abs(rate) * bending
                moved = size * jnp.where(rate > 0.0, prev, after)
                along_x = per_cell * abs(math.cos(heading(d)))
                along_y = per_cell * abs(math.sin(heading(d)))
                fixed = 0.0
                if d != LEAD_DIRS:
                    if d < LEAD_DIRS:
                        row = lead_ref[pl.ds(d * group_count + offset + f, 1), :]
                        edge, shift = lead_row, lead_shift
                    else:
                        row = trail_ref[pl.ds((d - LEAD_DIRS - 1) * group_count + offset + f, 1), :]
                        edge, shift = trail_row, trail_shift
                    side = jnp.where(rows_at == edge, jnp.broadcast_to(row, (8, 256)), pltpu.roll(here, shift, 0))
                    moved = moved + along_x * side
                    fixed += along_x
                if d != 0:
                    halo = pltpu.roll(lat_ref[d], lax.rem((lat_lane % 128) + 128 - (offset + f), 128), 1)
                    halo = jnp.concatenate([halo, halo], axis=1)
                    side = jnp.where(lanes_at == lat_lane, halo, pltpu.roll(here, lat_shift, 1))
                    moved = moved + along_y * side
                    fixed += along_y
                result = (here - inverse * ((size + fixed) * here - moved)) * sea
                if slabs is not None and is_sent(d):
                    send_ref[slabs[d] + f] = result
                elif slabs is not None:
                    keep_ref[d - SIDE_DIRS, f] = result
                total = total + result
            if summed:
                steep_out_ref[...] += weight * total
            return inverse * (1.0 / FREQ_STEP), weight * FREQ_STEP**2

        base = 0
        for first, count, dirs, slabs, summed in passes:
            factors = jnp.float32(1.0 / frequency(first)), jnp.float32((frequency(first) / frequency(NFREQ - 1)) ** 2)
            lax.fori_loop(0, count, functools.partial(one, first, dirs, slabs, summed, base), factors)
            base += count

    half = lax.axis_index("comp")

    @pl.when(half == 0)
    def _():
        body(False)

    @pl.when(half != 0)
    def _():
        body(True)

    if carries:
        send_ref[send_ref.shape[0] - 1] = steep_out_ref[...]


def advect_chunk(passes, group, carries, sea, slopes, spec, sides, steep, raw, after):
    vmem = pl.BlockSpec(memory_space=pltpu.VMEM)
    hold = pl.BlockSpec(memory_space=pl.ANY)
    slabs = sum(count * len(place) for _, count, _, place, _ in passes if place is not None)
    raw = () if raw is None else (raw,)
    out_shape = [
        jax.ShapeDtypeStruct((slabs + carries, 8, 256), jnp.float32),
        jax.ShapeDtypeStruct((HALF_DIRS - 2 * SIDE_DIRS, passes[0][1], 8, 256), jnp.float32),
    ]
    if any(summed for *_, summed in passes):
        out_shape.append(jax.ShapeDtypeStruct((8, 256), jnp.float32))
    return pl.pallas_call(
        functools.partial(advect_kernel, group, passes, carries, len(after), len(raw)),
        out_shape=out_shape,
        in_specs=[vmem, vmem, hold, vmem, vmem, vmem, vmem] + [vmem] * len(raw) + [hold] * len(after),
        out_specs=[vmem] * len(out_shape),
        scratch_shapes=[
            pltpu.VMEM((HALF_DIRS, sum(p[1] for p in passes), 8, 256), jnp.float32),
            pltpu.VMEM((HALF_DIRS, 8, 256), jnp.float32),
            pltpu.SemaphoreType.DMA((len(passes),)),
        ],
        compiler_params=pltpu.CompilerParams(vmem_limit_bytes=VMEM_BYTES),
        cost_estimate=SMALL_COST,
    )(sea, slopes, spec, *sides, steep, *raw, *after)


def source_kernel(
    first, count, inner, outer, chained, last,
    wind_ref, steep_a_ref, steep_b_ref, cum_ref, own_ref, keep_ref, other_ref, *rest,
):
    edge_own_ref, edge_other_ref = rest[:2] if outer else (None, None)
    rest = rest[(2 if outer else 0) + chained :]
    single = last and count == 1
    if single:
        out_ref, result, sems = rest
    else:
        out_ref, cum_out_ref, result, align, sems = rest
    weights = [math.cos(heading(m)) ** 2 / (9.0 * SATURATION_LEVEL) for m in range(SIDE_DIRS + 1)]
    steep = (steep_a_ref[...] + steep_b_ref[...]) * (1.0 / (NDIR * NFREQ))
    steep_sq = steep * steep
    if not single:
        for d in range(HALF_DIRS):
            align[d] = math.cos(heading(d)) * wind_ref[0] + math.sin(heading(d)) * wind_ref[1]
        cum_out_ref[...] = cum_ref[...]

    def leave(f, half):
        lanes = pl.ds(128 * half, 128)
        return pltpu.make_async_copy(result.at[:, f, :, lanes], out_ref.at[:, first + f, :, lanes], sems.at[f, half])

    def one(f, omega):
        gain = TIME_STEP * WIND_GROWTH * omega
        loss_sat = TIME_STEP * SATURATION_LOSS * omega
        loss_cum = TIME_STEP * CUMULATIVE_LOSS / NFREQ * omega
        loss_steep = TIME_STEP * STEEPNESS_LOSS * omega
        for half in range(2):
            lanes = slice(128 * half, 128 * half + 128)

            def slab(d, main, edge):
                return main[inner[d] + f, :, lanes] if d in inner else edge[outer[d] + f, :, lanes]

            first_dirs, last_dirs = ALL_DIRS[:SIDE_DIRS], ALL_DIRS[-SIDE_DIRS:]
            line = [slab(d, other_ref, edge_other_ref) for d in last_dirs]
            line += [slab(d, own_ref, edge_own_ref) for d in first_dirs]
            line += [keep_ref[i, f, :, lanes] for i in range(HALF_DIRS - 2 * SIDE_DIRS)]
            line += [slab(d, own_ref, edge_own_ref) for d in last_dirs]
            line += [slab(d, other_ref, edge_other_ref) for d in first_dirs]
            base = 1.0 + loss_steep * steep_sq[:, lanes]
            for d in range(HALF_DIRS):
                at = d + SIDE_DIRS
                level = weights[0] * line[at] - 1.0
                for m in range(1, SIDE_DIRS + 1):
                    level = level + weights[m] * (line[at - m] + line[at + m])
                excess = jnp.maximum(level, 0.0)
                square = excess * excess
                if single:
                    cum = cum_ref[d, :, lanes]
                    along = math.cos(heading(d)) * wind_ref[0, :, lanes] + math.sin(heading(d)) * wind_ref[1, :, lanes]
                else:
                    cum = cum_out_ref[d, :, lanes]
                    cum_out_ref[d, :, lanes] = cum + square
                    along = align[d, :, lanes]
                grown = 1.0 + gain * jnp.maximum(along * omega - 1.0, 0.0)
                lost = base + loss_sat * square + loss_cum * cum
                result[d, f, :, lanes] = line[at] * grown / lost
            leave(f, half).start()
        return omega * FREQ_STEP

    if single:
        one(0, jnp.float32(frequency(first)))
    else:
        lax.fori_loop(0, count, one, jnp.float32(frequency(first)))
    for f in range(count):
        for half in range(2):
            leave(f, half).wait()


def source_chunk(first, count, inner, outer, last, wind, steep_own, steep_other, cum, own, keep, other, edges, out):
    vmem = pl.BlockSpec(memory_space=pltpu.VMEM)
    hold = pl.BlockSpec(memory_space=pl.ANY)
    chained = out is not None
    operands = (wind, steep_own, steep_other, cum, own, keep, other, *edges) + ((out,) if chained else ())
    out_shape = [jax.ShapeDtypeStruct((HALF_DIRS, NFREQ, 8, 256), jnp.float32)]
    single = last and count == 1
    running = [] if last else [jax.ShapeDtypeStruct((HALF_DIRS, 8, 256), jnp.float32)]
    result = pl.pallas_call(
        functools.partial(source_kernel, first, count, inner, outer, chained, last),
        out_shape=out_shape + running,
        in_specs=[vmem] * (7 + len(edges)) + [hold] * chained,
        out_specs=[hold] + [vmem] * len(running),
        scratch_shapes=[pltpu.VMEM((HALF_DIRS, 8, 256), jnp.float32)] * (last and not single)
        + [pltpu.VMEM((HALF_DIRS, count, 8, 256), jnp.float32)]
        + [pltpu.VMEM((HALF_DIRS, 8, 256), jnp.float32)] * (not single)
        + [pltpu.SemaphoreType.DMA((count, 2))],
        input_output_aliases={len(operands) - 1: 0} if chained else {},
        compiler_params=pltpu.CompilerParams(vmem_limit_bytes=VMEM_BYTES),
        cost_estimate=SMALL_COST,
    )(*operands)
    return result[0], None if last else result[1]


def ring_pairs(size, step, wrap):
    return [(i, (i + step) % size) for i in range(size) if wrap or 0 <= i + step < size]


def paired_shards(spectrum, sea_mask, owner_list, owner_count, slopes, friction, wind_angle):
    tiles_x, tiles_y = lax.axis_size("tx"), lax.axis_size("ty")
    half = lax.axis_index("comp")
    sign = 1.0 - 2.0 * half.astype(jnp.float32)
    spec = spectrum.reshape(HALF_DIRS, NFREQ, 8, 256)
    sea = sea_mask.astype(jnp.float32)
    turn = slopes * sign
    wind = (sign * WIND_FACTOR / GRAVITY) * friction * jnp.stack([jnp.cos(wind_angle), jnp.sin(wind_angle)])

    def joined(axis_size, step, wrap):
        ahead = ring_pairs(axis_size, step, wrap)
        back = ring_pairs(axis_size, -step, wrap)
        return ahead + [(axis_size + i, axis_size + j) for i, j in back]

    swap = [(0, 1), (1, 0)]
    lead_pairs = joined(tiles_x, 1, True)
    trail_pairs = joined(tiles_x, -1, True)
    lat_pairs = joined(tiles_y, 1, False)

    rows = pltpu.with_memory_space_constraint(spectrum.reshape(HALF_DIRS * NFREQ * 8, 256), pltpu.HBM)
    spec = pltpu.with_memory_space_constraint(spec, pltpu.HBM)
    bounds = chunk_bounds()
    raw = raw_edges(spec)

    def halo(g, after):
        begin, end = HALO_GROUPS[g]
        lead, trail, lat = pack(begin, end - begin, sea, rows, after)
        sides = (
            lax.ppermute(lead, ("comp", "tx"), lead_pairs),
            lax.ppermute(trail, ("comp", "tx"), trail_pairs),
            lax.ppermute(lat, ("comp", "ty"), lat_pairs),
        )
        return sides, lead

    first_sides, _ = halo(0, raw)
    raw = lax.ppermute(raw, "comp", swap)
    early = sum(end <= HALO_GROUPS[0][1] for _, end in bounds)
    counts = [end - begin for begin, end in bounds]
    places = [slab_index(INNER_DIRS if i == 0 else ALL_DIRS, counts[i]) for i in range(len(bounds))]
    edge_place = slab_index(OUTER_DIRS, counts[0], base=2 * SIDE_DIRS * counts[1])

    def advect(passes, sides, carries, steep, raw, after):
        group = HALO_GROUPS[0] if sides is first_sides else HALO_GROUPS[1]
        return advect_chunk(passes, group, carries, sea, turn, spec, sides, steep, raw, after)

    sent, kept, received, sums = [], [], [], []

    def send(result):
        sent.append(result[0])
        kept.append(result[1])
        received.append(lax.ppermute(result[0], "comp", swap))

    def source(upto):
        for j in range(len(sums), upto):
            outer, edges = (edge_place, (sent[1], received[1])) if j == 0 else (None, ())
            state[:] = source_chunk(
                bounds[j][0], counts[j], places[j], outer, j == len(bounds) - 1, wind, steep, steep_other,
                state[1], sent[j], kept[j], received[j], edges, state[0],
            )
            sums.append(state[1])

    steep = jnp.zeros((8, 256), jnp.float32)
    for i in range(early):
        passes = [(bounds[i][0], counts[i], INNER_DIRS if i == 0 else ALL_DIRS, places[i], True)]
        after = ()
        if i == 1:
            passes.append((bounds[0][0], counts[0], OUTER_DIRS, edge_place, True))
        if i >= 2:
            after = (received[i - 2], packed)
        result = advect(passes, first_sides, False, steep, raw if i else None, after)
        send(result)
        steep = result[2]
        if i == 1:
            later_sides, packed = halo(1, steep)
    state = [None, jnp.zeros((HALF_DIRS, 8, 256), jnp.float32)]
    summing = SUM_CHUNKS
    ahead = bounds[early + summing][0]
    cuts = [ahead + (NFREQ - ahead) * n // summing for n in range(summing + 1)]
    for i in range(early, len(bounds)):
        after = (received[i - 2],)
        if i in SOURCES_DONE:
            source(SOURCES_DONE[i])
            after += (sums[-1],)
        n = i - early
        passes = [(bounds[i][0], counts[i], ALL_DIRS, places[i], n < summing)]
        if n < summing:
            passes.append((cuts[n], cuts[n + 1] - cuts[n], ALL_DIRS, None, True))
        result = advect(passes, later_sides, n == summing - 1, steep, raw, after)
        send(result)
        if n < summing:
            steep = result[2]
        if n == summing - 1:
            steep_other = received[i][-1]
    source(len(bounds))
    out = state[0]
    return out.reshape(spectrum.shape)


def fits_pairs(mesh, spectrum):
    return (
        mesh.shape["comp"] == 2
        and spectrum.shape[0] == NDIR * NFREQ
        and spectrum.shape[1] == 8 * mesh.shape["tx"]
        and spectrum.shape[2] == 256 * mesh.shape["ty"]
    )


def solution(mesh):
    in_specs = (
        P("comp", "tx", "ty"),
        P("tx", "ty"),
        P("tx", "ty", None, None),
        P("tx", "ty", None),
        P(None, "tx", "ty"),
        P("tx", "ty"),
        P("tx", "ty"),
    )
    out_specs = P("comp", "tx", "ty")

    def step(spectrum, *others):
        body = paired_shards if fits_pairs(mesh, spectrum) else shards
        mapped = jax.shard_map(body, mesh=mesh, in_specs=in_specs, out_specs=out_specs, check_vma=False)
        return mapped(spectrum, *others)

    return step
```
